32 devices in a mesh: ctx: 8 (over z, core), exp: 4 (over y, x).
Axes of the slice: x: 2, y: 2, z: 4, core: 2. Of those that a mesh axis runs over, the one named last changes fastest.
Arguments:
- tokens: bfloat16 [4096, 2048], P(('ctx', 'exp')), may hold values from -12 to 12
- ln1_gain: float32 [2048], replicated, may hold values from 0.5 to 2
- w_query: bfloat16 [2048, 2048], P(None, 'exp')
- key_weight: bfloat16 [2048, 256], replicated
- value_weight: bfloat16 [2048, 256], replicated, may hold values from -0.125 to 0.125
- q_gain: float32 [128], replicated, may hold values from 0.5 to 5.5
- k_gain: float32 [128], replicated, may hold values from 0.5 to 5.5
- w_out: bfloat16 [2048, 2048], P('exp'), may hold values from -0.125 to 0.125
- ln2_gain: float32 [2048], replicated, may hold values from 0.5 to 2
- expert_ids: int32 [4096, 8], P(('ctx', 'exp')), may hold values from 0 to 31, all different within a row; in each aligned block of 128 rows (0 to 127, 128 to 255, ...) at most 48 rows name the same one
- route_weights: int32 [4096, 8], P(('ctx', 'exp')), may hold values from 1 to 255
- w_gate: bfloat16 [32, 2048, 768], P(('ctx', 'exp')), may hold values from -0.125 to 0.125
- w_up: bfloat16 [32, 2048, 768], P(('ctx', 'exp')), may hold values from -0.125 to 0.125
- w_down: bfloat16 [32, 768, 2048], P(('ctx', 'exp')), may hold values from -0.21875 to 0.21875
Outputs:
- layer_out: bfloat16 [4096, 2048], P(('ctx', 'exp'))
The draws below stay inside these ranges and needn't reach their ends.
Inputs may be any that keep to these rules, and one draw needn't show every extreme that they name: `expert_ids`: each token names 8 different experts; among the 128 rows of one device no expert is named by more than 48 rows. `route_weights`: a choice weighs the value divided by 1024.
All inputs are finite; a program needn't handle non-finite values.
Results may differ from the reference program's by a relative error of at most 0.02.
The reference program's roundings to bfloat16 on the way count: a program that leaves them out, or rounds other values in their place, can miss the bound.
Values may be sent and summed in bfloat16 or wider, within the bound.
No kernel may reach another device: no remote copies, remote signals or barrier semaphores. Data moves between devices by JAX's collectives and lax.ppermute only.
A program may use at most 128 MiB of HBM per device.

```python
import math
import jax
import jax.numpy as jnp
import numpy as np
from jax import lax

MODEL_WIDTH = 2048
HEAD_SIZE = 128
QUERY_HEADS = 16
KEY_VALUE_HEADS = 2
FF = 768
TOP = 8
TOK_DEV = 128
SEQUENCE_TOKENS = 4096
EXPERTS = 32
CAP = 48


def draw_tokens(key, part):
    raw_key, scale_key = jax.random.split(key, 2)
    scales = jnp.exp(jax.random.uniform(scale_key, (SEQUENCE_TOKENS, 1), jnp.float32, jnp.log(0.5), jnp.log(2.0)))
    values_raw = jnp.clip(jax.random.normal(raw_key, (SEQUENCE_TOKENS, MODEL_WIDTH), jnp.float32), -6.0, 6.0)
    return (values_raw * scales).astype(jnp.bfloat16)


def key_matrix(key):
    return jax.random.normal(jax.random.fold_in(key, 7), (MODEL_WIDTH, KEY_VALUE_HEADS * HEAD_SIZE), jnp.float32) * MODEL_WIDTH ** (-0.5)


def draw_key_weight(key, part):
    return key_matrix(key).astype(jnp.bfloat16)


def draw_w_query(key, part):
    weight_matrix = jax.random.normal(jax.random.fold_in(key, 11), (MODEL_WIDTH, QUERY_HEADS * HEAD_SIZE), jnp.float32) * MODEL_WIDTH ** (-0.5)
    return weight_matrix.astype(jnp.bfloat16)


def gain_vector(key, salt_value):
    folded = jax.random.fold_in(key, salt_value)
    return jnp.exp(jax.random.uniform(folded, (HEAD_SIZE,), jnp.float32, jnp.log(0.5), jnp.log(2.0)))


def draw_q_gain(key, part):
    return gain_vector(key, 3)


def draw_k_gain(key, part):
    return gain_vector(key, 5)


def with_ends(entries, stream_key, smallest, top_value):
    index_at = [jax.random.randint(jax.random.fold_in(stream_key, axis), (), 0, length) for axis, length in enumerate(entries.shape)]
    main_axis = entries.shape.index(max(entries.shape))
    neighbour = index_at[:main_axis] + [(index_at[main_axis] + 1) % entries.shape[main_axis]] + index_at[main_axis + 1:]
    return entries.at[tuple(index_at)].set(smallest).at[tuple(neighbour)].set(top_value)


def shard_levels(own_key, dims, cuts, low, largest):
    factor_of = 1.0
    for axis_at, blocks in cuts:
        steps = jax.random.uniform(jax.random.fold_in(jax.random.fold_in(own_key, 6), axis_at), (blocks,), jnp.float32, low / len(cuts), largest / len(cuts))
        factor_of = factor_of * jnp.repeat(jnp.exp(steps), dims[axis_at] // blocks).reshape((-1,) + (1,) * (len(dims) - 1 - axis_at))
    return factor_of


def assign_block(rng, own, number, rows, count, top, limit, skew):
    ranking = jax.random.permutation(rng, count)
    heavy_load, ordinary = load_shares(count, rows * top, limit, skew, True), load_shares(count, rows * top, limit, skew, False)
    places = jnp.arange(count)

    def named(tallies, rotation):
        used = int((tallies > 0).sum())
        fixed = max(1, used // 4)
        shifted = fixed + (places - fixed + rotation * (used - fixed)) % max(1, count - fixed)
        return jnp.zeros((count,), jnp.int32).at[ranking[jnp.where(places < fixed, places, shifted)]].set(jnp.asarray(tallies, jnp.int32))

    tallies = jnp.where(number % 4 == 0, named(heavy_load, number // 4), named(ordinary, number - number // 4 - 1))
    mixed = jax.random.permutation(jax.random.fold_in(own, 3), count)
    source_of, taker = mixed[0:count // 2 * 2:2], mixed[1:count // 2 * 2:2]
    slack = jnp.minimum(tallies[source_of] - 1, limit - tallies[taker]) // 2
    slack = jnp.where((source_of == ranking[0]) | (taker == ranking[0]) | (tallies[taker] == 0), 0, jnp.maximum(slack, 0))
    shifted = jax.random.randint(jax.random.fold_in(own, 4), (count // 2,), 0, 1 << 20) % (slack + 1)
    tallies = tallies.at[source_of].add(-shifted).at[taker].add(shifted)
    items = jnp.searchsorted(jnp.cumsum(tallies), jnp.arange(rows * top), side="right").astype(jnp.int32)
    listing = items.reshape(top, rows).T
    listing = listing[jax.random.permutation(jax.random.fold_in(own, 1), rows)]
    rotation = jax.random.randint(jax.random.fold_in(own, 2), (rows, 1), 0, top)
    return jnp.take_along_axis(listing, (jnp.arange(top)[None, :] + rotation) % top, axis=1)


def load_shares(amount, total, bound, slope, full):
    weights = [(1 << 20) // math.isqrt(rank ** slope) + 1 for rank in range(1, amount + 1)]
    largest = bound if full else min(bound, max(-(-total // amount), total * weights[0] // sum(weights)))
    least = 1 if total - largest >= amount - 1 else 0
    counts, rest = [largest] + [least] * (amount - 1), total - largest - least * (amount - 1)
    while rest > 0:
        candidates = [i for i in range(1, amount) if counts[i] < largest] or [i for i in range(1, amount) if counts[i] < bound]
        mass, budget = sum([weights[i] for i in candidates]), rest
        for i in candidates:
            addition = min(bound - counts[i], max(1, budget * weights[i] // mass), rest)
            counts[i] = counts[i] + addition
            rest = rest - addition
    return np.array(counts)


def bell_draw(rng, shape, scale, most, cuts=(), held_as=jnp.bfloat16):
    array = jax.random.normal(rng, shape, jnp.float32) * scale
    if len(cuts) > 0:
        array = shard_levels(rng, shape, cuts, -0.22, 0.18) * array
    return jnp.clip(array, min=-most, max=most).astype(held_as)


def setup_inputs(seed: int = 0) -> dict:
    splits = jax.random.split(jax.random.key(seed), 15)
    tokens = draw_tokens(jax.random.fold_in(splits[14], 71), 0)
    ln1_gain = jnp.clip(jnp.exp(jax.random.uniform(splits[1], (MODEL_WIDTH,), jnp.float32, math.log(0.5), math.log(2.0))), 0.5, 2.0)
    w_query = draw_w_query(jax.random.fold_in(splits[14], 71), 0)
    key_weight = draw_key_weight(jax.random.fold_in(splits[14], 71), 0)
    value_weight = bell_draw(splits[4], (MODEL_WIDTH, KEY_VALUE_HEADS * HEAD_SIZE), MODEL_WIDTH ** -0.5, 0.125)
    q_gain = draw_q_gain(jax.random.fold_in(splits[14], 71), 0)
    k_gain = draw_k_gain(jax.random.fold_in(splits[14], 71), 0)
    w_out = bell_draw(splits[7], (QUERY_HEADS * HEAD_SIZE, MODEL_WIDTH), (QUERY_HEADS * HEAD_SIZE) ** -0.5, 0.125, ((0, 4),))
    ln2_gain = jnp.clip(jnp.exp(jax.random.uniform(splits[8], (MODEL_WIDTH,), jnp.float32, math.log(0.5), math.log(2.0))), 0.5, 2.0)
    expert_ids_keys = jax.random.split(jax.random.fold_in(splits[9], 1), SEQUENCE_TOKENS // TOK_DEV)
    expert_ids_turns = jax.random.permutation(jax.random.fold_in(splits[9], 3), SEQUENCE_TOKENS // TOK_DEV)
    expert_ids = jax.vmap(lambda own, number: assign_block(jax.random.fold_in(splits[9], 2), own, number, TOK_DEV, EXPERTS, TOP, CAP, 2))(expert_ids_keys, expert_ids_turns).reshape((SEQUENCE_TOKENS, TOP))
    route_weights = with_ends(jax.random.randint(splits[10], (SEQUENCE_TOKENS, TOP), 1, 256), jax.random.fold_in(splits[10], 1), 1, 255).astype(jnp.int32)
    w_gate = bell_draw(splits[11], (EXPERTS, MODEL_WIDTH, FF), MODEL_WIDTH ** -0.5, 0.125, ((0, 32),))
    w_up = bell_draw(splits[12], (EXPERTS, MODEL_WIDTH, FF), MODEL_WIDTH ** -0.5, 0.125, ((0, 32),))
    w_down = bell_draw(splits[13], (EXPERTS, FF, MODEL_WIDTH), FF ** -0.5, 0.21875, ((0, 32),))
    return {"tokens": tokens, "ln1_gain": ln1_gain, "w_query": w_query, "key_weight": key_weight, "value_weight": value_weight, "q_gain": q_gain, "k_gain": k_gain, "w_out": w_out, "ln2_gain": ln2_gain, "expert_ids": expert_ids, "route_weights": route_weights, "w_gate": w_gate, "w_up": w_up, "w_down": w_down}


eps_value = 1e-06
theta_value = 1000000.0

def rms_scale(value_states, norm_gain):
    return value_states * lax.rsqrt(lax.optimization_barrier(jnp.mean(value_states * value_states, axis=-1, keepdims=True)) + eps_value) * norm_gain

def rotate(value_states, positions):
    half_size = value_states.shape[-1] // 2
    frequency = theta_value ** (-2.0 * jnp.arange(half_size, dtype=jnp.float32) / value_states.shape[-1])
    angles = positions.astype(jnp.float32)[:, None] * frequency[None, :]
    cosine = jnp.cos(angles)
    sine_part = jnp.sin(angles)
    leading = value_states[..., :half_size]
    second = value_states[..., half_size:]
    return jnp.concatenate([leading * cosine - second * sine_part, second * cosine + leading * sine_part], axis=-1)

def reference(tokens, ln1_gain, w_query, key_weight, value_weight, q_gain, k_gain, w_out, ln2_gain, expert_ids, route_weights, w_gate, w_up, w_down):
    group_width = QUERY_HEADS // KEY_VALUE_HEADS
    inputs32 = tokens.astype(jnp.float32)
    normed_input = rms_scale(inputs32, ln1_gain).astype(jnp.bfloat16)
    positions = jnp.arange(SEQUENCE_TOKENS).astype(jnp.int32)
    query_all = jnp.dot(normed_input, w_query, preferred_element_type=jnp.float32).reshape(SEQUENCE_TOKENS, QUERY_HEADS, HEAD_SIZE).transpose(1, 0, 2)
    queries = rotate(rms_scale(query_all, q_gain), positions).astype(jnp.bfloat16)
    every_key = jnp.dot(normed_input, key_weight, preferred_element_type=jnp.float32).reshape(SEQUENCE_TOKENS, KEY_VALUE_HEADS, HEAD_SIZE).transpose(1, 0, 2)
    keys = rotate(rms_scale(every_key, k_gain), positions).astype(jnp.bfloat16)
    value_states = jnp.dot(normed_input, value_weight, preferred_element_type=jnp.float32).astype(jnp.bfloat16)
    value_states = value_states.reshape(SEQUENCE_TOKENS, KEY_VALUE_HEADS, HEAD_SIZE).transpose(1, 0, 2)
    query_block = min(SEQUENCE_TOKENS, 1024)
    block_count = SEQUENCE_TOKENS // query_block
    scale_factor = HEAD_SIZE ** (-0.5)

    def one_head(head_index):
        head_queries = queries[head_index].astype(jnp.float32)
        head_keys = keys[head_index // group_width].astype(jnp.float32)
        head_values = value_states[head_index // group_width].astype(jnp.float32)

        def one_block(block_index):
            first_row = (block_index * query_block).astype(jnp.int32)
            query_rows = lax.dynamic_slice_in_dim(head_queries, first_row, query_block, 0)
            scores = jnp.dot(query_rows, head_keys.T, precision=lax.Precision.HIGHEST) * scale_factor
            query_pos = first_row + jnp.arange(query_block).astype(jnp.int32)
            visible = positions[None, :] <= query_pos[:, None]
            scores = jnp.where(visible, scores, -jnp.inf)
            row_max = lax.optimization_barrier(jnp.max(scores, axis=1, keepdims=True))
            weights = jnp.exp(scores - row_max)
            row_sum = lax.optimization_barrier(jnp.sum(weights, axis=1, keepdims=True))
            rounded = lax.optimization_barrier(weights.astype(jnp.bfloat16)).astype(jnp.float32)
            mixed = jnp.dot(rounded, head_values, precision=lax.Precision.HIGHEST)
            return (mixed / row_sum).astype(jnp.bfloat16)
        return lax.map(one_block, jnp.arange(block_count)).reshape(SEQUENCE_TOKENS, HEAD_SIZE)
    attended = lax.map(one_head, jnp.arange(QUERY_HEADS))
    attended = attended.transpose(1, 0, 2).reshape(SEQUENCE_TOKENS, QUERY_HEADS * HEAD_SIZE)
    attention = jnp.dot(attended, w_out, preferred_element_type=jnp.float32)
    residual = (inputs32 + attention).astype(jnp.bfloat16)
    normed2 = rms_scale(residual.astype(jnp.float32), ln2_gain).astype(jnp.bfloat16)
    slots_total = SEQUENCE_TOKENS // TOK_DEV * CAP
    flat_ids = expert_ids.reshape(-1)
    flat_tokens = (jnp.arange(SEQUENCE_TOKENS * TOP) // TOP).astype(jnp.int32)
    flat_weights = route_weights.reshape(-1).astype(jnp.float32) / 1024.0
    chosen = (flat_ids[:, None] == jnp.arange(EXPERTS)[None, :]).astype(jnp.int32)
    rank_table = jnp.cumsum(chosen, axis=0) - chosen
    slot_index = lax.optimization_barrier(jnp.sum(rank_table * chosen, axis=1))
    table_rows = jnp.zeros((EXPERTS, slots_total), jnp.int32).at[flat_ids, slot_index].set(flat_tokens)
    table_weights = jnp.zeros((EXPERTS, slots_total), jnp.float32).at[flat_ids, slot_index].set(flat_weights)

    def add_expert(mixture, expert_inputs):
        rows_index, row_weights, gate_matrix, up_matrix, down_matrix = expert_inputs
        gathered = normed2[rows_index]
        gate_act = jnp.dot(gathered, gate_matrix, preferred_element_type=jnp.float32)
        up_act = jnp.dot(gathered, up_matrix, preferred_element_type=jnp.float32)
        hidden = (jax.nn.silu(gate_act) * up_act).astype(jnp.bfloat16)
        produced = jnp.dot(hidden, down_matrix, preferred_element_type=jnp.float32).astype(jnp.bfloat16)
        return (mixture.at[rows_index].add(row_weights[:, None] * produced.astype(jnp.float32)), None)
    mixture, unused = lax.scan(add_expert, jnp.zeros((SEQUENCE_TOKENS, MODEL_WIDTH), jnp.float32), (table_rows, table_weights, w_gate, w_up, w_down))
    return (residual.astype(jnp.float32) + mixture).astype(jnp.bfloat16)
```

```python
import jax
import jax.numpy as jnp
from jax import lax
from jax.experimental import pallas as pl
from jax.experimental.pallas import tpu as pltpu
from jax.sharding import PartitionSpec as P

HEAD_SIZE = 128
QUERY_HEADS = 16
KEY_VALUE_HEADS = 2
TOP = 8


eps_value = 1e-06
theta_value = 1000000.0
floor_value = -1e30
LOG2E = 1.4426950408889634


def rms_scale(value_states, norm_gain):
    return (
        value_states
        * lax.rsqrt(jnp.mean(value_states * value_states, axis=-1, keepdims=True) + eps_value)
        * norm_gain
    )


def rotate(value_states, positions):
    half_size = value_states.shape[-1] // 2
    frequency = theta_value ** (
        -2.0 * jnp.arange(half_size, dtype=jnp.float32) / value_states.shape[-1]
    )
    angles = positions.astype(jnp.float32)[:, None] * frequency[None, :]
    cosine = jnp.cos(angles)
    sine_part = jnp.sin(angles)
    leading = value_states[..., :half_size]
    second = value_states[..., half_size:]
    return jnp.concatenate(
        [leading * cosine - second * sine_part, second * cosine + leading * sine_part], axis=-1
    )


def attention_kernel(block_ref, query_ref, key_ref, value_ref, out_ref):
    rows = query_ref.shape[0]
    heads = query_ref.shape[1] // HEAD_SIZE
    scale = HEAD_SIZE ** (-0.5) * LOG2E
    block = block_ref[0]

    def one_block(first, state, masked):
        keys = key_ref[pl.ds(first, rows), :]
        values = value_ref[pl.ds(first, rows), :]
        if masked:
            key_pos = lax.broadcasted_iota(jnp.int32, (rows, rows), 0)
            query_pos = lax.broadcasted_iota(jnp.int32, (rows, rows), 1)
            hidden = key_pos > query_pos
        result = []
        for head in range(heads):
            top, total, mixed = state[head]
            queries = query_ref[:, head * HEAD_SIZE : (head + 1) * HEAD_SIZE]
            scores = lax.dot_general(
                keys, queries, (((1,), (1,)), ((), ())), preferred_element_type=jnp.float32
            )
            if masked:
                scores = jnp.where(hidden, floor_value, scores)
            new_top = jnp.maximum(top, jnp.max(scores, axis=0, keepdims=True))
            weights = jnp.exp2((scores - new_top) * scale)
            rescale = jnp.exp2((top - new_top) * scale)
            total = total * rescale + jnp.sum(weights, axis=0, keepdims=True)
            mixed = mixed * rescale + lax.dot_general(
                values,
                weights.astype(jnp.bfloat16),
                (((0,), (0,)), ((), ())),
                preferred_element_type=jnp.float32,
            )
            result.append((new_top, total, mixed))
        return tuple(result)

    state = tuple(
        (
            jnp.full((1, rows), floor_value, jnp.float32),
            jnp.zeros((1, rows), jnp.float32),
            jnp.zeros((HEAD_SIZE, rows), jnp.float32),
        )
        for _ in range(heads)
    )
    state = lax.fori_loop(
        0, block, lambda i, s: one_block(pl.multiple_of(i * rows, rows), s, False), state
    )
    state = one_block(pl.multiple_of(block * rows, rows), state, True)
    for head in range(heads):
        _, total, mixed = state[head]
        out_ref[head * HEAD_SIZE : (head + 1) * HEAD_SIZE, :] = (mixed / total).astype(jnp.bfloat16)


def attend(block, queries, key_rows, value_rows):
    rows, width = queries.shape
    total = key_rows.shape[0]
    return pl.pallas_call(
        attention_kernel,
        out_shape=jax.ShapeDtypeStruct((width, rows), jnp.bfloat16),
        in_specs=[pl.BlockSpec(memory_space=pltpu.SMEM)] + [pl.BlockSpec(memory_space=pltpu.VMEM)] * 3,
        out_specs=pl.BlockSpec(memory_space=pltpu.VMEM),
        compiler_params=pltpu.CompilerParams(vmem_limit_bytes=56 * 1024 * 1024),
        cost_estimate=pl.CostEstimate(
            flops=4 * width * rows * total,
            bytes_accessed=2 * (2 * rows * width + 2 * total * HEAD_SIZE),
            transcendentals=rows * total * width // HEAD_SIZE,
        ),
        name="attention",
    )(block, queries, key_rows, value_rows)


def shards(
    tokens,
    ln1_gain,
    w_query,
    key_weight,
    value_weight,
    q_gain,
    k_gain,
    w_out,
    ln2_gain,
    expert_ids,
    route_weights,
    w_gate,
    w_up,
    w_down,
):
    rows_dev = tokens.shape[0]
    ctx_count = lax.axis_size("ctx")
    exp_count = lax.axis_size("exp")
    ctx_rows = rows_dev * exp_count
    heads_dev = w_query.shape[1] // HEAD_SIZE
    group_width = QUERY_HEADS // KEY_VALUE_HEADS
    kv_head = lax.axis_index("exp") * heads_dev // group_width
    inputs32 = tokens.astype(jnp.float32)
    normed_input = rms_scale(inputs32, ln1_gain).astype(jnp.bfloat16)
    key_cols = lax.dynamic_slice_in_dim(key_weight, kv_head * HEAD_SIZE, HEAD_SIZE, 1)
    value_cols = lax.dynamic_slice_in_dim(value_weight, kv_head * HEAD_SIZE, HEAD_SIZE, 1)
    joined = jnp.concatenate([w_query, key_cols, value_cols], axis=1)
    projected = jnp.dot(
        lax.all_gather(normed_input, "exp", axis=0, tiled=True),
        joined,
        preferred_element_type=jnp.float32,
    )
    ctx_first = lax.axis_index("ctx") * ctx_rows
    positions = ctx_first + jnp.arange(ctx_rows)
    query_cols = heads_dev * HEAD_SIZE
    query_heads = projected[:, :query_cols].reshape(ctx_rows, heads_dev, HEAD_SIZE)
    queries = (
        rotate(rms_scale(query_heads, q_gain).transpose(1, 0, 2), positions)
        .astype(jnp.bfloat16)
        .transpose(1, 0, 2)
        .reshape(ctx_rows, query_cols)
    )
    keys_all = rotate(
        rms_scale(projected[:, query_cols : query_cols + HEAD_SIZE], k_gain), positions
    ).astype(jnp.bfloat16)
    values_all = projected[:, query_cols + HEAD_SIZE :].astype(jnp.bfloat16)
    both = lax.all_gather(
        jnp.concatenate([keys_all, values_all], axis=1), "ctx", axis=0, tiled=True
    )
    block = lax.axis_index("ctx").astype(jnp.int32).reshape(1)
    attended = attend(block, queries, both[:, :HEAD_SIZE], both[:, HEAD_SIZE:])
    attention = lax.psum_scatter(
        lax.dot_general(
            attended, w_out, (((0,), (0,)), ((), ())), preferred_element_type=jnp.float32
        ).astype(jnp.bfloat16),
        "exp",
        scatter_dimension=0,
        tiled=True,
    ).astype(jnp.float32)
    residual = (inputs32 + attention).astype(jnp.bfloat16)
    normed2 = rms_scale(residual.astype(jnp.float32), ln2_gain).astype(jnp.bfloat16)
    experts = ctx_count * exp_count
    capacity = max(2, 3 * rows_dev * TOP // (2 * experts))
    chosen = expert_ids[:, :, None] == jnp.arange(experts)[None, None, :]
    counts = jnp.sum(chosen, axis=1, dtype=jnp.int32)
    rank_table = jnp.cumsum(counts, axis=0, dtype=jnp.int32) - counts
    slot_index = jnp.sum(jnp.where(chosen, rank_table[:, None, :], 0), axis=2)
    routing = jnp.stack([expert_ids, slot_index, route_weights], axis=0)
    routing = lax.all_gather(routing, "ctx", axis=0)
    first_expert = lax.axis_index("ctx") * exp_count
    local = routing[:, 0] - first_expert
    place = jnp.where(
        (local >= 0) & (local < exp_count), local * capacity + routing[:, 1], -1
    )
    hot = place[:, :, :, None] == jnp.arange(exp_count * capacity)[None, None, None, :]
    dispatch = jnp.any(hot, axis=2).astype(jnp.bfloat16)
    weight_frac = routing[:, 2].astype(jnp.float32) / 1024.0
    combine = jnp.sum(jnp.where(hot, weight_frac[:, :, :, None], 0.0), axis=2).astype(jnp.bfloat16)
    width = normed2.shape[1]
    gathered = lax.all_gather(normed2, "ctx", axis=0)
    outgoing = jnp.einsum(
        "bts,btd->bsd", dispatch, gathered, preferred_element_type=jnp.float32
    ).astype(jnp.bfloat16)
    outgoing = (
        outgoing.reshape(ctx_count, exp_count, capacity, width)
        .transpose(1, 0, 2, 3)
        .reshape(exp_count * ctx_count * capacity, width)
    )
    flat_rows = lax.all_to_all(outgoing, "exp", split_axis=0, concat_axis=0, tiled=True)
    gate_act = jnp.dot(flat_rows, w_gate[0], preferred_element_type=jnp.float32)
    up_act = jnp.dot(flat_rows, w_up[0], preferred_element_type=jnp.float32)
    hidden = (jax.nn.silu(gate_act) * up_act).astype(jnp.bfloat16)
    produced = jnp.dot(hidden, w_down[0], preferred_element_type=jnp.float32).astype(jnp.bfloat16)
    returned = lax.all_to_all(produced, "exp", split_axis=0, concat_axis=0, tiled=True)
    returned = (
        returned.reshape(exp_count, ctx_count, capacity, width)
        .transpose(1, 0, 2, 3)
        .reshape(ctx_count, exp_count * capacity, width)
    )
    partial = jnp.einsum("bts,bsd->btd", combine, returned, preferred_element_type=jnp.float32)
    mixture = lax.psum_scatter(
        partial.astype(jnp.bfloat16), "ctx", scatter_dimension=0, tiled=True
    )[0].astype(jnp.float32)
    return (residual.astype(jnp.float32) + mixture).astype(jnp.bfloat16)


def solution(mesh):
    in_specs = (
        P(("ctx", "exp"), None),
        P(),
        P(None, "exp"),
        P(),
        P(),
        P(),
        P(),
        P("exp", None),
        P(),
        P(("ctx", "exp"), None),
        P(("ctx", "exp"), None),
        P(("ctx", "exp"), None, None),
        P(("ctx", "exp"), None, None),
        P(("ctx", "exp"), None, None),
    )
    out_specs = P(("ctx", "exp"), None)
    return jax.shard_map(shards, mesh=mesh, in_specs=in_specs, out_specs=out_specs, check_vma=False)
```

```python
import functools

import jax
import jax.numpy as jnp
from jax import lax
from jax.experimental import pallas as pl
from jax.experimental.pallas import tpu as pltpu
from jax.sharding import PartitionSpec as P

HEAD_SIZE = 128
QUERY_HEADS = 16
KEY_VALUE_HEADS = 2
TOP = 8
LOG2E = 1.4426950408889634

eps_value = 1e-06
theta_value = 1000000.0
floor_value = -1e30

VMEM = pl.BlockSpec(memory_space=pltpu.VMEM)
SMEM = pl.BlockSpec(memory_space=pltpu.SMEM)
PARAMS = pltpu.CompilerParams(vmem_limit_bytes=48 * 1024 * 1024)


def rms_scale(value_states, norm_gain):
    return (
        value_states
        * lax.rsqrt(jnp.mean(value_states * value_states, axis=-1, keepdims=True) + eps_value)
        * norm_gain
    )


def swap(array, axis, distance):
    pairs = [(i, i ^ distance) for i in range(lax.axis_size(axis))]
    return lax.ppermute(array, axis, pairs)


def tie(array, *others):
    if not others:
        return array
    return lax.optimization_barrier((array, *others))[0]


def rope_tables(positions):
    half = HEAD_SIZE // 2
    frequency = theta_value ** (-2.0 * jnp.arange(half, dtype=jnp.float32) / HEAD_SIZE)
    angles = positions.astype(jnp.float32)[:, None] * frequency[None, :]
    cosine, sine = jnp.cos(angles), jnp.sin(angles)
    return jnp.concatenate([cosine, cosine], axis=1), jnp.concatenate([-sine, sine], axis=1)


def normed_rotated(states, gain, cosine, sine):
    states = rms_scale(states, gain)
    return states * cosine + pltpu.roll(states, HEAD_SIZE // 2, 1) * sine


def key_value_kernel(tokens, gain, key_weight, value_weight, k_gain, cosine, sine, out):
    normed = rms_scale(tokens[...].astype(jnp.float32), gain[...]).astype(jnp.bfloat16)
    keys = jnp.dot(normed, key_weight[...], preferred_element_type=jnp.float32)
    values = jnp.dot(normed, value_weight[...], preferred_element_type=jnp.float32)
    for head in range(out.shape[0]):
        cols = slice(head * HEAD_SIZE, (head + 1) * HEAD_SIZE)
        rotated = normed_rotated(keys[:, cols], k_gain[...], cosine[...], sine[...])
        out[head, :, :HEAD_SIZE] = rotated.astype(jnp.bfloat16)
        out[head, :, HEAD_SIZE:] = values[:, cols].astype(jnp.bfloat16)


def query_kernel(*refs):
    *pieces, gain, w_query, q_gain, cosine, sine, out = refs
    rows = pieces[0].shape[0]
    heads = w_query.shape[1] // HEAD_SIZE
    for at, piece in enumerate(pieces):
        normed = rms_scale(piece[...].astype(jnp.float32), gain[...]).astype(jnp.bfloat16)
        queries = jnp.dot(normed, w_query[...], preferred_element_type=jnp.float32)
        here = pl.ds(at * rows, rows)
        for head in range(heads):
            cols = slice(head * HEAD_SIZE, (head + 1) * HEAD_SIZE)
            rotated = normed_rotated(queries[:, cols], q_gain[...], cosine[here, :], sine[here, :])
            out[at, pl.ds(head * rows, rows), :] = rotated.astype(jnp.bfloat16)


def attention_kernel(distance, rows, place, queries, both, w_out, out):
    block, me = place[0], place[1]
    heads = w_out.shape[0] // HEAD_SIZE
    width = heads * rows
    span = rows * (place.shape[0] - 2)
    scale = HEAD_SIZE ** (-0.5) * LOG2E
    asked = queries[0]

    def step(first, state, masked):
        keys = both[pl.ds(first, span), :HEAD_SIZE]
        values = both[pl.ds(first, span), HEAD_SIZE:]
        scores = lax.dot_general(
            keys, asked, (((1,), (1,)), ((), ())), preferred_element_type=jnp.float32
        )
        if masked:
            at = lax.broadcasted_iota(jnp.int32, (span, width), 0)
            key_pos = (me ^ (at // rows)) * rows + at % rows
            query = lax.broadcasted_iota(jnp.int32, (span, width), 1)
            scores = jnp.where(
                key_pos <= (me ^ distance) * rows + query % rows, scores, floor_value
            )
        top, total, mixed = state
        new_top = jnp.maximum(top, jnp.max(scores, axis=0, keepdims=True))
        weights = jnp.exp2((scores - new_top) * scale)
        rescale = jnp.exp2((top - new_top) * scale)
        total = total * rescale + jnp.sum(weights, axis=0, keepdims=True)
        mixed = mixed * rescale + lax.dot_general(
            values,
            weights.astype(jnp.bfloat16),
            (((0,), (0,)), ((), ())),
            preferred_element_type=jnp.float32,
        )
        return new_top, total, mixed

    state = (
        jnp.full((1, width), floor_value, jnp.float32),
        jnp.zeros((1, width), jnp.float32),
        jnp.zeros((HEAD_SIZE, width), jnp.float32),
    )
    state = step(pl.multiple_of(block * span, span), state, True)
    state = lax.fori_loop(
        0, block, lambda i, s: step(pl.multiple_of(i * span, span), s, False), state
    )
    _, total, mixed = state
    attended = (mixed / total).astype(jnp.bfloat16)
    attended = jnp.concatenate(
        [attended[:, head * rows : (head + 1) * rows] for head in range(heads)], axis=0
    )
    out[...] = lax.dot_general(
        attended, w_out[...], (((0,), (0,)), ((), ())), preferred_element_type=jnp.float32
    ).astype(jnp.bfloat16)


def residual_kernel(*refs):
    tokens, *partials, gain, residual, normed = refs
    attention = partials[0][...].astype(jnp.float32)
    for partial in partials[1:]:
        attention = attention + partial[...].astype(jnp.float32)
    rounded = (tokens[...].astype(jnp.float32) + attention).astype(jnp.bfloat16)
    residual[...] = rounded
    normed[...] = rms_scale(rounded.astype(jnp.float32), gain[...]).astype(jnp.bfloat16)


def slot_targets(routing, block, expert):
    table = routing[block].astype(jnp.float32)
    named = table[:TOP] == expert.astype(jnp.float32)
    slot = jnp.max(jnp.where(named, table[TOP : 2 * TOP], -1.0), axis=0, keepdims=True)
    weight = jnp.sum(jnp.where(named, table[2 * TOP :], 0.0), axis=0, keepdims=True)
    return slot.astype(jnp.int32), weight * (1.0 / 1024.0)


def dispatch_kernel(group, capacity, place, routing, same, other, *outs):
    block, me = place[0], place[1]
    count = len(outs)
    rows = same.shape[0]
    slots = lax.broadcasted_iota(jnp.int32, (capacity, rows), 0)
    for at, source in enumerate((same, other)):
        parts = []
        for distance in range(count):
            slot, _ = slot_targets(routing, block ^ (2 * group + at), block * count + (me ^ distance))
            parts.append(jnp.where(slots == slot, 1.0, 0.0))
        hot = jnp.concatenate(parts, axis=0).astype(jnp.bfloat16)
        picked = jnp.dot(hot, source[...], preferred_element_type=jnp.float32)
        picked = picked.astype(jnp.bfloat16)
        for distance in range(count):
            outs[distance][at * capacity : (at + 1) * capacity, :] = picked[
                distance * capacity : (distance + 1) * capacity
            ]


def combine_kernel(group, capacity, place, routing, *refs):
    *returned, same, other = refs
    block, me = place[0], place[1]
    count = len(returned)
    rows = same.shape[0]
    slots = lax.broadcasted_iota(jnp.int32, (capacity, rows), 0)
    for at, out in enumerate((same, other)):
        parts = []
        for distance in range(count):
            slot, weight = slot_targets(
                routing, block ^ (2 * group + at), block * count + (me ^ distance)
            )
            parts.append(jnp.where(slots == slot, weight, 0.0))
        shares = jnp.concatenate(parts, axis=0).astype(jnp.bfloat16)
        produced = jnp.concatenate(
            [ref[at * capacity : (at + 1) * capacity, :] for ref in returned], axis=0
        )
        out[...] = lax.dot_general(
            shares, produced, (((0,), (0,)), ((), ())), preferred_element_type=jnp.float32
        ).astype(jnp.bfloat16)


def call(kernel, out_shape, specs, flops, *args, name):
    outs = out_shape if isinstance(out_shape, list) else [out_shape]
    moved = sum(a.size * a.dtype.itemsize for a in [*args, *outs])
    return pl.pallas_call(
        kernel,
        out_shape=out_shape,
        in_specs=specs,
        out_specs=jax.tree.map(lambda _: VMEM, out_shape),
        compiler_params=PARAMS,
        cost_estimate=pl.CostEstimate(flops=flops, bytes_accessed=moved, transcendentals=0),
        name=name,
    )(*args)


def shards(
    tokens,
    ln1_gain,
    w_query,
    key_weight,
    value_weight,
    q_gain,
    k_gain,
    w_out,
    ln2_gain,
    expert_ids,
    route_weights,
    w_gate,
    w_up,
    w_down,
):
    rows, width = tokens.shape
    ctx_count = lax.axis_size("ctx")
    exp_count = lax.axis_size("exp")
    ctx_rows = rows * exp_count
    heads_dev = w_query.shape[1] // HEAD_SIZE
    group_width = QUERY_HEADS // KEY_VALUE_HEADS
    me_ctx = lax.axis_index("ctx").astype(jnp.int32)
    me_exp = lax.axis_index("exp").astype(jnp.int32)
    place = jnp.stack([me_ctx, me_exp] + [jnp.int32(0)] * exp_count)
    peers = list(range(exp_count))
    bf16 = functools.partial(jax.ShapeDtypeStruct, dtype=jnp.bfloat16)

    pieces = [tokens] + [swap(tokens, "exp", d) for d in peers[1:]]

    ln1_row = ln1_gain.reshape(1, width)
    own_first = me_ctx * ctx_rows + me_exp * rows
    cosine, sine = rope_tables(own_first + jnp.arange(rows))
    own_kv = call(
        key_value_kernel,
        bf16((KEY_VALUE_HEADS, rows, 2 * HEAD_SIZE)),
        [VMEM] * 7,
        4 * rows * width * KEY_VALUE_HEADS * HEAD_SIZE,
        tokens,
        ln1_row,
        key_weight,
        value_weight,
        k_gain.reshape(1, HEAD_SIZE),
        cosine,
        sine,
        name="own_kv",
    )

    def head_kv(distance):
        head = (me_exp ^ distance) * heads_dev // group_width
        return lax.dynamic_index_in_dim(own_kv, head, 0, keepdims=False)

    block_kv = jnp.concatenate(
        [head_kv(0)] + [swap(head_kv(d), "exp", d) for d in peers[1:]], axis=0
    )
    both = lax.all_gather(block_kv, "ctx", axis=0, tiled=True)

    experts = ctx_count * exp_count
    capacity = max(2, 3 * rows * TOP // (2 * experts))
    capacity = -(-capacity // 16) * 16
    chosen = expert_ids[:, :, None] == jnp.arange(experts)[None, None, :]
    counts = jnp.sum(chosen, axis=1, dtype=jnp.int32)
    rank_table = jnp.cumsum(counts, axis=0, dtype=jnp.int32) - counts
    slot_index = jnp.sum(jnp.where(chosen, rank_table[:, None, :], 0), axis=2)
    routing = jnp.concatenate([expert_ids, slot_index, route_weights], axis=1).T
    routing = lax.all_gather(tie(routing.astype(jnp.bfloat16), both), "ctx", axis=0)

    positions = jnp.concatenate(
        [me_ctx * ctx_rows + (me_exp ^ d) * rows + jnp.arange(rows) for d in peers]
    )
    cosine, sine = rope_tables(positions)
    queries = call(
        query_kernel,
        bf16((exp_count, heads_dev * rows, HEAD_SIZE)),
        [VMEM] * (exp_count + 5),
        2 * ctx_rows * width * w_query.shape[1],
        *pieces,
        ln1_row,
        w_query,
        q_gain.reshape(1, HEAD_SIZE),
        cosine,
        sine,
        name="queries",
    )

    order = sorted(peers, key=lambda d: -bin(d).count("1"))
    partials, last = {}, ()
    for d in order:
        partials[d] = call(
            functools.partial(attention_kernel, d, rows),
            bf16((rows, width)),
            [SMEM, VMEM, VMEM, VMEM],
            4 * rows * w_query.shape[1] * both.shape[0] + 2 * rows * w_out.size,
            place,
            tie(queries[d : d + 1], *last),
            both,
            w_out,
            name="attention",
        )
        last = (partials[d],)
    parts = [partials[0]] + [swap(partials[d], "exp", d) for d in order if d]
    residual, normed = call(
        residual_kernel,
        [bf16((rows, width)), bf16((rows, width))],
        [VMEM] * (exp_count + 2),
        10 * rows * width,
        tokens,
        *parts,
        ln2_gain.reshape(1, width),
        name="residual",
    )

    groups = ctx_count // 2
    far = [normed]
    for g in range(1, groups):
        far.append(swap(tie(normed, *([far[g - 1]] if g > 2 else [])), "ctx", 2 * g))
    in_flight = {d: () for d in peers[1:]}
    arrived = []
    for g in range(groups):
        mate = swap(far[g], "ctx", 1)
        outgoing = call(
            functools.partial(dispatch_kernel, g, capacity),
            [bf16((2 * capacity, width)) for _ in peers],
            [SMEM, VMEM, VMEM, VMEM],
            4 * exp_count * capacity * rows * width,
            place,
            routing,
            far[g],
            mate,
            name="dispatch",
        )
        came = [outgoing[0]]
        for d in peers[1:]:
            came.append(swap(tie(outgoing[d], *in_flight[d]), "exp", d))
            in_flight[d] = (came[d],)
        arrived.append(came)

    turns = [g for g in range(2, groups)] + [g for g in (1, 0) if g < groups]
    mixture = residual.astype(jnp.float32)
    produced = {}
    for g in range(groups):
        flat_rows = jnp.concatenate(arrived[g], axis=0)
        gate_act = jnp.dot(flat_rows, w_gate[0], preferred_element_type=jnp.float32)
        up_act = jnp.dot(flat_rows, w_up[0], preferred_element_type=jnp.float32)
        hidden = (jax.nn.silu(gate_act) * up_act).astype(jnp.bfloat16)
        made = jnp.dot(hidden, w_down[0], preferred_element_type=jnp.float32)
        made = made.astype(jnp.bfloat16)
        produced[g] = [made[d * 2 * capacity : (d + 1) * 2 * capacity] for d in peers]
    for g in turns:
        back = [produced[g][0]]
        for d in peers[1:]:
            back.append(swap(tie(produced[g][d], *in_flight[d]), "exp", d))
            in_flight[d] = (back[d],)
        same, other = call(
            functools.partial(combine_kernel, g, capacity),
            [bf16((rows, width)), bf16((rows, width))],
            [SMEM, VMEM] + [VMEM] * exp_count,
            4 * exp_count * capacity * rows * width,
            place,
            routing,
            *back,
            name="combine",
        )
        total = same.astype(jnp.float32) + swap(other, "ctx", 1).astype(jnp.float32)
        if g:
            total = swap(total.astype(jnp.bfloat16), "ctx", 2 * g).astype(jnp.float32)
        mixture = mixture + total
    return mixture.astype(jnp.bfloat16)


def solution(mesh):
    in_specs = (
        P(("ctx", "exp"), None),
        P(),
        P(None, "exp"),
        P(),
        P(),
        P(),
        P(),
        P("exp", None),
        P(),
        P(("ctx", "exp"), None),
        P(("ctx", "exp"), None),
        P(("ctx", "exp"), None, None),
        P(("ctx", "exp"), None, None),
        P(("ctx", "exp"), None, None),
    )
    out_specs = P(("ctx", "exp"), None)
    return jax.shard_map(shards, mesh=mesh, in_specs=in_specs, out_specs=out_specs, check_vma=False)
```

```python
import functools

import jax
import jax.numpy as jnp
from jax import lax
from jax.experimental import pallas as pl
from jax.experimental.pallas import tpu as pltpu
from jax.sharding import PartitionSpec as P

HEAD_SIZE = 128
QUERY_HEADS = 16
KEY_VALUE_HEADS = 2
TOP = 8
LOG2E = 1.4426950408889634

eps_value = 1e-06
theta_value = 1000000.0
floor_value = -1e30

VMEM = pl.BlockSpec(memory_space=pltpu.VMEM)
SMEM = pl.BlockSpec(memory_space=pltpu.SMEM)
ANY = pl.BlockSpec(memory_space=pl.ANY)
PARAMS = pltpu.CompilerParams(vmem_limit_bytes=24 * 1024 * 1024)


def rms_scale(value_states, norm_gain):
    return (
        value_states
        * lax.rsqrt(jnp.mean(value_states * value_states, axis=-1, keepdims=True) + eps_value)
        * norm_gain
    )


def swap(array, axis, distance):
    pairs = [(i, i ^ distance) for i in range(lax.axis_size(axis))]
    return lax.ppermute(array, axis, pairs)


def tie(array, *others):
    if not others:
        return array
    return lax.optimization_barrier((array, *others))[0]


def rope_tables(positions):
    half = HEAD_SIZE // 2
    frequency = theta_value ** (-2.0 * jnp.arange(half, dtype=jnp.float32) / HEAD_SIZE)
    angles = positions.astype(jnp.float32)[:, None] * frequency[None, :]
    cosine, sine = jnp.cos(angles), jnp.sin(angles)
    return jnp.concatenate([cosine, cosine], axis=1), jnp.concatenate([-sine, sine], axis=1)


def normed_rotated(states, gain, cosine, sine):
    states = rms_scale(states, gain)
    return states * cosine + pltpu.roll(states, HEAD_SIZE // 2, 1) * sine


def load_all(pairs, sems):
    copies = []
    for source, target in pairs:
        part = max(16, source.shape[0] // 4)
        for first in range(0, source.shape[0], part):
            here = pl.ds(first, part)
            copies.append(
                pltpu.make_async_copy(source.at[here], target.at[here], sems.at[len(copies)])
            )
    for copy in copies:
        copy.start()
    return copies


def own_rows_kernel(
    experts, tokens, key_weight, value_weight, gain, k_gain, cosine, sine, ids, shares, out, table,
    rows_in, key_in, value_in, sems,
):
    copies = load_all([(tokens, rows_in), (key_weight, key_in), (value_weight, value_in)], sems)
    rows = tokens.shape[0]
    chosen_ids = ids[...]
    lanes = lax.broadcasted_iota(jnp.int32, (experts, rows), 0)
    chosen = jnp.zeros((experts, rows), jnp.float32)
    for k in range(TOP):
        chosen = chosen + jnp.where(lanes == chosen_ids[k : k + 1], 1.0, 0.0)
    earlier = lax.broadcasted_iota(jnp.int32, (rows, rows), 0) < lax.broadcasted_iota(
        jnp.int32, (rows, rows), 1
    )
    rank = jnp.dot(
        chosen.astype(jnp.bfloat16),
        jnp.where(earlier, 1.0, 0.0).astype(jnp.bfloat16),
        preferred_element_type=jnp.float32,
    )
    slots = [
        jnp.sum(jnp.where(lanes == chosen_ids[k : k + 1], rank, 0.0), axis=0, keepdims=True)
        for k in range(TOP)
    ]
    slots = jnp.concatenate(slots, axis=0)
    left = jnp.concatenate([chosen_ids, shares[...]], axis=0).astype(jnp.float32)
    table[:, :rows] = left.astype(jnp.bfloat16)
    table[:, rows:] = jnp.concatenate([slots, jnp.zeros_like(slots)], axis=0).astype(jnp.bfloat16)
    for copy in copies:
        copy.wait()
    normed = rms_scale(rows_in[...].astype(jnp.float32), gain[...]).astype(jnp.bfloat16)
    keys = jnp.dot(normed, key_in[...], preferred_element_type=jnp.float32)
    values = jnp.dot(normed, value_in[...], preferred_element_type=jnp.float32)
    for head in range(out.shape[0]):
        cols = slice(head * HEAD_SIZE, (head + 1) * HEAD_SIZE)
        rotated = normed_rotated(keys[:, cols], k_gain[...], cosine[...], sine[...])
        out[head, :, :HEAD_SIZE] = rotated.astype(jnp.bfloat16)
        out[head, :, HEAD_SIZE:] = values[:, cols].astype(jnp.bfloat16)


def query_kernel(*refs):
    *pieces, gain, w_query, q_gain, cosine, sine, out = refs
    rows = pieces[0].shape[0]
    heads = w_query.shape[1] // HEAD_SIZE
    for at, piece in enumerate(pieces):
        normed = rms_scale(piece[...].astype(jnp.float32), gain[...]).astype(jnp.bfloat16)
        queries = jnp.dot(normed, w_query[...], preferred_element_type=jnp.float32)
        here = pl.ds(at * rows, rows)
        for head in range(heads):
            cols = slice(head * HEAD_SIZE, (head + 1) * HEAD_SIZE)
            rotated = normed_rotated(queries[:, cols], q_gain[...], cosine[here, :], sine[here, :])
            out[at, pl.ds(head * rows, rows), :] = rotated.astype(jnp.bfloat16)


def attention_kernel(distance, rows, place, queries, both, w_out, out):
    block, me = place[0], place[1]
    heads = w_out.shape[0] // HEAD_SIZE
    width = heads * rows
    span = rows * (place.shape[0] - 2)
    stride = span + 2 * TOP
    scale = HEAD_SIZE ** (-0.5) * LOG2E
    asked = queries[0]

    def step(first, state, masked):
        keys = both[pl.ds(first, span), :HEAD_SIZE]
        values = both[pl.ds(first, span), HEAD_SIZE:]
        scores = lax.dot_general(
            keys, asked, (((1,), (1,)), ((), ())), preferred_element_type=jnp.float32
        )
        if masked:
            at = lax.broadcasted_iota(jnp.int32, (span, width), 0)
            key_pos = (me ^ (at // rows)) * rows + at % rows
            query = lax.broadcasted_iota(jnp.int32, (span, width), 1)
            scores = jnp.where(
                key_pos <= (me ^ distance) * rows + query % rows, scores, floor_value
            )
        top, total, mixed = state
        new_top = jnp.maximum(top, jnp.max(scores, axis=0, keepdims=True))
        weights = jnp.exp2((scores - new_top) * scale)
        rescale = jnp.exp2((top - new_top) * scale)
        total = total * rescale + jnp.sum(weights, axis=0, keepdims=True)
        mixed = mixed * rescale + lax.dot_general(
            values,
            weights.astype(jnp.bfloat16),
            (((0,), (0,)), ((), ())),
            preferred_element_type=jnp.float32,
        )
        return new_top, total, mixed

    state = (
        jnp.full((1, width), floor_value, jnp.float32),
        jnp.zeros((1, width), jnp.float32),
        jnp.zeros((HEAD_SIZE, width), jnp.float32),
    )
    state = step(pl.multiple_of(block * stride, 2 * TOP), state, True)
    state = lax.fori_loop(
        0, block, lambda i, s: step(pl.multiple_of(i * stride, 2 * TOP), s, False), state
    )
    _, total, mixed = state
    attended = (mixed / total).astype(jnp.bfloat16)
    attended = jnp.concatenate(
        [attended[:, head * rows : (head + 1) * rows] for head in range(heads)], axis=0
    )
    out[...] = lax.dot_general(
        attended, w_out[...], (((0,), (0,)), ((), ())), preferred_element_type=jnp.float32
    ).astype(jnp.bfloat16)


def residual_kernel(*refs):
    tokens, *partials, gain, residual, normed = refs
    attention = partials[0][...].astype(jnp.float32)
    for partial in partials[1:]:
        attention = attention + partial[...].astype(jnp.float32)
    rounded = (tokens[...].astype(jnp.float32) + attention).astype(jnp.bfloat16)
    residual[...] = rounded
    normed[...] = rms_scale(rounded.astype(jnp.float32), gain[...]).astype(jnp.bfloat16)


def slot_targets(routing, block, expert):
    table = routing[block].astype(jnp.float32)
    rows = table.shape[1] // 2
    named = table[:TOP, :rows] == expert.astype(jnp.float32)
    slot = jnp.max(jnp.where(named, table[:TOP, rows:], -1.0), axis=0, keepdims=True)
    weight = jnp.sum(jnp.where(named, table[TOP:, :rows], 0.0), axis=0, keepdims=True)
    return slot.astype(jnp.int32), weight * (1.0 / 1024.0)


def dispatch_kernel(group, capacity, place, routing, same, other, *outs):
    block, me = place[0], place[1]
    count = len(outs)
    rows = same.shape[0]
    slots = lax.broadcasted_iota(jnp.int32, (capacity, rows), 0)
    for at, source in enumerate((same, other)):
        parts = []
        for distance in range(count):
            slot, _ = slot_targets(routing, block ^ (2 * group + at), block * count + (me ^ distance))
            parts.append(jnp.where(slots == slot, 1.0, 0.0))
        hot = jnp.concatenate(parts, axis=0).astype(jnp.bfloat16)
        picked = jnp.dot(hot, source[...], preferred_element_type=jnp.float32)
        picked = picked.astype(jnp.bfloat16)
        for distance in range(count):
            outs[distance][at * capacity : (at + 1) * capacity, :] = picked[
                distance * capacity : (distance + 1) * capacity
            ]


def combine_kernel(group, capacity, place, routing, *refs):
    *returned, same, other = refs
    block, me = place[0], place[1]
    count = len(returned)
    rows = same.shape[0]
    slots = lax.broadcasted_iota(jnp.int32, (capacity, rows), 0)
    for at, out in enumerate((same, other)):
        parts = []
        for distance in range(count):
            slot, weight = slot_targets(
                routing, block ^ (2 * group + at), block * count + (me ^ distance)
            )
            parts.append(jnp.where(slots == slot, weight, 0.0))
        shares = jnp.concatenate(parts, axis=0).astype(jnp.bfloat16)
        produced = jnp.concatenate(
            [ref[at * capacity : (at + 1) * capacity, :] for ref in returned], axis=0
        )
        out[...] = lax.dot_general(
            shares, produced, (((0,), (0,)), ((), ())), preferred_element_type=jnp.float32
        ).astype(jnp.bfloat16)


def expert_kernel(*refs):
    count = (len(refs) - 4) // 2
    came, (w_gate, w_up, w_down), made, hidden = refs[:count], refs[count : count + 3], refs[count + 3 : -1], refs[-1]
    part = came[0].shape[0]
    rows = jnp.concatenate([ref[...] for ref in came], axis=0)
    for first in range(0, hidden.shape[1], 256):
        cols = slice(first, first + 256)
        gate = jnp.dot(rows, w_gate[:, cols], preferred_element_type=jnp.float32)
        up = jnp.dot(rows, w_up[:, cols], preferred_element_type=jnp.float32)
        hidden[:, cols] = (gate / (1.0 + jnp.exp(-gate)) * up).astype(jnp.bfloat16)
    for first in range(0, w_down.shape[1], 512):
        cols = slice(first, first + 512)
        product = jnp.dot(hidden[...], w_down[:, cols], preferred_element_type=jnp.float32)
        product = product.astype(jnp.bfloat16)
        for at, ref in enumerate(made):
            ref[:, cols] = product[at * part : (at + 1) * part]


def call(kernel, out_shape, specs, *args, name, scratch=()):
    return pl.pallas_call(
        kernel,
        out_shape=out_shape,
        in_specs=specs,
        out_specs=jax.tree.map(lambda _: VMEM, out_shape),
        scratch_shapes=scratch,
        compiler_params=PARAMS,
        cost_estimate=pl.CostEstimate(flops=1000, bytes_accessed=1000, transcendentals=0),
        name=name,
    )(*args)


def shards(
    tokens,
    ln1_gain,
    w_query,
    key_weight,
    value_weight,
    q_gain,
    k_gain,
    w_out,
    ln2_gain,
    expert_ids,
    route_weights,
    w_gate,
    w_up,
    w_down,
):
    rows, width = tokens.shape
    ctx_count = lax.axis_size("ctx")
    exp_count = lax.axis_size("exp")
    ctx_rows = rows * exp_count
    heads_dev = w_query.shape[1] // HEAD_SIZE
    group_width = QUERY_HEADS // KEY_VALUE_HEADS
    me_ctx = lax.axis_index("ctx").astype(jnp.int32)
    me_exp = lax.axis_index("exp").astype(jnp.int32)
    place = jnp.stack([me_ctx, me_exp] + [jnp.int32(0)] * exp_count)
    peers = list(range(exp_count))
    bf16 = functools.partial(jax.ShapeDtypeStruct, dtype=jnp.bfloat16)

    pieces = {0: tokens}
    for d in peers[1:]:
        if d & (d - 1) == 0:
            pieces[d] = swap(tokens, "exp", d)

    experts = ctx_count * exp_count
    capacity = max(2, 3 * rows * TOP // (2 * experts))
    capacity = -(-capacity // 16) * 16
    ln1_row = ln1_gain.reshape(1, width)
    own_first = me_ctx * ctx_rows + me_exp * rows
    cosine, sine = rope_tables(own_first + jnp.arange(rows))
    kv_width = key_weight.shape[1]
    own_kv, table = call(
        functools.partial(own_rows_kernel, experts),
        [bf16((KEY_VALUE_HEADS, rows, 2 * HEAD_SIZE)), bf16((2 * TOP, 2 * rows))],
        [ANY] * 3 + [VMEM] * 6,
        tokens,
        key_weight,
        value_weight,
        ln1_row,
        k_gain.reshape(1, HEAD_SIZE),
        cosine,
        sine,
        expert_ids.T,
        route_weights.T,
        name="own_rows",
        scratch=[
            pltpu.VMEM((rows, width), jnp.bfloat16),
            pltpu.VMEM((width, kv_width), jnp.bfloat16),
            pltpu.VMEM((width, kv_width), jnp.bfloat16),
            pltpu.SemaphoreType.DMA((12,)),
        ],
    )

    def head_kv(distance):
        head = (me_exp ^ distance) * heads_dev // group_width
        return lax.dynamic_index_in_dim(own_kv, head, 0, keepdims=False)

    block_kv = [head_kv(0)] + [swap(head_kv(d), "exp", d) for d in peers[1:]]
    for d in peers[1:]:
        if d not in pieces:
            pieces[d] = swap(tie(tokens, *block_kv[1:]), "exp", d)
    both = lax.all_gather(jnp.concatenate(block_kv + [table], axis=0), "ctx", axis=0, tiled=True)
    routing = both.reshape(ctx_count, ctx_rows + 2 * TOP, 2 * HEAD_SIZE)[:, ctx_rows:]

    positions = jnp.concatenate(
        [me_ctx * ctx_rows + (me_exp ^ d) * rows + jnp.arange(rows) for d in peers]
    )
    cosine, sine = rope_tables(positions)
    queries = call(
        query_kernel,
        bf16((exp_count, heads_dev * rows, HEAD_SIZE)),
        [VMEM] * (exp_count + 5),
        *[pieces[d] for d in peers],
        ln1_row,
        w_query,
        q_gain.reshape(1, HEAD_SIZE),
        cosine,
        sine,
        name="queries",
    )

    order = sorted(peers, key=lambda d: -bin(d).count("1"))
    partials, last = {}, ()
    for d in order:
        partials[d] = call(
            functools.partial(attention_kernel, d, rows),
            bf16((rows, width)),
            [SMEM, VMEM, VMEM, VMEM],
            place,
            tie(queries[d : d + 1], *last),
            both,
            w_out,
            name="attention",
        )
        last = (partials[d],)
    parts = [partials[0]] + [swap(partials[d], "exp", d) for d in order if d]
    residual, normed = call(
        residual_kernel,
        [bf16((rows, width)), bf16((rows, width))],
        [VMEM] * (exp_count + 2),
        tokens,
        *parts,
        ln2_gain.reshape(1, width),
        name="residual",
    )

    groups = ctx_count // 2
    far = [normed]
    for g in range(1, groups):
        far.append(swap(tie(normed, *([far[g - 1]] if g > 2 else [])), "ctx", 2 * g))
    in_flight = {d: () for d in peers[1:]}
    arrived = []
    for g in range(groups):
        mate = swap(far[g], "ctx", 1)
        outgoing = call(
            functools.partial(dispatch_kernel, g, capacity),
            [bf16((2 * capacity, width)) for _ in peers],
            [SMEM, VMEM, VMEM, VMEM],
            place,
            routing,
            far[g],
            mate,
            name="dispatch",
        )
        came = [outgoing[0]]
        for d in peers[1:]:
            came.append(swap(tie(outgoing[d], *in_flight[d]), "exp", d))
            in_flight[d] = (came[d],)
        arrived.append(came)

    turns = [g for g in range(2, groups)] + [g for g in (1, 0) if g < groups]
    mixture = residual.astype(jnp.float32)
    produced = {}
    for g in range(groups):
        produced[g] = call(
            expert_kernel,
            [bf16((2 * capacity, width)) for _ in peers],
            [VMEM] * (exp_count + 3),
            *arrived[g],
            w_gate[0],
            w_up[0],
            w_down[0],
            name="expert",
            scratch=[pltpu.VMEM((2 * capacity * exp_count, w_gate.shape[2]), jnp.bfloat16)],
        )
    for g in turns:
        back = [produced[g][0]]
        for d in peers[1:]:
            back.append(swap(tie(produced[g][d], *in_flight[d]), "exp", d))
            in_flight[d] = (back[d],)
        same, other = call(
            functools.partial(combine_kernel, g, capacity),
            [bf16((rows, width)), bf16((rows, width))],
            [SMEM, VMEM] + [VMEM] * exp_count,
            place,
            routing,
            *back,
            name="combine",
        )
        total = same.astype(jnp.float32) + swap(other, "ctx", 1).astype(jnp.float32)
        if g:
            total = swap(total.astype(jnp.bfloat16), "ctx", 2 * g).astype(jnp.float32)
        mixture = mixture + total
    return mixture.astype(jnp.bfloat16)


def solution(mesh):
    in_specs = (
        P(("ctx", "exp"), None),
        P(),
        P(None, "exp"),
        P(),
        P(),
        P(),
        P(),
        P("exp", None),
        P(),
        P(("ctx", "exp"), None),
        P(("ctx", "exp"), None),
        P(("ctx", "exp"), None, None),
        P(("ctx", "exp"), None, None),
        P(("ctx", "exp"), None, None),
    )
    out_specs = P(("ctx", "exp"), None)
    return jax.shard_map(shards, mesh=mesh, in_specs=in_specs, out_specs=out_specs, check_vma=False)
```

```python
import functools

import jax
import jax.numpy as jnp
from jax import lax
from jax.experimental import pallas as pl
from jax.experimental.pallas import tpu as pltpu
from jax.sharding import PartitionSpec as P

HEAD_SIZE = 128
QUERY_HEADS = 16
KEY_VALUE_HEADS = 2
TOP = 8
LOG2E = 1.4426950408889634

eps_value = 1e-06
theta_value = 1000000.0
floor_value = -1e30

VMEM = pl.BlockSpec(memory_space=pltpu.VMEM)
SMEM = pl.BlockSpec(memory_space=pltpu.SMEM)
ANY = pl.BlockSpec(memory_space=pl.ANY)


def rms_scale(value_states, norm_gain):
    return (
        value_states
        * lax.rsqrt(jnp.mean(value_states * value_states, axis=-1, keepdims=True) + eps_value)
        * norm_gain
    )


def swap(array, axis, distance):
    pairs = [(i, i ^ distance) for i in range(lax.axis_size(axis))]
    return lax.ppermute(array, axis, pairs)


def tie(array, *others):
    if not others:
        return array
    return lax.optimization_barrier((array, *others))[0]


def rope_tables(positions):
    half = HEAD_SIZE // 2
    frequency = theta_value ** (-2.0 * jnp.arange(half, dtype=jnp.float32) / HEAD_SIZE)
    angles = positions.astype(jnp.float32)[:, None] * frequency[None, :]
    cosine, sine = jnp.cos(angles), jnp.sin(angles)
    return jnp.concatenate([cosine, cosine], axis=1), jnp.concatenate([-sine, sine], axis=1)


def normed_rotated(states, gain, cosine, sine):
    states = rms_scale(states, gain)
    return states * cosine + pltpu.roll(states, HEAD_SIZE // 2, 1) * sine


def load_all(pairs, sems):
    copies = []
    for source, target in pairs:
        part = source.shape[0] // 4 if source.shape[0] >= 128 and source.shape[1] > 128 else source.shape[0]
        for first in range(0, source.shape[0], part):
            here = pl.ds(first, part)
            copies.append(
                pltpu.make_async_copy(source.at[here], target.at[here], sems.at[len(copies)])
            )
    for copy in copies:
        copy.start()
    return copies


def own_rows_kernel(experts, *refs):
    sources, (out, table), targets, sems = refs[:9], refs[9:11], refs[11:20], refs[20]
    copies = load_all(list(zip(sources, targets)), sems)
    ids, shares, tokens, gain, key_weight, value_weight, k_gain, cosine, sine = targets
    copies[0].wait()
    copies[1].wait()
    rows = tokens.shape[0]
    chosen_ids = ids[...]
    lanes = lax.broadcasted_iota(jnp.int32, (experts, rows), 0)
    chosen = jnp.zeros((experts, rows), jnp.float32)
    for k in range(TOP):
        chosen = chosen + jnp.where(lanes == chosen_ids[k : k + 1], 1.0, 0.0)
    earlier = lax.broadcasted_iota(jnp.int32, (rows, rows), 0) < lax.broadcasted_iota(
        jnp.int32, (rows, rows), 1
    )
    rank = jnp.dot(
        chosen.astype(jnp.bfloat16),
        jnp.where(earlier, 1.0, 0.0).astype(jnp.bfloat16),
        preferred_element_type=jnp.float32,
    )
    slots = [
        jnp.sum(jnp.where(lanes == chosen_ids[k : k + 1], rank, 0.0), axis=0, keepdims=True)
        for k in range(TOP)
    ]
    slots = jnp.concatenate(slots, axis=0)
    left = jnp.concatenate([chosen_ids, shares[...]], axis=0).astype(jnp.float32)
    table[:, :rows] = left.astype(jnp.bfloat16)
    table[:, rows:] = jnp.concatenate([slots, jnp.zeros_like(slots)], axis=0).astype(jnp.bfloat16)
    for copy in copies[2:]:
        copy.wait()
    normed = rms_scale(tokens[...].astype(jnp.float32), gain[...]).astype(jnp.bfloat16)
    keys = jnp.dot(normed, key_weight[...], preferred_element_type=jnp.float32)
    values = jnp.dot(normed, value_weight[...], preferred_element_type=jnp.float32)
    for head in range(out.shape[0]):
        cols = slice(head * HEAD_SIZE, (head + 1) * HEAD_SIZE)
        rotated = normed_rotated(keys[:, cols], k_gain[...], cosine[...], sine[...])
        out[head, :, :HEAD_SIZE] = rotated.astype(jnp.bfloat16)
        out[head, :, HEAD_SIZE:] = values[:, cols].astype(jnp.bfloat16)


def query_kernel(*refs):
    *pieces, gain, w_query, q_gain, cosine, sine, out = refs
    rows = pieces[0].shape[0]
    heads = w_query.shape[1] // HEAD_SIZE
    for at, piece in enumerate(pieces):
        normed = rms_scale(piece[...].astype(jnp.float32), gain[...]).astype(jnp.bfloat16)
        queries = jnp.dot(normed, w_query[...], preferred_element_type=jnp.float32)
        here = pl.ds(at * rows, rows)
        for head in range(heads):
            cols = slice(head * HEAD_SIZE, (head + 1) * HEAD_SIZE)
            rotated = normed_rotated(queries[:, cols], q_gain[...], cosine[here, :], sine[here, :])
            out[at, pl.ds(head * rows, rows), :] = rotated.astype(jnp.bfloat16)


def attention_kernel(distances, rows, place, queries, both, w_out, *outs):
    block, me = place[0], place[1]
    heads = w_out.shape[0] // HEAD_SIZE
    width = heads * rows
    span = rows * (place.shape[0] - 2)
    stride = span + 2 * TOP
    scale = HEAD_SIZE ** (-0.5) * LOG2E

    def step(first, states, masked):
        keys = both[pl.ds(first, span), :HEAD_SIZE]
        values = both[pl.ds(first, span), HEAD_SIZE:]
        result = []
        for at, (top, total, mixed) in enumerate(states):
            scores = lax.dot_general(
                keys, queries[at], (((1,), (1,)), ((), ())), preferred_element_type=jnp.float32
            )
            if masked:
                row = lax.broadcasted_iota(jnp.int32, (span, width), 0)
                key_pos = (me ^ (row // rows)) * rows + row % rows
                query = lax.broadcasted_iota(jnp.int32, (span, width), 1) % rows
                query_pos = (me ^ distances[at]) * rows + query
                scores = jnp.where(key_pos <= query_pos, scores, floor_value)
            new_top = jnp.maximum(top, jnp.max(scores, axis=0, keepdims=True))
            weights = jnp.exp2((scores - new_top) * scale)
            rescale = jnp.exp2((top - new_top) * scale)
            total = total * rescale + jnp.sum(weights, axis=0, keepdims=True)
            mixed = mixed * rescale + lax.dot_general(
                values,
                weights.astype(jnp.bfloat16),
                (((0,), (0,)), ((), ())),
                preferred_element_type=jnp.float32,
            )
            result.append((new_top, total, mixed))
        return tuple(result)

    states = tuple(
        (
            jnp.full((1, width), floor_value, jnp.float32),
            jnp.zeros((1, width), jnp.float32),
            jnp.zeros((HEAD_SIZE, width), jnp.float32),
        )
        for _ in distances
    )
    states = step(pl.multiple_of(block * stride, 2 * TOP), states, True)
    states = lax.fori_loop(
        0, block, lambda i, s: step(pl.multiple_of(i * stride, 2 * TOP), s, False), states
    )
    for (_, total, mixed), out in zip(states, outs):
        attended = (mixed / total).astype(jnp.bfloat16)
        attended = jnp.concatenate(
            [attended[:, head * rows : (head + 1) * rows] for head in range(heads)], axis=0
        )
        out[...] = lax.dot_general(
            attended, w_out[...], (((0,), (0,)), ((), ())), preferred_element_type=jnp.float32
        ).astype(jnp.bfloat16)


def add_kernel(total, partial, out):
    out[...] = total[...].astype(jnp.float32) + partial[...].astype(jnp.float32)


def residual_kernel(tokens, attention, partial, gain, residual, normed):
    summed = attention[...].astype(jnp.float32) + partial[...].astype(jnp.float32)
    rounded = (tokens[...].astype(jnp.float32) + summed).astype(jnp.bfloat16)
    residual[...] = rounded
    normed[...] = rms_scale(rounded.astype(jnp.float32), gain[...]).astype(jnp.bfloat16)


def slot_targets(routing, block, expert):
    table = routing[block].astype(jnp.float32)
    rows = table.shape[1] // 2
    named = table[:TOP, :rows] == expert.astype(jnp.float32)
    slot = jnp.max(jnp.where(named, table[:TOP, rows:], -1.0), axis=0, keepdims=True)
    weight = jnp.sum(jnp.where(named, table[TOP:, :rows], 0.0), axis=0, keepdims=True)
    return slot.astype(jnp.int32), weight * (1.0 / 1024.0)


def dispatch_kernel(group, capacity, place, routing, same, other, *outs):
    block, me = place[0], place[1]
    count = len(outs)
    rows = same.shape[0]
    slots = lax.broadcasted_iota(jnp.int32, (capacity, rows), 0)
    for at, source in enumerate((same, other)):
        parts = []
        for distance in range(count):
            slot, _ = slot_targets(routing, block ^ (2 * group + at), block * count + (me ^ distance))
            parts.append(jnp.where(slots == slot, 1.0, 0.0))
        hot = jnp.concatenate(parts, axis=0).astype(jnp.bfloat16)
        picked = jnp.dot(hot, source[...], preferred_element_type=jnp.float32)
        picked = picked.astype(jnp.bfloat16)
        for distance in range(count):
            outs[distance][at * capacity : (at + 1) * capacity, :] = picked[
                distance * capacity : (distance + 1) * capacity
            ]


def combine_kernel(group, capacity, place, routing, *refs):
    *returned, same, other = refs
    block, me = place[0], place[1]
    count = len(returned)
    rows = same.shape[0]
    slots = lax.broadcasted_iota(jnp.int32, (capacity, rows), 0)
    for at, out in enumerate((same, other)):
        parts = []
        for distance in range(count):
            slot, weight = slot_targets(
                routing, block ^ (2 * group + at), block * count + (me ^ distance)
            )
            parts.append(jnp.where(slots == slot, weight, 0.0))
        shares = jnp.concatenate(parts, axis=0).astype(jnp.bfloat16)
        produced = jnp.concatenate(
            [ref[at * capacity : (at + 1) * capacity, :] for ref in returned], axis=0
        )
        out[...] = lax.dot_general(
            shares, produced, (((0,), (0,)), ((), ())), preferred_element_type=jnp.float32
        ).astype(jnp.bfloat16)


def expert_kernel(*refs):
    count = (len(refs) - 4) // 2
    came, (w_gate, w_up, w_down), made, hidden = refs[:count], refs[count : count + 3], refs[count + 3 : -1], refs[-1]
    part = came[0].shape[0]
    rows = jnp.concatenate([ref[...] for ref in came], axis=0)
    for first in range(0, hidden.shape[1], 256):
        cols = slice(first, first + 256)
        gate = jnp.dot(rows, w_gate[:, cols], preferred_element_type=jnp.float32)
        up = jnp.dot(rows, w_up[:, cols], preferred_element_type=jnp.float32)
        hidden[:, cols] = (gate / (1.0 + jnp.exp(-gate)) * up).astype(jnp.bfloat16)
    for first in range(0, w_down.shape[1], 512):
        cols = slice(first, first + 512)
        product = jnp.dot(hidden[...], w_down[:, cols], preferred_element_type=jnp.float32)
        product = product.astype(jnp.bfloat16)
        for at, ref in enumerate(made):
            ref[:, cols] = product[at * part : (at + 1) * part]


def call(kernel, out_shape, specs, *args, name, scratch=(), limit=24, flops=1000):
    return pl.pallas_call(
        kernel,
        out_shape=out_shape,
        in_specs=specs,
        out_specs=jax.tree.map(lambda _: VMEM, out_shape),
        scratch_shapes=scratch,
        compiler_params=pltpu.CompilerParams(vmem_limit_bytes=limit * 1024 * 1024),
        cost_estimate=pl.CostEstimate(flops=flops, bytes_accessed=1000, transcendentals=0),
        name=name,
    )(*args)


def shards(
    tokens,
    ln1_gain,
    w_query,
    key_weight,
    value_weight,
    q_gain,
    k_gain,
    w_out,
    ln2_gain,
    expert_ids,
    route_weights,
    w_gate,
    w_up,
    w_down,
):
    rows, width = tokens.shape
    ctx_count = lax.axis_size("ctx")
    exp_count = lax.axis_size("exp")
    ctx_rows = rows * exp_count
    heads_dev = w_query.shape[1] // HEAD_SIZE
    group_width = QUERY_HEADS // KEY_VALUE_HEADS
    me_ctx = lax.axis_index("ctx").astype(jnp.int32)
    me_exp = lax.axis_index("exp").astype(jnp.int32)
    place = jnp.stack([me_ctx, me_exp] + [jnp.int32(0)] * exp_count)
    peers = list(range(exp_count))
    bf16 = functools.partial(jax.ShapeDtypeStruct, dtype=jnp.bfloat16)

    pieces = {0: tokens}
    for d in peers[1:]:
        if d & (d - 1) == 0:
            pieces[d] = swap(tokens, "exp", d)

    experts = ctx_count * exp_count
    capacity = max(2, 3 * rows * TOP // (2 * experts))
    capacity = -(-capacity // 16) * 16
    ln1_row = ln1_gain.reshape(1, width)
    own_first = me_ctx * ctx_rows + me_exp * rows
    cosine, sine = rope_tables(own_first + jnp.arange(rows))
    own_args = [
        expert_ids.T,
        route_weights.T,
        tokens,
        ln1_row,
        key_weight,
        value_weight,
        k_gain.reshape(1, HEAD_SIZE),
        cosine,
        sine,
    ]
    own_kv, table = call(
        functools.partial(own_rows_kernel, experts),
        [bf16((KEY_VALUE_HEADS, rows, 2 * HEAD_SIZE)), bf16((2 * TOP, 2 * rows))],
        [ANY] * 9,
        *own_args,
        name="own_rows",
        scratch=[pltpu.VMEM(a.shape, a.dtype) for a in own_args] + [pltpu.SemaphoreType.DMA((18,))],
        limit=60,
    )

    def head_kv(distance):
        head = (me_exp ^ distance) * heads_dev // group_width
        return lax.dynamic_index_in_dim(own_kv, head, 0, keepdims=False)

    block_kv = [head_kv(0)] + [swap(head_kv(d), "exp", d) for d in peers[1:]]
    for d in peers[1:]:
        if d not in pieces:
            pieces[d] = swap(tie(tokens, *block_kv[1:]), "exp", d)
    both = jnp.concatenate(block_kv + [table], axis=0)
    both = tie(both, *[pieces[d] for d in peers[1:] if d & (d - 1) == 0])
    both = lax.all_gather(both, "ctx", axis=0, tiled=True)
    routing = both.reshape(ctx_count, ctx_rows + 2 * TOP, 2 * HEAD_SIZE)[:, ctx_rows:]

    positions = jnp.concatenate(
        [me_ctx * ctx_rows + (me_exp ^ d) * rows + jnp.arange(rows) for d in peers]
    )
    cosine, sine = rope_tables(positions)
    queries = call(
        query_kernel,
        bf16((exp_count, heads_dev * rows, HEAD_SIZE)),
        [VMEM] * (exp_count + 5),
        *[pieces[d] for d in peers],
        ln1_row,
        w_query,
        q_gain.reshape(1, HEAD_SIZE),
        cosine,
        sine,
        name="queries",
    )

    order = sorted(peers, key=lambda d: -bin(d).count("1"))
    partials, last = {}, ()
    for some in [[d] for d in order]:
        asked = queries[some[0] : some[0] + 1]
        made = call(
            functools.partial(attention_kernel, some, rows),
            [bf16((rows, width)) for _ in some],
            [SMEM, VMEM, VMEM, VMEM],
            place,
            tie(asked, *last),
            both,
            w_out,
            name="attention",
        )
        partials.update(zip(some, made))
        last = tuple(made)
    attention = partials[0]
    parts = [swap(partials[d], "exp", d) for d in order if d]
    for part in parts[:-1]:
        attention = call(
            add_kernel,
            jax.ShapeDtypeStruct((rows, width), jnp.float32),
            [VMEM] * 2,
            attention,
            part,
            name="add",
            flops=3_000_000_000,
        )
    residual, normed = call(
        residual_kernel,
        [bf16((rows, width)), bf16((rows, width))],
        [VMEM] * 4,
        tokens,
        attention,
        parts[-1],
        ln2_gain.reshape(1, width),
        name="residual",
    )

    groups = ctx_count // 2
    far = [normed]
    for g in range(1, groups):
        far.append(swap(tie(normed, *([far[g - 1]] if g > 2 else [])), "ctx", 2 * g))
    in_flight = {d: () for d in peers[1:]}
    arrived, sent = [], ()
    for g in range(groups):
        mate = swap(tie(far[g], *sent), "ctx", 1)
        outgoing = call(
            functools.partial(dispatch_kernel, g, capacity),
            [bf16((2 * capacity, width)) for _ in peers],
            [SMEM, VMEM, VMEM, VMEM],
            place,
            routing,
            far[g],
            mate,
            name="dispatch",
        )
        came = [outgoing[0]]
        for d in peers[1:]:
            came.append(swap(tie(outgoing[d], *in_flight[d]), "exp", d))
            in_flight[d] = (came[d],)
        sent = tuple(came[1:]) if g == 0 else ()
        arrived.append(came)

    turns = [g for g in range(2, groups)] + [g for g in (1, 0) if g < groups]
    mixture = residual.astype(jnp.float32)
    produced, sums, hop = {}, (), ()
    for g in range(groups):
        produced[g] = call(
            expert_kernel,
            [bf16((2 * capacity, width)) for _ in peers],
            [VMEM] * (exp_count + 3),
            *arrived[g],
            w_gate[0],
            w_up[0],
            w_down[0],
            name="expert",
            scratch=[pltpu.VMEM((2 * capacity * exp_count, w_gate.shape[2]), jnp.bfloat16)],
        )
    for g in turns:
        back = [tie(produced[g][0], *sums)]
        for d in peers[1:]:
            back.append(swap(tie(produced[g][d], *in_flight[d]), "exp", d))
            in_flight[d] = (back[d],)
        same, other = call(
            functools.partial(combine_kernel, g, capacity),
            [bf16((rows, width)), bf16((rows, width))],
            [SMEM, VMEM] + [VMEM] * exp_count,
            place,
            routing,
            *back,
            name="combine",
        )
        total = same.astype(jnp.float32) + swap(other, "ctx", 1).astype(jnp.float32)
        if g:
            total = total.astype(jnp.bfloat16)
            sums = (total,)
            total = swap(tie(total, *(hop if g > 1 else ())), "ctx", 2 * g)
            hop = (total,)
            total = total.astype(jnp.float32)
        mixture = mixture + total
    return mixture.astype(jnp.bfloat16)


def solution(mesh):
    in_specs = (
        P(("ctx", "exp"), None),
        P(),
        P(None, "exp"),
        P(),
        P(),
        P(),
        P(),
        P("exp", None),
        P(),
        P(("ctx", "exp"), None),
        P(("ctx", "exp"), None),
        P(("ctx", "exp"), None, None),
        P(("ctx", "exp"), None, None),
        P(("ctx", "exp"), None, None),
    )
    out_specs = P(("ctx", "exp"), None)
    return jax.shard_map(shards, mesh=mesh, in_specs=in_specs, out_specs=out_specs, check_vma=False)
```

```python
import functools

import jax
import jax.numpy as jnp
from jax import lax
from jax.experimental import pallas as pl
from jax.experimental.pallas import tpu as pltpu
from jax.sharding import PartitionSpec as P

HEAD_SIZE = 128
QUERY_HEADS = 16
KEY_VALUE_HEADS = 2
TOP = 8
LOG2E = 1.4426950408889634

eps_value = 1e-06
theta_value = 1000000.0
floor_value = -1e30

VMEM = pl.BlockSpec(memory_space=pltpu.VMEM)
SMEM = pl.BlockSpec(memory_space=pltpu.SMEM)
ANY = pl.BlockSpec(memory_space=pl.ANY)


def rms_scale(value_states, norm_gain):
    return (
        value_states
        * lax.rsqrt(jnp.mean(value_states * value_states, axis=-1, keepdims=True) + eps_value)
        * norm_gain
    )


def swap(array, axis, distance):
    pairs = [(i, i ^ distance) for i in range(lax.axis_size(axis))]
    return lax.ppermute(array, axis, pairs)


def tie(array, *others):
    if not others:
        return array
    return lax.optimization_barrier((array, *others))[0]


def rope_tables(positions):
    half = HEAD_SIZE // 2
    frequency = theta_value ** (-2.0 * jnp.arange(half, dtype=jnp.float32) / HEAD_SIZE)
    angles = positions.astype(jnp.float32)[:, None] * frequency[None, :]
    return jnp.cos(angles), jnp.sin(angles)


def both_halves(cosine, sine):
    return jnp.concatenate([cosine, cosine], axis=1), jnp.concatenate([-sine, sine], axis=1)


def normed_rotated(states, gain, cosine, sine):
    states = rms_scale(states, gain)
    return states * cosine + pltpu.roll(states, HEAD_SIZE // 2, 1) * sine


def load_all(pairs, sems):
    copies = []
    for source, target in pairs:
        part = source.shape[0] // 4 if source.shape[0] >= 128 and source.shape[1] > 128 else source.shape[0]
        for first in range(0, source.shape[0], part):
            here = pl.ds(first, part)
            copies.append(
                pltpu.make_async_copy(source.at[here], target.at[here], sems.at[len(copies)])
            )
    for copy in copies:
        copy.start()
    return copies


def own_rows_kernel(experts, heads_dev, place, *refs):
    peers = len(refs) - 20
    sources, outs, table, targets, sems = refs[:9], refs[9:-11], refs[-11], refs[-10:-1], refs[-1]
    copies = load_all(list(zip(sources, targets)), sems)
    ids, shares, tokens, gain, key_weight, value_weight, k_gain, cosine, sine = targets
    copies[0].wait()
    copies[1].wait()
    rows = tokens.shape[0]
    chosen_ids = ids[...]
    lanes = lax.broadcasted_iota(jnp.int32, (experts, rows), 0)
    chosen = jnp.zeros((experts, rows), jnp.float32)
    for k in range(TOP):
        chosen = chosen + jnp.where(lanes == chosen_ids[k : k + 1], 1.0, 0.0)
    earlier = lax.broadcasted_iota(jnp.int32, (rows, rows), 0) < lax.broadcasted_iota(
        jnp.int32, (rows, rows), 1
    )
    rank = jnp.dot(
        chosen.astype(jnp.bfloat16),
        jnp.where(earlier, 1.0, 0.0).astype(jnp.bfloat16),
        preferred_element_type=jnp.float32,
    )
    slots = [
        jnp.sum(jnp.where(lanes == chosen_ids[k : k + 1], rank, 0.0), axis=0, keepdims=True)
        for k in range(TOP)
    ]
    slots = jnp.concatenate(slots, axis=0)
    left = jnp.concatenate([chosen_ids, shares[...]], axis=0).astype(jnp.float32)
    table[:, :rows] = left.astype(jnp.bfloat16)
    table[:, rows:] = jnp.concatenate([slots, jnp.zeros_like(slots)], axis=0).astype(jnp.bfloat16)
    for copy in copies[2:]:
        copy.wait()
    normed = rms_scale(tokens[...].astype(jnp.float32), gain[...]).astype(jnp.bfloat16)
    keys = jnp.dot(normed, key_weight[...], preferred_element_type=jnp.float32)
    values = jnp.dot(normed, value_weight[...], preferred_element_type=jnp.float32)
    cosine, sine = both_halves(cosine[...], sine[...])
    for head in range(KEY_VALUE_HEADS):
        cols = slice(head * HEAD_SIZE, (head + 1) * HEAD_SIZE)
        rotated = normed_rotated(keys[:, cols], k_gain[...], cosine, sine)
        pair = jnp.concatenate([rotated, values[:, cols]], axis=1).astype(jnp.bfloat16)
        for distance in range(peers):
            asked = (place[1] ^ distance) * heads_dev // (QUERY_HEADS // KEY_VALUE_HEADS)

            @pl.when(asked == head)
            def _(out=outs[distance], pair=pair):
                out[...] = pair


def query_kernel(*refs):
    *pieces, gain, w_query, q_gain, cosine, sine, out = refs
    rows = pieces[0].shape[0]
    heads = w_query.shape[1] // HEAD_SIZE
    for at, piece in enumerate(pieces):
        normed = rms_scale(piece[...].astype(jnp.float32), gain[...]).astype(jnp.bfloat16)
        queries = jnp.dot(normed, w_query[...], preferred_element_type=jnp.float32)
        here = pl.ds(at * rows, rows)
        turn = both_halves(cosine[here, :], sine[here, :])
        for head in range(heads):
            cols = slice(head * HEAD_SIZE, (head + 1) * HEAD_SIZE)
            rotated = normed_rotated(queries[:, cols], q_gain[...], *turn)
            out[at, pl.ds(head * rows, rows), :] = rotated.astype(jnp.bfloat16)


def attention_kernel(distances, rows, place, queries, both, w_out, *outs):
    block, me = place[0], place[1]
    heads = w_out.shape[0] // HEAD_SIZE
    width = heads * rows
    span = rows * (place.shape[0] - 2)
    stride = span + 2 * TOP
    scale = HEAD_SIZE ** (-0.5) * LOG2E

    def step(first, states, masked):
        keys = both[pl.ds(first, span), :HEAD_SIZE]
        values = both[pl.ds(first, span), HEAD_SIZE:]
        result = []
        for at, (top, total, mixed) in enumerate(states):
            scores = lax.dot_general(
                keys, queries[at], (((1,), (1,)), ((), ())), preferred_element_type=jnp.float32
            )
            if masked:
                row = lax.broadcasted_iota(jnp.int32, (span, width), 0)
                key_pos = (me ^ (row // rows)) * rows + row % rows
                query = lax.broadcasted_iota(jnp.int32, (span, width), 1) % rows
                query_pos = (me ^ distances[at]) * rows + query
                scores = jnp.where(key_pos <= query_pos, scores, floor_value)
            new_top = jnp.maximum(top, jnp.max(scores, axis=0, keepdims=True))
            weights = jnp.exp2((scores - new_top) * scale)
            rescale = jnp.exp2((top - new_top) * scale)
            total = total * rescale + jnp.sum(weights, axis=0, keepdims=True)
            mixed = mixed * rescale + lax.dot_general(
                values,
                weights.astype(jnp.bfloat16),
                (((0,), (0,)), ((), ())),
                preferred_element_type=jnp.float32,
            )
            result.append((new_top, total, mixed))
        return tuple(result)

    states = tuple(
        (
            jnp.full((1, width), floor_value, jnp.float32),
            jnp.zeros((1, width), jnp.float32),
            jnp.zeros((HEAD_SIZE, width), jnp.float32),
        )
        for _ in distances
    )
    states = step(pl.multiple_of(block * stride, 2 * TOP), states, True)
    states = lax.fori_loop(
        0, block, lambda i, s: step(pl.multiple_of(i * stride, 2 * TOP), s, False), states
    )
    for (_, total, mixed), out in zip(states, outs):
        attended = (mixed / total).astype(jnp.bfloat16)
        attended = jnp.concatenate(
            [attended[:, head * rows : (head + 1) * rows] for head in range(heads)], axis=0
        )
        out[...] = lax.dot_general(
            attended, w_out[...], (((0,), (0,)), ((), ())), preferred_element_type=jnp.float32
        ).astype(jnp.bfloat16)


def residual_kernel(tokens, attention, partial, gain, residual, normed):
    summed = attention[...].astype(jnp.float32) + partial[...].astype(jnp.float32)
    rounded = (tokens[...].astype(jnp.float32) + summed).astype(jnp.bfloat16)
    residual[...] = rounded
    normed[...] = rms_scale(rounded.astype(jnp.float32), gain[...]).astype(jnp.bfloat16)


def slot_targets(routing, block, expert):
    table = routing[block].astype(jnp.float32)
    rows = table.shape[1] // 2
    named = table[:TOP, :rows] == expert.astype(jnp.float32)
    slot = jnp.max(jnp.where(named, table[:TOP, rows:], -1.0), axis=0, keepdims=True)
    weight = jnp.sum(jnp.where(named, table[TOP:, :rows], 0.0), axis=0, keepdims=True)
    return slot.astype(jnp.int32), weight * (1.0 / 1024.0)


def plane_targets(place, routing, count, distance, group):
    block, me = place[0], place[1]
    return [
        slot_targets(routing, block ^ (2 * group), (block ^ core) * count + (me ^ distance))
        for core in (0, 1)
    ]


def dispatch_kernel(group, capacity, place, routing, source, *outs):
    count = len(outs)
    slots = lax.broadcasted_iota(jnp.int32, (capacity, source.shape[0]), 0)
    parts = []
    for distance in range(count):
        for slot, _ in plane_targets(place, routing, count, distance, group):
            parts.append(jnp.where(slots == slot, 1.0, 0.0))
    hot = jnp.concatenate(parts, axis=0).astype(jnp.bfloat16)
    picked = jnp.dot(hot, source[...], preferred_element_type=jnp.float32).astype(jnp.bfloat16)
    for distance, out in enumerate(outs):
        out[...] = picked[2 * distance * capacity : 2 * (distance + 1) * capacity]


def combine_kernel(group, capacity, place, routing, *refs):
    *returned, out = refs
    count = len(returned)
    slots = lax.broadcasted_iota(jnp.int32, (capacity, out.shape[0]), 0)
    parts = []
    for distance in range(count):
        for slot, weight in plane_targets(place, routing, count, distance, group):
            parts.append(jnp.where(slots == slot, weight, 0.0))
    shares = jnp.concatenate(parts, axis=0).astype(jnp.bfloat16)
    produced = jnp.concatenate([ref[...] for ref in returned], axis=0)
    out[...] = lax.dot_general(
        shares, produced, (((0,), (0,)), ((), ())), preferred_element_type=jnp.float32
    ).astype(jnp.bfloat16)


def expert_kernel(*refs):
    *came, mate, w_gate, w_up, w_down, own, other, hidden = refs
    capacity = came[0].shape[0] // 2
    half = own.shape[0]
    rows = jnp.concatenate([ref[:capacity, :] for ref in came] + [mate[...]], axis=0)
    for first in range(0, hidden.shape[1], 256):
        cols = slice(first, first + 256)
        gate = jnp.dot(rows, w_gate[:, cols], preferred_element_type=jnp.float32)
        up = jnp.dot(rows, w_up[:, cols], preferred_element_type=jnp.float32)
        hidden[:, cols] = (gate / (1.0 + jnp.exp(-gate)) * up).astype(jnp.bfloat16)
    for first in range(0, w_down.shape[1], 512):
        cols = slice(first, first + 512)
        product = jnp.dot(hidden[...], w_down[:, cols], preferred_element_type=jnp.float32)
        product = product.astype(jnp.bfloat16)
        own[:, cols] = product[:half]
        other[:, cols] = product[half:]


def sum_kernel(*refs):
    *parts, out = refs
    total = parts[0][...].astype(jnp.float32)
    for part in parts[1:]:
        total = total + part[...].astype(jnp.float32)
    out[...] = total.astype(out.dtype)


def call(kernel, out_shape, specs, *args, name, scratch=(), limit=24, flops=1000):
    return pl.pallas_call(
        kernel,
        out_shape=out_shape,
        in_specs=specs,
        out_specs=jax.tree.map(lambda _: VMEM, out_shape),
        scratch_shapes=scratch,
        compiler_params=pltpu.CompilerParams(vmem_limit_bytes=limit * 1024 * 1024),
        cost_estimate=pl.CostEstimate(flops=flops, bytes_accessed=1000, transcendentals=0),
        name=name,
    )(*args)


def shards(
    tokens,
    ln1_gain,
    w_query,
    key_weight,
    value_weight,
    q_gain,
    k_gain,
    w_out,
    ln2_gain,
    expert_ids,
    route_weights,
    w_gate,
    w_up,
    w_down,
):
    rows, width = tokens.shape
    ctx_count = lax.axis_size("ctx")
    exp_count = lax.axis_size("exp")
    ctx_rows = rows * exp_count
    heads_dev = w_query.shape[1] // HEAD_SIZE
    group_width = QUERY_HEADS // KEY_VALUE_HEADS
    me_ctx = lax.axis_index("ctx").astype(jnp.int32)
    me_exp = lax.axis_index("exp").astype(jnp.int32)
    place = jnp.stack([me_ctx, me_exp] + [jnp.int32(0)] * exp_count)
    peers = list(range(exp_count))
    bf16 = functools.partial(jax.ShapeDtypeStruct, dtype=jnp.bfloat16)

    experts = ctx_count * exp_count
    capacity = max(2, 3 * rows * TOP // (2 * experts))
    capacity = -(-capacity // 16) * 16
    ln1_row = ln1_gain.reshape(1, width)
    own_first = me_ctx * ctx_rows + me_exp * rows
    cosine, sine = rope_tables(own_first + jnp.arange(rows))
    own_args = [
        expert_ids.T,
        route_weights.T,
        tokens,
        ln1_row,
        key_weight,
        value_weight,
        k_gain.reshape(1, HEAD_SIZE),
        cosine,
        sine,
    ]
    *own_kv, table = call(
        functools.partial(own_rows_kernel, experts, heads_dev),
        [bf16((rows, 2 * HEAD_SIZE)) for _ in peers] + [bf16((2 * TOP, 2 * rows))],
        [SMEM] + [ANY] * 9,
        place,
        *own_args,
        name="own_rows",
        scratch=[pltpu.VMEM(a.shape, a.dtype) for a in own_args] + [pltpu.SemaphoreType.DMA((18,))],
        limit=60,
    )
    block_kv = [own_kv[0]] + [swap(own_kv[d], "exp", d) for d in peers[1:]]
    both = lax.all_gather(jnp.concatenate(block_kv + [table], axis=0), "ctx", axis=0, tiled=True)
    sent = tie(tokens, *block_kv[1:])
    pieces = [tokens] + [swap(sent, "exp", d) for d in peers[1:]]
    routing = both.reshape(ctx_count, ctx_rows + 2 * TOP, 2 * HEAD_SIZE)[:, ctx_rows:]

    positions = jnp.concatenate(
        [me_ctx * ctx_rows + (me_exp ^ d) * rows + jnp.arange(rows) for d in peers]
    )
    cosine, sine = rope_tables(positions)
    queries = call(
        query_kernel,
        bf16((exp_count, heads_dev * rows, HEAD_SIZE)),
        [VMEM] * (exp_count + 5),
        *pieces,
        ln1_row,
        w_query,
        q_gain.reshape(1, HEAD_SIZE),
        cosine,
        sine,
        name="queries",
    )

    order = sorted(peers, key=lambda d: -bin(d).count("1"))
    partials, last = {}, ()
    for some in [[d] for d in order]:
        asked = queries[some[0] : some[0] + 1]
        made = call(
            functools.partial(attention_kernel, some, rows),
            [bf16((rows, width)) for _ in some],
            [SMEM, VMEM, VMEM, VMEM],
            place,
            tie(asked, *last),
            both,
            w_out,
            name="attention",
        )
        partials.update(zip(some, made))
        last = tuple(made)
    attention = partials[0]
    parts = [swap(partials[d], "exp", d) for d in order if d]
    for part in parts[:-1]:
        attention = call(
            sum_kernel,
            jax.ShapeDtypeStruct((rows, width), jnp.float32),
            [VMEM] * 2,
            attention,
            part,
            name="add",
            flops=3_000_000_000,
        )
    residual, normed = call(
        residual_kernel,
        [bf16((rows, width)), bf16((rows, width))],
        [VMEM] * 4,
        tokens,
        attention,
        parts[-1],
        ln2_gain.reshape(1, width),
        name="residual",
    )

    groups = ctx_count // 2
    far = [normed]
    for g in range(1, groups):
        far.append(swap(tie(normed, *([far[g - 1]] if g > 2 else [])), "ctx", 2 * g))
    in_flight = {d: () for d in peers[1:]}

    def send(array, d):
        came = swap(tie(array, *in_flight[d]), "exp", d)
        in_flight[d] = (came,)
        return came

    arrived = []
    for g in range(groups):
        outgoing = call(
            functools.partial(dispatch_kernel, g, capacity),
            [bf16((2 * capacity, width)) for _ in peers],
            [SMEM, VMEM, VMEM],
            place,
            routing,
            far[g],
            name="dispatch",
        )
        arrived.append([outgoing[0]] + [send(outgoing[d], d) for d in peers[1:]])

    produced = []
    half = exp_count * capacity
    for came in arrived:
        mate = swap(jnp.concatenate([rows_in[capacity:] for rows_in in came], axis=0), "ctx", 1)
        own, other = call(
            expert_kernel,
            [bf16((half, width)), bf16((half, width))],
            [VMEM] * (exp_count + 4),
            *came,
            mate,
            w_gate[0],
            w_up[0],
            w_down[0],
            name="expert",
            scratch=[pltpu.VMEM((2 * half, w_gate.shape[2]), jnp.bfloat16)],
        )
        produced.append((own, swap(other, "ctx", 1)))

    totals, hop = [], ()
    for g in [*range(2, groups), *(g for g in (1, 0) if g < groups)]:
        back = []
        for d in peers:
            mine = slice(d * capacity, (d + 1) * capacity)
            back.append(jnp.concatenate([part[mine] for part in produced[g]], axis=0))
        back = [back[0]] + [send(back[d], d) for d in peers[1:]]
        total = call(
            functools.partial(combine_kernel, g, capacity),
            bf16((rows, width)),
            [SMEM, VMEM] + [VMEM] * exp_count,
            place,
            routing,
            *back,
            name="combine",
        )
        if g:
            total = swap(tie(total, *(hop if g > 1 else ())), "ctx", 2 * g)
            hop = (total,)
        totals.append(total)
    early = call(
        sum_kernel,
        jax.ShapeDtypeStruct((rows, width), jnp.float32),
        [VMEM] * groups,
        residual,
        *totals[:-1],
        name="add",
        flops=10_000_000_000,
    )
    return call(
        sum_kernel, bf16((rows, width)), [VMEM] * 2, early, totals[-1], name="add"
    )


def solution(mesh):
    in_specs = (
        P(("ctx", "exp"), None),
        P(),
        P(None, "exp"),
        P(),
        P(),
        P(),
        P(),
        P("exp", None),
        P(),
        P(("ctx", "exp"), None),
        P(("ctx", "exp"), None),
        P(("ctx", "exp"), None, None),
        P(("ctx", "exp"), None, None),
        P(("ctx", "exp"), None, None),
    )
    out_specs = P(("ctx", "exp"), None)
    return jax.shard_map(shards, mesh=mesh, in_specs=in_specs, out_specs=out_specs, check_vma=False)
```

```python
import functools

import jax
import jax.numpy as jnp
from jax import lax
from jax.experimental import pallas as pl
from jax.experimental.pallas import tpu as pltpu
from jax.sharding import PartitionSpec as P

HEAD_SIZE = 128
QUERY_HEADS = 16
KEY_VALUE_HEADS = 2
TOP = 8
LOG2E = 1.4426950408889634

eps_value = 1e-06
theta_value = 1000000.0
floor_value = -1e30

VMEM = pl.BlockSpec(memory_space=pltpu.VMEM)
SMEM = pl.BlockSpec(memory_space=pltpu.SMEM)
ANY = pl.BlockSpec(memory_space=pl.ANY)


def rms_scale(value_states, norm_gain):
    return (
        value_states
        * lax.rsqrt(jnp.mean(value_states * value_states, axis=-1, keepdims=True) + eps_value)
        * norm_gain
    )


def swap(array, axis, distance):
    pairs = [(i, i ^ distance) for i in range(lax.axis_size(axis))]
    return lax.ppermute(array, axis, pairs)


def tie(array, *others):
    if not others:
        return array
    return lax.optimization_barrier((array, *others))[0]


def rope_tables(positions):
    half = HEAD_SIZE // 2
    frequency = theta_value ** (-2.0 * jnp.arange(half, dtype=jnp.float32) / HEAD_SIZE)
    angles = positions.astype(jnp.float32)[:, None] * frequency[None, :]
    return jnp.cos(angles), jnp.sin(angles)


def both_halves(cosine, sine):
    return jnp.concatenate([cosine, cosine], axis=1), jnp.concatenate([-sine, sine], axis=1)


def normed_rotated(states, gain, cosine, sine):
    states = rms_scale(states, gain)
    return states * cosine + pltpu.roll(states, HEAD_SIZE // 2, 1) * sine


def load_all(pairs, sems):
    copies = []
    for source, target in pairs:
        part = source.shape[0] // 4 if source.shape[0] >= 128 and source.shape[1] > 128 else source.shape[0]
        for first in range(0, source.shape[0], part):
            here = pl.ds(first, part)
            copies.append(
                pltpu.make_async_copy(source.at[here], target.at[here], sems.at[len(copies)])
            )
    for copy in copies:
        copy.start()
    return copies


def own_rows_kernel(experts, heads_dev, place, *refs):
    peers = len(refs) - 20
    sources, outs, table, targets, sems = refs[:9], refs[9:-11], refs[-11], refs[-10:-1], refs[-1]
    copies = load_all(list(zip(sources, targets)), sems)
    ids, shares, tokens, gain, key_weight, value_weight, k_gain, cosine, sine = targets
    copies[0].wait()
    copies[1].wait()
    rows = tokens.shape[0]
    chosen_ids = ids[...]
    lanes = lax.broadcasted_iota(jnp.int32, (experts, rows), 0)
    chosen = jnp.zeros((experts, rows), jnp.float32)
    for k in range(TOP):
        chosen = chosen + jnp.where(lanes == chosen_ids[k : k + 1], 1.0, 0.0)
    earlier = lax.broadcasted_iota(jnp.int32, (rows, rows), 0) < lax.broadcasted_iota(
        jnp.int32, (rows, rows), 1
    )
    rank = jnp.dot(
        chosen.astype(jnp.bfloat16),
        jnp.where(earlier, 1.0, 0.0).astype(jnp.bfloat16),
        preferred_element_type=jnp.float32,
    )
    slots = [
        jnp.sum(jnp.where(lanes == chosen_ids[k : k + 1], rank, 0.0), axis=0, keepdims=True)
        for k in range(TOP)
    ]
    slots = jnp.concatenate(slots, axis=0)
    left = jnp.concatenate([chosen_ids, shares[...]], axis=0).astype(jnp.float32)
    table[:, :rows] = left.astype(jnp.bfloat16)
    table[:, rows:] = jnp.concatenate([slots, jnp.zeros_like(slots)], axis=0).astype(jnp.bfloat16)
    for copy in copies[2:]:
        copy.wait()
    normed = rms_scale(tokens[...].astype(jnp.float32), gain[...]).astype(jnp.bfloat16)
    keys = jnp.dot(normed, key_weight[...], preferred_element_type=jnp.float32)
    values = jnp.dot(normed, value_weight[...], preferred_element_type=jnp.float32)
    cosine, sine = both_halves(cosine[...], sine[...])
    for head in range(KEY_VALUE_HEADS):
        cols = slice(head * HEAD_SIZE, (head + 1) * HEAD_SIZE)
        rotated = normed_rotated(keys[:, cols], k_gain[...], cosine, sine)
        pair = jnp.concatenate([rotated, values[:, cols]], axis=1).astype(jnp.bfloat16)
        for distance in range(peers):
            asked = (place[1] ^ distance) * heads_dev // (QUERY_HEADS // KEY_VALUE_HEADS)

            @pl.when(asked == head)
            def _(out=outs[distance], pair=pair):
                out[...] = pair


def query_kernel(*refs):
    *pieces, gain, w_query, q_gain, cosine, sine, out = refs
    rows = pieces[0].shape[0]
    heads = w_query.shape[1] // HEAD_SIZE
    for at, piece in enumerate(pieces):
        normed = rms_scale(piece[...].astype(jnp.float32), gain[...]).astype(jnp.bfloat16)
        queries = jnp.dot(normed, w_query[...], preferred_element_type=jnp.float32)
        here = pl.ds(at * rows, rows)
        turn = both_halves(cosine[here, :], sine[here, :])
        for head in range(heads):
            cols = slice(head * HEAD_SIZE, (head + 1) * HEAD_SIZE)
            rotated = normed_rotated(queries[:, cols], q_gain[...], *turn)
            out[at, pl.ds(head * rows, rows), :] = rotated.astype(jnp.bfloat16)


def attention_kernel(distances, rows, place, queries, both, w_out, *outs):
    block, me = place[0], place[1]
    heads = w_out.shape[0] // HEAD_SIZE
    width = heads * rows
    span = rows * (place.shape[0] - 2)
    stride = span + 2 * TOP
    scale = HEAD_SIZE ** (-0.5) * LOG2E

    def step(first, states, masked):
        keys = both[pl.ds(first, span), :HEAD_SIZE]
        values = both[pl.ds(first, span), HEAD_SIZE:]
        result = []
        for at, (top, total, mixed) in enumerate(states):
            scores = lax.dot_general(
                keys, queries[at], (((1,), (1,)), ((), ())), preferred_element_type=jnp.float32
            )
            if masked:
                row = lax.broadcasted_iota(jnp.int32, (span, width), 0)
                key_pos = (me ^ (row // rows)) * rows + row % rows
                query = lax.broadcasted_iota(jnp.int32, (span, width), 1) % rows
                query_pos = (me ^ distances[at]) * rows + query
                scores = jnp.where(key_pos <= query_pos, scores, floor_value)
            new_top = jnp.maximum(top, jnp.max(scores, axis=0, keepdims=True))
            weights = jnp.exp2((scores - new_top) * scale)
            rescale = jnp.exp2((top - new_top) * scale)
            total = total * rescale + jnp.sum(weights, axis=0, keepdims=True)
            mixed = mixed * rescale + lax.dot_general(
                values,
                weights.astype(jnp.bfloat16),
                (((0,), (0,)), ((), ())),
                preferred_element_type=jnp.float32,
            )
            result.append((new_top, total, mixed))
        return tuple(result)

    states = tuple(
        (
            jnp.full((1, width), floor_value, jnp.float32),
            jnp.zeros((1, width), jnp.float32),
            jnp.zeros((HEAD_SIZE, width), jnp.float32),
        )
        for _ in distances
    )
    states = step(pl.multiple_of(block * stride, 2 * TOP), states, True)
    states = lax.fori_loop(
        0, block, lambda i, s: step(pl.multiple_of(i * stride, 2 * TOP), s, False), states
    )
    for (_, total, mixed), out in zip(states, outs):
        attended = (mixed / total).astype(jnp.bfloat16)
        attended = jnp.concatenate(
            [attended[:, head * rows : (head + 1) * rows] for head in range(heads)], axis=0
        )
        out[...] = lax.dot_general(
            attended, w_out[...], (((0,), (0,)), ((), ())), preferred_element_type=jnp.float32
        ).astype(jnp.bfloat16)


def residual_kernel(tokens, attention, partial, gain, residual, normed):
    summed = attention[...].astype(jnp.float32) + partial[...].astype(jnp.float32)
    rounded = (tokens[...].astype(jnp.float32) + summed).astype(jnp.bfloat16)
    residual[...] = rounded
    normed[...] = rms_scale(rounded.astype(jnp.float32), gain[...]).astype(jnp.bfloat16)


def slot_targets(table, expert):
    table = table.astype(jnp.float32)
    rows = table.shape[1] // 2
    named = table[:TOP, :rows] == expert.astype(jnp.float32)
    slot = jnp.max(jnp.where(named, table[:TOP, rows:], -1.0), axis=0, keepdims=True)
    weight = jnp.sum(jnp.where(named, table[TOP:, :rows], 0.0), axis=0, keepdims=True)
    return slot.astype(jnp.int32), weight * (1.0 / 1024.0)


def plane_targets(group, place, routing, near, away):
    block, me, count = place[0], place[1], routing.shape[0]
    table = routing[near, block ^ (2 * group)]
    return [slot_targets(table, (block ^ core) * count + (me ^ away)) for core in (0, 1)]


def route_order(route):
    near, away = route
    return [n ^ a for a in away for n in near]


def dispatch_kernel(routes, group, capacity, place, routing, *refs):
    sources = refs[: sum(len(near) for near, _ in routes)]
    outs = refs[len(sources) :]
    rows = sources[0].shape[0]
    slots = lax.broadcasted_iota(jnp.int32, (capacity, rows), 0)
    for near, away in routes:
        some, sources = sources[: len(near)], sources[len(near) :]
        mine, outs = outs[: len(away)], outs[len(away) :]
        for at, (n, source) in enumerate(zip(near, some)):
            parts = []
            for a in away:
                for slot, _ in plane_targets(group, place, routing, n, a):
                    parts.append(jnp.where(slots == slot, 1.0, 0.0))
            hot = jnp.concatenate(parts, axis=0).astype(jnp.bfloat16)
            picked = jnp.dot(hot, source[...], preferred_element_type=jnp.float32)
            picked = picked.astype(jnp.bfloat16)
            for part in range(2 * len(away)):
                first = ((part % 2) * len(near) + at) * capacity
                mine[part // 2][first : first + capacity, :] = picked[
                    part * capacity : (part + 1) * capacity
                ]


def combine_kernel(routes, group, capacity, place, routing, *refs):
    arrived = refs[: sum(len(away) + 1 for _, away in routes)]
    kept, *outs = refs[len(arrived) :]
    rows, width = kept.shape[0], arrived[0].shape[1]
    slots = lax.broadcasted_iota(jnp.int32, (capacity, rows), 0)
    for side, (near, away) in enumerate(routes):
        some, arrived = arrived[: len(away) + 1], arrived[len(away) + 1 :]
        for at, n in enumerate(near):
            shares, produced = [], []
            for index, a in enumerate(away):
                for core, (slot, weight) in enumerate(plane_targets(group, place, routing, n, a)):
                    shares.append(jnp.where(slots == slot, weight, 0.0))
                    piece = some[index + 1] if index else some[core]
                    first = ((core if index else 0) * len(near) + at) * capacity
                    produced.append(piece[first : first + capacity, :])
            total = lax.dot_general(
                jnp.concatenate(shares, axis=0).astype(jnp.bfloat16),
                jnp.concatenate(produced, axis=0),
                (((0,), (0,)), ((), ())),
                preferred_element_type=jnp.float32,
            )
            if n:
                outs[0][...] = total.astype(jnp.bfloat16)
                outs = outs[1:]
            else:
                kept[:, side * width : (side + 1) * width] = total


def gather_kernel(kept, *refs):
    *parts, out = refs
    width = parts[0].shape[1]
    count = out.shape[1] // width
    first = 0
    for side, some in enumerate(split_parts(parts, count)):
        cols = slice(first, first + width)
        total = kept[:, cols]
        for part in some:
            total = total + part[...].astype(jnp.float32)
        out[:, cols] = total.astype(out.dtype)
        first += width


def split_parts(parts, count):
    assert count == 2
    return parts[:1], parts[1:]


def expert_kernel(routes, capacity, *refs):
    count = sum(len(away) for _, away in routes)
    came, (mate, w_gate, w_up, w_down) = refs[:count], refs[count : count + 4]
    own, other = refs[count + 4 : 2 * count + 4], refs[2 * count + 4 : 3 * count + 4]
    rows_in, hidden = refs[3 * count + 4 :]
    width = came[0].shape[1]
    half = rows_in.shape[1] // 2
    places = []
    for side, (near, away) in enumerate(routes):
        base = sum(len(some) for _, some in routes[:side])
        for at, d in enumerate(route_order((near, away))):
            places.append((side, base + at // len(near), (at % len(near)) * capacity, d * capacity))
    for at, (side, piece, first, to) in enumerate(places):
        rows_in[side, to : to + capacity, :] = came[piece][first : first + capacity, :]
        to = half + to
        rows_in[side, to : to + capacity, :] = mate[at * capacity : (at + 1) * capacity, :]
    for first in range(0, hidden.shape[1], 256):
        cols = slice(first, first + 256)
        gate = up = 0.0
        for side in range(len(routes)):
            depth = slice(side * width, (side + 1) * width)
            rows = rows_in[side]
            gate = gate + jnp.dot(rows, w_gate[depth, cols], preferred_element_type=jnp.float32)
            up = up + jnp.dot(rows, w_up[depth, cols], preferred_element_type=jnp.float32)
        hidden[:, cols] = (gate / (1.0 + jnp.exp(-gate)) * up).astype(jnp.bfloat16)
    for side in range(len(routes)):
        for first in range(0, width, 256):
            cols = slice(first, first + 256)
            down = w_down[:, side * width + first : side * width + first + 256]
            product = jnp.dot(hidden[...], down, preferred_element_type=jnp.float32)
            product = product.astype(jnp.bfloat16)
            for where, piece, to, at in places:
                if where == side:
                    here = slice(to, to + capacity)
                    own[piece][here, cols] = product[at : at + capacity]
                    other[piece][here, cols] = product[half + at : half + at + capacity]


def sum_kernel(*refs):
    *parts, out = refs
    total = parts[0][...].astype(jnp.float32)
    for part in parts[1:]:
        total = total + part[...].astype(jnp.float32)
    out[...] = total.astype(out.dtype)


def call(kernel, out_shape, specs, *args, name, scratch=(), limit=24, flops=1000):
    return pl.pallas_call(
        kernel,
        out_shape=out_shape,
        in_specs=specs,
        out_specs=jax.tree.map(lambda _: VMEM, out_shape),
        scratch_shapes=scratch,
        compiler_params=pltpu.CompilerParams(vmem_limit_bytes=limit * 1024 * 1024),
        cost_estimate=pl.CostEstimate(flops=flops, bytes_accessed=1000, transcendentals=0),
        name=name,
    )(*args)


def shards(
    tokens,
    ln1_gain,
    w_query,
    key_weight,
    value_weight,
    q_gain,
    k_gain,
    w_out,
    ln2_gain,
    expert_ids,
    route_weights,
    w_gate,
    w_up,
    w_down,
):
    rows, width = tokens.shape
    ctx_count = lax.axis_size("ctx")
    exp_count = lax.axis_size("exp")
    ctx_rows = rows * exp_count
    heads_dev = w_query.shape[1] // HEAD_SIZE
    group_width = QUERY_HEADS // KEY_VALUE_HEADS
    me_ctx = lax.axis_index("ctx").astype(jnp.int32)
    me_exp = lax.axis_index("exp").astype(jnp.int32)
    place = jnp.stack([me_ctx, me_exp] + [jnp.int32(0)] * exp_count)
    peers = list(range(exp_count))
    bf16 = functools.partial(jax.ShapeDtypeStruct, dtype=jnp.bfloat16)

    experts = ctx_count * exp_count
    capacity = max(2, 3 * rows * TOP // (2 * experts))
    capacity = -(-capacity // 16) * 16
    ln1_row = ln1_gain.reshape(1, width)
    own_first = me_ctx * ctx_rows + me_exp * rows
    cosine, sine = rope_tables(own_first + jnp.arange(rows))
    own_args = [
        expert_ids.T,
        route_weights.T,
        tokens,
        ln1_row,
        key_weight,
        value_weight,
        k_gain.reshape(1, HEAD_SIZE),
        cosine,
        sine,
    ]
    *own_kv, table = call(
        functools.partial(own_rows_kernel, experts, heads_dev),
        [bf16((rows, 2 * HEAD_SIZE)) for _ in peers] + [bf16((2 * TOP, 2 * rows))],
        [SMEM] + [ANY] * 9,
        place,
        *own_args,
        name="own_rows",
        scratch=[pltpu.VMEM(a.shape, a.dtype) for a in own_args] + [pltpu.SemaphoreType.DMA((18,))],
        limit=60,
    )
    block_kv = [own_kv[0]] + [swap(own_kv[d], "exp", d) for d in peers[1:]]
    both = lax.all_gather(jnp.concatenate(block_kv + [table], axis=0), "ctx", axis=0, tiled=True)
    sent = tie(tokens, *block_kv[1:])
    pieces = [tokens] + [swap(sent, "exp", d) for d in peers[1:]]
    routing = both.reshape(ctx_count, ctx_rows + 2 * TOP, 2 * HEAD_SIZE)[:, ctx_rows:]
    routing = jnp.stack([routing] + [swap(routing, "exp", d) for d in peers[1:]], axis=0)

    positions = jnp.concatenate(
        [me_ctx * ctx_rows + (me_exp ^ d) * rows + jnp.arange(rows) for d in peers]
    )
    cosine, sine = rope_tables(positions)
    queries = call(
        query_kernel,
        bf16((exp_count, heads_dev * rows, HEAD_SIZE)),
        [VMEM] * (exp_count + 5),
        *pieces,
        ln1_row,
        w_query,
        q_gain.reshape(1, HEAD_SIZE),
        cosine,
        sine,
        name="queries",
    )

    order = sorted(peers, key=lambda d: -bin(d).count("1"))
    partials, last = {}, ()
    for some in [[d] for d in order]:
        asked = queries[some[0] : some[0] + 1]
        made = call(
            functools.partial(attention_kernel, some, rows),
            [bf16((rows, width)) for _ in some],
            [SMEM, VMEM, VMEM, VMEM],
            place,
            tie(asked, *last, *([routing] if last else [])),
            both,
            w_out,
            name="attention",
        )
        partials.update(zip(some, made))
        last = tuple(made)
    attention = partials[0]
    parts = [swap(partials[d], "exp", d) for d in order if d]
    for part in parts[:-1]:
        attention = call(
            sum_kernel,
            jax.ShapeDtypeStruct((rows, width), jnp.float32),
            [VMEM] * 2,
            attention,
            part,
            name="add",
            flops=3_000_000_000,
        )
    residual, normed = call(
        residual_kernel,
        [bf16((rows, width)), bf16((rows, width))],
        [VMEM] * 4,
        tokens,
        attention,
        parts[-1],
        ln2_gain.reshape(1, width),
        name="residual",
    )

    groups = ctx_count // 2
    low, high = [0, 1], list(range(0, exp_count, 2))
    routes = [(low, high), (high, low)]
    half = width // 2
    far = [normed]
    for g in range(1, groups):
        far.append(swap(tie(normed, *([far[g - 1]] if g > 2 else [])), "ctx", 2 * g))
    in_flight = {}

    def send(array, d, kind):
        came = swap(tie(array, *in_flight.get((kind, d), ())), "exp", d)
        in_flight[kind, d] = (came,)
        return came

    arrived = []
    for g in range(groups):
        sources = []
        for side, (near, _) in enumerate(routes):
            part = far[g][:, side * half : (side + 1) * half]
            sources += [part] + [send(part, n, "whole") for n in near[1:]]
        outgoing = call(
            functools.partial(dispatch_kernel, routes, g, capacity),
            [bf16((2 * len(near) * capacity, half)) for near, away in routes for _ in away],
            [SMEM, VMEM] + [VMEM] * len(sources),
            place,
            routing,
            *sources,
            name="dispatch",
        )
        onward = [a for _, away in routes for a in away]
        arrived.append([send(out, a, "picked") if a else out for out, a in zip(outgoing, onward)])

    produced = []
    slots = exp_count * capacity
    for came in arrived:
        mate = jnp.concatenate([part[part.shape[0] // 2 :] for part in came], axis=0)
        made = call(
            functools.partial(expert_kernel, routes, capacity),
            [bf16((len(near) * capacity, half)) for near, away in routes for _ in away] * 2,
            [VMEM] * (len(came) + 4),
            *came,
            swap(mate, "ctx", 1),
            w_gate[0],
            w_up[0],
            w_down[0],
            name="expert",
            scratch=[
                pltpu.VMEM((2, 2 * slots, half), jnp.bfloat16),
                pltpu.VMEM((2 * slots, w_gate.shape[2]), jnp.bfloat16),
            ],
        )
        own, other = made[: len(came)], made[len(came) :]
        produced.append([(mine, swap(mates, "ctx", 1)) for mine, mates in zip(own, other)])

    totals, hop = [], ()
    for g in [*range(2, groups), *(g for g in (1, 0) if g < groups)]:
        back, pieces = [], iter(produced[g])
        for _, away in routes:
            for a in away:
                pair = next(pieces)
                back += [send(jnp.concatenate(pair, axis=0), a, "picked")] if a else pair
        onward = [n for near, _ in routes for n in near[1:]]
        kept, *sums = call(
            functools.partial(combine_kernel, routes, g, capacity),
            [jax.ShapeDtypeStruct((rows, width), jnp.float32)] + [bf16((rows, half)) for _ in onward],
            [SMEM, VMEM] + [VMEM] * len(back),
            place,
            routing,
            *back,
            name="combine",
        )
        sums = [send(part, n, "whole") for part, n in zip(sums, onward)]
        total = call(
            gather_kernel,
            bf16((rows, width)),
            [VMEM] * (1 + len(sums)),
            kept,
            *sums,
            name="gather",
        )
        if g:
            total = swap(tie(total, *(hop if g > 1 else ())), "ctx", 2 * g)
            hop = (total,)
        totals.append(total)
    early = call(
        sum_kernel,
        jax.ShapeDtypeStruct((rows, width), jnp.float32),
        [VMEM] * groups,
        residual,
        *totals[:-1],
        name="add",
        flops=10_000_000_000,
    )
    return call(
        sum_kernel, bf16((rows, width)), [VMEM] * 2, early, totals[-1], name="add"
    )


def solution(mesh):
    in_specs = (
        P(("ctx", "exp"), None),
        P(),
        P(None, "exp"),
        P(),
        P(),
        P(),
        P(),
        P("exp", None),
        P(),
        P(("ctx", "exp"), None),
        P(("ctx", "exp"), None),
        P(("ctx", "exp"), None, None),
        P(("ctx", "exp"), None, None),
        P(("ctx", "exp"), None, None),
    )
    out_specs = P(("ctx", "exp"), None)
    return jax.shard_map(shards, mesh=mesh, in_specs=in_specs, out_specs=out_specs, check_vma=False)
```

```python
import functools

import jax
import jax.numpy as jnp
from jax import lax
from jax.experimental import pallas as pl
from jax.experimental.pallas import tpu as pltpu
from jax.sharding import PartitionSpec as P

HEAD_SIZE = 128
QUERY_HEADS = 16
KEY_VALUE_HEADS = 2
TOP = 8
LOG2E = 1.4426950408889634

eps_value = 1e-06
theta_value = 1000000.0
floor_value = -1e30

VMEM = pl.BlockSpec(memory_space=pltpu.VMEM)
SMEM = pl.BlockSpec(memory_space=pltpu.SMEM)
ANY = pl.BlockSpec(memory_space=pl.ANY)


def rms_scale(value_states, norm_gain):
    return (
        value_states
        * lax.rsqrt(jnp.mean(value_states * value_states, axis=-1, keepdims=True) + eps_value)
        * norm_gain
    )


def swap(array, axis, distance):
    pairs = [(i, i ^ distance) for i in range(lax.axis_size(axis))]
    return lax.ppermute(array, axis, pairs)


def tie(array, *others):
    if not others:
        return array
    return lax.optimization_barrier((array, *others))[0]


def rope_tables(positions):
    half = HEAD_SIZE // 2
    frequency = theta_value ** (-2.0 * jnp.arange(half, dtype=jnp.float32) / HEAD_SIZE)
    angles = positions.astype(jnp.float32)[:, None] * frequency[None, :]
    return jnp.cos(angles), jnp.sin(angles)


def both_halves(cosine, sine):
    return jnp.concatenate([cosine, cosine], axis=1), jnp.concatenate([-sine, sine], axis=1)


def normed_rotated(states, gain, cosine, sine):
    states = rms_scale(states, gain)
    return states * cosine + pltpu.roll(states, HEAD_SIZE // 2, 1) * sine


def load_all(pairs, sems):
    copies = []
    for source, target in pairs:
        part = source.shape[0] // 4 if source.shape[0] >= 128 and source.shape[1] > 128 else source.shape[0]
        for first in range(0, source.shape[0], part):
            here = pl.ds(first, part)
            copies.append(
                pltpu.make_async_copy(source.at[here], target.at[here], sems.at[len(copies)])
            )
    for copy in copies:
        copy.start()
    return copies


def own_rows_kernel(experts, heads_dev, place, *refs):
    peers = len(refs) - 19
    sources, outs, targets, sems = refs[:9], refs[9:-10], refs[-10:-1], refs[-1]
    copies = load_all(list(zip(sources, targets)), sems)
    ids, shares, tokens, gain, key_weight, value_weight, k_gain, cosine, sine = targets
    copies[0].wait()
    copies[1].wait()
    rows = tokens.shape[0]
    chosen_ids = ids[...]
    lanes = lax.broadcasted_iota(jnp.int32, (experts, rows), 0)
    chosen = jnp.zeros((experts, rows), jnp.float32)
    for k in range(TOP):
        chosen = chosen + jnp.where(lanes == chosen_ids[k : k + 1], 1.0, 0.0)
    earlier = lax.broadcasted_iota(jnp.int32, (rows, rows), 0) < lax.broadcasted_iota(
        jnp.int32, (rows, rows), 1
    )
    rank = jnp.dot(
        chosen.astype(jnp.bfloat16),
        jnp.where(earlier, 1.0, 0.0).astype(jnp.bfloat16),
        preferred_element_type=jnp.float32,
    )
    slots = [
        jnp.sum(jnp.where(lanes == chosen_ids[k : k + 1], rank, 0.0), axis=0, keepdims=True)
        for k in range(TOP)
    ]
    slots = jnp.concatenate(slots, axis=0)
    left = jnp.concatenate([chosen_ids, shares[...]], axis=0).astype(jnp.float32)
    right = jnp.concatenate([slots, jnp.zeros_like(slots)], axis=0)
    for out in outs:
        out[rows:, :] = jnp.concatenate([left, right], axis=1).astype(jnp.bfloat16)
    for copy in copies[2:]:
        copy.wait()
    normed = rms_scale(tokens[...].astype(jnp.float32), gain[...]).astype(jnp.bfloat16)
    keys = jnp.dot(normed, key_weight[...], preferred_element_type=jnp.float32)
    values = jnp.dot(normed, value_weight[...], preferred_element_type=jnp.float32)
    cosine, sine = both_halves(cosine[...], sine[...])
    for head in range(KEY_VALUE_HEADS):
        cols = slice(head * HEAD_SIZE, (head + 1) * HEAD_SIZE)
        rotated = normed_rotated(keys[:, cols], k_gain[...], cosine, sine)
        pair = jnp.concatenate([rotated, values[:, cols]], axis=1).astype(jnp.bfloat16)
        for distance in range(peers):
            asked = (place[1] ^ distance) * heads_dev // (QUERY_HEADS // KEY_VALUE_HEADS)

            @pl.when(asked == head)
            def _(out=outs[distance], pair=pair):
                out[:rows, :] = pair


def query_kernel(*refs):
    *pieces, gain, w_query, q_gain, cosine, sine, out = refs
    rows = pieces[0].shape[0]
    heads = w_query.shape[1] // HEAD_SIZE
    for at, piece in enumerate(pieces):
        normed = rms_scale(piece[...].astype(jnp.float32), gain[...]).astype(jnp.bfloat16)
        queries = jnp.dot(normed, w_query[...], preferred_element_type=jnp.float32)
        here = pl.ds(at * rows, rows)
        turn = both_halves(cosine[here, :], sine[here, :])
        for head in range(heads):
            cols = slice(head * HEAD_SIZE, (head + 1) * HEAD_SIZE)
            rotated = normed_rotated(queries[:, cols], q_gain[...], *turn)
            out[at, pl.ds(head * rows, rows), :] = rotated.astype(jnp.bfloat16)


def attention_kernel(distances, rows, place, queries, both, w_out, *outs):
    block, me = place[0], place[1]
    heads = w_out.shape[0] // HEAD_SIZE
    width = heads * rows
    span = rows * (place.shape[0] - 2)
    stride = span + 2 * TOP * (place.shape[0] - 2)
    scale = HEAD_SIZE ** (-0.5) * LOG2E

    def step(first, states, masked):
        keys = both[pl.ds(first, span), :HEAD_SIZE]
        values = both[pl.ds(first, span), HEAD_SIZE:]
        result = []
        for at, (top, total, mixed) in enumerate(states):
            scores = lax.dot_general(
                keys, queries[at], (((1,), (1,)), ((), ())), preferred_element_type=jnp.float32
            )
            if masked:
                row = lax.broadcasted_iota(jnp.int32, (span, width), 0)
                key_pos = (me ^ (row // rows)) * rows + row % rows
                query = lax.broadcasted_iota(jnp.int32, (span, width), 1) % rows
                query_pos = (me ^ distances[at]) * rows + query
                scores = jnp.where(key_pos <= query_pos, scores, floor_value)
            new_top = jnp.maximum(top, jnp.max(scores, axis=0, keepdims=True))
            weights = jnp.exp2((scores - new_top) * scale)
            rescale = jnp.exp2((top - new_top) * scale)
            total = total * rescale + jnp.sum(weights, axis=0, keepdims=True)
            mixed = mixed * rescale + lax.dot_general(
                values,
                weights.astype(jnp.bfloat16),
                (((0,), (0,)), ((), ())),
                preferred_element_type=jnp.float32,
            )
            result.append((new_top, total, mixed))
        return tuple(result)

    states = tuple(
        (
            jnp.full((1, width), floor_value, jnp.float32),
            jnp.zeros((1, width), jnp.float32),
            jnp.zeros((HEAD_SIZE, width), jnp.float32),
        )
        for _ in distances
    )
    states = step(pl.multiple_of(block * stride, 2 * TOP), states, True)
    states = lax.fori_loop(
        0, block, lambda i, s: step(pl.multiple_of(i * stride, 2 * TOP), s, False), states
    )
    for (_, total, mixed), out in zip(states, outs):
        attended = (mixed / total).astype(jnp.bfloat16)
        attended = jnp.concatenate(
            [attended[:, head * rows : (head + 1) * rows] for head in range(heads)], axis=0
        )
        out[...] = lax.dot_general(
            attended, w_out[...], (((0,), (0,)), ((), ())), preferred_element_type=jnp.float32
        ).astype(jnp.bfloat16)


def residual_kernel(tokens, attention, partial, gain, residual, normed):
    summed = attention[...].astype(jnp.float32) + partial[...].astype(jnp.float32)
    rounded = (tokens[...].astype(jnp.float32) + summed).astype(jnp.bfloat16)
    residual[...] = rounded
    normed[...] = rms_scale(rounded.astype(jnp.float32), gain[...]).astype(jnp.bfloat16)


def slot_targets(table, expert):
    table = table.astype(jnp.float32)
    rows = table.shape[1] // 2
    named = table[:TOP, :rows] == expert.astype(jnp.float32)
    slot = jnp.max(jnp.where(named, table[:TOP, rows:], -1.0), axis=0, keepdims=True)
    weight = jnp.sum(jnp.where(named, table[TOP:, :rows], 0.0), axis=0, keepdims=True)
    return slot.astype(jnp.int32), weight * (1.0 / 1024.0)


def plane_targets(group, place, routing, near, away):
    block, me, count = place[0], place[1], routing.shape[1]
    table = routing[block ^ (2 * group), near]
    return [slot_targets(table, (block ^ core) * count + (me ^ away)) for core in (0, 1)]


def route_order(route):
    near, away = route
    return [n ^ a for a in away for n in near]


def dispatch_kernel(routes, group, capacity, place, routing, *refs):
    sources = refs[: sum(len(near) for near, _ in routes)]
    outs = refs[len(sources) :]
    rows = sources[0].shape[0]
    slots = lax.broadcasted_iota(jnp.int32, (capacity, rows), 0)
    for near, away in routes:
        some, sources = sources[: len(near)], sources[len(near) :]
        mine, outs = outs[: len(away)], outs[len(away) :]
        for at, (n, source) in enumerate(zip(near, some)):
            parts = []
            for a in away:
                for slot, _ in plane_targets(group, place, routing, n, a):
                    parts.append(jnp.where(slots == slot, 1.0, 0.0))
            hot = jnp.concatenate(parts, axis=0).astype(jnp.bfloat16)
            picked = jnp.dot(hot, source[...], preferred_element_type=jnp.float32)
            picked = picked.astype(jnp.bfloat16)
            for part in range(2 * len(away)):
                first = ((part % 2) * len(near) + at) * capacity
                mine[part // 2][first : first + capacity, :] = picked[
                    part * capacity : (part + 1) * capacity
                ]


def combine_kernel(routes, group, capacity, place, routing, *refs):
    arrived = refs[: sum(len(away) + 1 for _, away in routes)]
    kept, *outs = refs[len(arrived) :]
    rows, width = kept.shape[0], arrived[0].shape[1]
    slots = lax.broadcasted_iota(jnp.int32, (capacity, rows), 0)
    for side, (near, away) in enumerate(routes):
        some, arrived = arrived[: len(away) + 1], arrived[len(away) + 1 :]
        for at, n in enumerate(near):
            shares, produced = [], []
            for index, a in enumerate(away):
                for core, (slot, weight) in enumerate(plane_targets(group, place, routing, n, a)):
                    shares.append(jnp.where(slots == slot, weight, 0.0))
                    piece = some[index + 1] if index else some[core]
                    first = ((core if index else 0) * len(near) + at) * capacity
                    produced.append(piece[first : first + capacity, :])
            total = lax.dot_general(
                jnp.concatenate(shares, axis=0).astype(jnp.bfloat16),
                jnp.concatenate(produced, axis=0),
                (((0,), (0,)), ((), ())),
                preferred_element_type=jnp.float32,
            )
            if n:
                outs[0][...] = total.astype(jnp.bfloat16)
                outs = outs[1:]
            else:
                kept[:, side * width : (side + 1) * width] = total


def gather_kernel(counts, kept, *refs):
    *parts, out = refs
    width = out.shape[1] // len(counts)
    for side, count in enumerate(counts):
        cols = slice(side * width, (side + 1) * width)
        total = kept[:, cols]
        for part in parts[:count]:
            total = total + part[...].astype(jnp.float32)
        parts = parts[count:]
        for part in parts[sum(counts[side + 1 :]) :]:
            total = total + part[:, cols].astype(jnp.float32)
        out[:, cols] = total.astype(out.dtype)


def expert_kernel(routes, capacity, *refs):
    count = sum(len(away) for _, away in routes)
    came, (mate, w_gate, w_up, w_down) = refs[:count], refs[count : count + 4]
    own, other = refs[count + 4 : 2 * count + 4], refs[2 * count + 4 : 3 * count + 4]
    rows_in, hidden = refs[3 * count + 4 :]
    width = came[0].shape[1]
    half = rows_in.shape[1] // 2
    places = []
    for side, (near, away) in enumerate(routes):
        base = sum(len(some) for _, some in routes[:side])
        for at, d in enumerate(route_order((near, away))):
            places.append((side, base + at // len(near), (at % len(near)) * capacity, d * capacity))
    for at, (side, piece, first, to) in enumerate(places):
        rows_in[side, to : to + capacity, :] = came[piece][first : first + capacity, :]
        to = half + to
        rows_in[side, to : to + capacity, :] = mate[at * capacity : (at + 1) * capacity, :]
    for first in range(0, hidden.shape[1], 256):
        cols = slice(first, first + 256)
        gate = up = 0.0
        for side in range(len(routes)):
            depth = slice(side * width, (side + 1) * width)
            rows = rows_in[side]
            gate = gate + jnp.dot(rows, w_gate[depth, cols], preferred_element_type=jnp.float32)
            up = up + jnp.dot(rows, w_up[depth, cols], preferred_element_type=jnp.float32)
        hidden[:, cols] = (gate / (1.0 + jnp.exp(-gate)) * up).astype(jnp.bfloat16)
    for side in range(len(routes)):
        for first in range(0, width, 256):
            cols = slice(first, first + 256)
            down = w_down[:, side * width + first : side * width + first + 256]
            product = jnp.dot(hidden[...], down, preferred_element_type=jnp.float32)
            product = product.astype(jnp.bfloat16)
            for where, piece, to, at in places:
                if where == side:
                    here = slice(to, to + capacity)
                    own[piece][here, cols] = product[at : at + capacity]
                    other[piece][here, cols] = product[half + at : half + at + capacity]


def sum_kernel(*refs):
    *parts, out = refs
    total = parts[0][...].astype(jnp.float32)
    for part in parts[1:]:
        total = total + part[...].astype(jnp.float32)
    out[...] = total.astype(out.dtype)


def call(kernel, out_shape, specs, *args, name, scratch=(), limit=24, flops=1000):
    return pl.pallas_call(
        kernel,
        out_shape=out_shape,
        in_specs=specs,
        out_specs=jax.tree.map(lambda _: VMEM, out_shape),
        scratch_shapes=scratch,
        compiler_params=pltpu.CompilerParams(vmem_limit_bytes=limit * 1024 * 1024),
        cost_estimate=pl.CostEstimate(flops=flops, bytes_accessed=1000, transcendentals=0),
        name=name,
    )(*args)


def shards(
    tokens,
    ln1_gain,
    w_query,
    key_weight,
    value_weight,
    q_gain,
    k_gain,
    w_out,
    ln2_gain,
    expert_ids,
    route_weights,
    w_gate,
    w_up,
    w_down,
):
    rows, width = tokens.shape
    ctx_count = lax.axis_size("ctx")
    exp_count = lax.axis_size("exp")
    ctx_rows = rows * exp_count
    heads_dev = w_query.shape[1] // HEAD_SIZE
    group_width = QUERY_HEADS // KEY_VALUE_HEADS
    me_ctx = lax.axis_index("ctx").astype(jnp.int32)
    me_exp = lax.axis_index("exp").astype(jnp.int32)
    place = jnp.stack([me_ctx, me_exp] + [jnp.int32(0)] * exp_count)
    peers = list(range(exp_count))
    bf16 = functools.partial(jax.ShapeDtypeStruct, dtype=jnp.bfloat16)

    experts = ctx_count * exp_count
    capacity = max(2, 3 * rows * TOP // (2 * experts))
    capacity = -(-capacity // 16) * 16
    ln1_row = ln1_gain.reshape(1, width)
    own_first = me_ctx * ctx_rows + me_exp * rows
    cosine, sine = rope_tables(own_first + jnp.arange(rows))
    own_args = [
        expert_ids.T,
        route_weights.T,
        tokens,
        ln1_row,
        key_weight,
        value_weight,
        k_gain.reshape(1, HEAD_SIZE),
        cosine,
        sine,
    ]
    own_kv = call(
        functools.partial(own_rows_kernel, experts, heads_dev),
        [bf16((rows + 2 * TOP, 2 * HEAD_SIZE)) for _ in peers],
        [SMEM] + [ANY] * 9,
        place,
        *own_args,
        name="own_rows",
        scratch=[pltpu.VMEM(a.shape, a.dtype) for a in own_args] + [pltpu.SemaphoreType.DMA((18,))],
        limit=60,
    )
    block_kv = [own_kv[0]] + [swap(own_kv[d], "exp", d) for d in peers[1:]]
    both = [part[:rows] for part in block_kv] + [part[rows:] for part in block_kv]
    both = lax.all_gather(jnp.concatenate(both, axis=0), "ctx", axis=0, tiled=True)
    sent = tie(tokens, *block_kv[1:])
    pieces = [tokens] + [swap(sent, "exp", d) for d in peers[1:]]
    routing = both.reshape(ctx_count, -1, 2 * HEAD_SIZE)[:, ctx_rows:]
    routing = routing.reshape(ctx_count, exp_count, 2 * TOP, 2 * HEAD_SIZE)

    positions = jnp.concatenate(
        [me_ctx * ctx_rows + (me_exp ^ d) * rows + jnp.arange(rows) for d in peers]
    )
    cosine, sine = rope_tables(positions)
    queries = call(
        query_kernel,
        bf16((exp_count, heads_dev * rows, HEAD_SIZE)),
        [VMEM] * (exp_count + 5),
        *pieces,
        ln1_row,
        w_query,
        q_gain.reshape(1, HEAD_SIZE),
        cosine,
        sine,
        name="queries",
    )

    order = sorted(peers, key=lambda d: -bin(d).count("1"))
    partials, last = {}, ()
    for some in [[d] for d in order]:
        asked = queries[some[0] : some[0] + 1]
        made = call(
            functools.partial(attention_kernel, some, rows),
            [bf16((rows, width)) for _ in some],
            [SMEM, VMEM, VMEM, VMEM],
            place,
            tie(asked, *last),
            both,
            w_out,
            name="attention",
        )
        partials.update(zip(some, made))
        last = tuple(made)
    attention = partials[0]
    parts = [swap(partials[d], "exp", d) for d in order if d]
    for part in parts[:-1]:
        attention = call(
            sum_kernel,
            jax.ShapeDtypeStruct((rows, width), jnp.float32),
            [VMEM] * 2,
            attention,
            part,
            name="add",
            flops=3_000_000_000,
        )
    residual, normed = call(
        residual_kernel,
        [bf16((rows, width)), bf16((rows, width))],
        [VMEM] * 4,
        tokens,
        attention,
        parts[-1],
        ln2_gain.reshape(1, width),
        name="residual",
    )

    groups = ctx_count // 2
    low, high = [0, 1], list(range(0, exp_count, 2))
    routes = [(low, high), (high, low)]
    half = width // 2
    far = [normed]
    for g in range(1, groups):
        far.append(swap(far[g & (g - 1)], "ctx", 2 * (g & -g)))
    in_flight = {}

    def send(array, d, kind):
        came = swap(tie(array, *in_flight.get((kind, d), ())), "exp", d)
        in_flight[kind, d] = (came,)
        return came

    arrived = []
    for g in range(groups):
        sources = []
        for side, (near, _) in enumerate(routes):
            part = far[g][:, side * half : (side + 1) * half]
            sources += [part] + [send(part, n, "whole") for n in near[1:]]
        outgoing = call(
            functools.partial(dispatch_kernel, routes, g, capacity),
            [bf16((2 * len(near) * capacity, half)) for near, away in routes for _ in away],
            [SMEM, VMEM] + [VMEM] * len(sources),
            place,
            routing,
            *sources,
            name="dispatch",
        )
        onward = [a for _, away in routes for a in away]
        arrived.append([send(out, a, "picked") if a else out for out, a in zip(outgoing, onward)])

    produced = []
    slots = exp_count * capacity
    for came in arrived:
        mate = jnp.concatenate([part[part.shape[0] // 2 :] for part in came], axis=0)
        made = call(
            functools.partial(expert_kernel, routes, capacity),
            [bf16((len(near) * capacity, half)) for near, away in routes for _ in away] * 2,
            [VMEM] * (len(came) + 4),
            *came,
            swap(mate, "ctx", 1),
            w_gate[0],
            w_up[0],
            w_down[0],
            name="expert",
            scratch=[
                pltpu.VMEM((2, 2 * slots, half), jnp.bfloat16),
                pltpu.VMEM((2 * slots, w_gate.shape[2]), jnp.bfloat16),
            ],
        )
        own, other = made[: len(came)], made[len(came) :]
        produced.append([(mine, swap(mates, "ctx", 1)) for mine, mates in zip(own, other)])

    passing = [[] for _ in range(groups)]
    for g in reversed(range(groups)):
        back, pieces = [], iter(produced[g])
        for _, away in routes:
            for a in away:
                pair = next(pieces)
                back += [send(jnp.concatenate(pair, axis=0), a, "picked")] if a else pair
        onward = [n for near, _ in routes for n in near[1:]]
        kept, *sums = call(
            functools.partial(combine_kernel, routes, g, capacity),
            [jax.ShapeDtypeStruct((rows, width), jnp.float32)] + [bf16((rows, half)) for _ in onward],
            [SMEM, VMEM] + [VMEM] * len(back),
            place,
            routing,
            *back,
            name="combine",
        )
        sums = [send(part, n, "whole") for part, n in zip(sums, onward)]
        total = call(
            functools.partial(gather_kernel, [len(near) - 1 for near, _ in routes]),
            bf16((rows, width)) if g else jax.ShapeDtypeStruct((rows, width), jnp.float32),
            [VMEM] * (1 + len(sums) + (len(passing[g]) if g else 0)),
            kept,
            *sums,
            *(passing[g] if g else []),
            name="gather",
        )
        if g:
            passing[g & (g - 1)].append(swap(total, "ctx", 2 * (g & -g)))
    early = call(
        sum_kernel,
        jax.ShapeDtypeStruct((rows, width), jnp.float32),
        [VMEM] * (1 + len(passing[0])),
        residual,
        *passing[0],
        name="add",
        flops=10_000_000_000,
    )
    return call(sum_kernel, bf16((rows, width)), [VMEM] * 2, early, total, name="add")


def solution(mesh):
    in_specs = (
        P(("ctx", "exp"), None),
        P(),
        P(None, "exp"),
        P(),
        P(),
        P(),
        P(),
        P("exp", None),
        P(),
        P(("ctx", "exp"), None),
        P(("ctx", "exp"), None),
        P(("ctx", "exp"), None, None),
        P(("ctx", "exp"), None, None),
        P(("ctx", "exp"), None, None),
    )
    out_specs = P(("ctx", "exp"), None)
    return jax.shard_map(shards, mesh=mesh, in_specs=in_specs, out_specs=out_specs, check_vma=False)
```

```python
import functools

import jax
import jax.numpy as jnp
from jax import lax
from jax.experimental import pallas as pl
from jax.experimental.pallas import tpu as pltpu
from jax.sharding import PartitionSpec as P

HEAD_SIZE = 128
QUERY_HEADS = 16
KEY_VALUE_HEADS = 2
TOP = 8
LOG2E = 1.4426950408889634

eps_value = 1e-06
theta_value = 1000000.0
floor_value = -1e30

VMEM = pl.BlockSpec(memory_space=pltpu.VMEM)
SMEM = pl.BlockSpec(memory_space=pltpu.SMEM)
ANY = pl.BlockSpec(memory_space=pl.ANY)


def rms_scale(value_states, norm_gain):
    return (
        value_states
        * lax.rsqrt(jnp.mean(value_states * value_states, axis=-1, keepdims=True) + eps_value)
        * norm_gain
    )


def swap(array, axis, distance):
    pairs = [(i, i ^ distance) for i in range(lax.axis_size(axis))]
    return lax.ppermute(array, axis, pairs)


def tie(array, *others):
    if not others:
        return array
    return lax.optimization_barrier((array, *others))[0]


def rope_tables(positions):
    half = HEAD_SIZE // 2
    frequency = theta_value ** (-2.0 * jnp.arange(half, dtype=jnp.float32) / HEAD_SIZE)
    angles = positions.astype(jnp.float32)[:, None] * frequency[None, :]
    return jnp.cos(angles), jnp.sin(angles)


def both_halves(cosine, sine):
    return jnp.concatenate([cosine, cosine], axis=1), jnp.concatenate([-sine, sine], axis=1)


def normed_rotated(states, gain, cosine, sine):
    states = rms_scale(states, gain)
    return states * cosine + pltpu.roll(states, HEAD_SIZE // 2, 1) * sine


def load_all(pairs, sems):
    copies = []
    for source, target in pairs:
        part = source.shape[0] // 4 if source.shape[0] >= 128 and source.shape[1] > 128 else source.shape[0]
        for first in range(0, source.shape[0], part):
            here = pl.ds(first, part)
            copies.append(
                pltpu.make_async_copy(source.at[here], target.at[here], sems.at[len(copies)])
            )
    for copy in copies:
        copy.start()
    return copies


def own_rows_kernel(experts, heads_dev, place, *refs):
    peers = len(refs) - 19
    sources, outs, targets, sems = refs[:9], refs[9:-10], refs[-10:-1], refs[-1]
    copies = load_all(list(zip(sources, targets)), sems)
    ids, shares, tokens, gain, key_weight, value_weight, k_gain, cosine, sine = targets
    copies[0].wait()
    copies[1].wait()
    rows = tokens.shape[0]
    chosen_ids = ids[...]
    lanes = lax.broadcasted_iota(jnp.int32, (experts, rows), 0)
    chosen = jnp.zeros((experts, rows), jnp.float32)
    for k in range(TOP):
        chosen = chosen + jnp.where(lanes == chosen_ids[k : k + 1], 1.0, 0.0)
    earlier = lax.broadcasted_iota(jnp.int32, (rows, rows), 0) < lax.broadcasted_iota(
        jnp.int32, (rows, rows), 1
    )
    rank = jnp.dot(
        chosen.astype(jnp.bfloat16),
        jnp.where(earlier, 1.0, 0.0).astype(jnp.bfloat16),
        preferred_element_type=jnp.float32,
    )
    slots = [
        jnp.sum(jnp.where(lanes == chosen_ids[k : k + 1], rank, 0.0), axis=0, keepdims=True)
        for k in range(TOP)
    ]
    slots = jnp.concatenate(slots, axis=0)
    left = jnp.concatenate([chosen_ids, shares[...]], axis=0).astype(jnp.float32)
    right = jnp.concatenate([slots, jnp.zeros_like(slots)], axis=0)
    for out in outs:
        out[rows:, :] = jnp.concatenate([left, right], axis=1).astype(jnp.bfloat16)
    for copy in copies[2:]:
        copy.wait()
    normed = rms_scale(tokens[...].astype(jnp.float32), gain[...]).astype(jnp.bfloat16)
    keys = jnp.dot(normed, key_weight[...], preferred_element_type=jnp.float32)
    values = jnp.dot(normed, value_weight[...], preferred_element_type=jnp.float32)
    cosine, sine = both_halves(cosine[...], sine[...])
    for head in range(KEY_VALUE_HEADS):
        cols = slice(head * HEAD_SIZE, (head + 1) * HEAD_SIZE)
        rotated = normed_rotated(keys[:, cols], k_gain[...], cosine, sine)
        pair = jnp.concatenate([rotated, values[:, cols]], axis=1).astype(jnp.bfloat16)
        for distance in range(peers):
            asked = (place[1] ^ distance) * heads_dev // (QUERY_HEADS // KEY_VALUE_HEADS)

            @pl.when(asked == head)
            def _(out=outs[distance], pair=pair):
                out[:rows, :] = pair


def query_kernel(*refs):
    *pieces, gain, w_query, q_gain, cosine, sine, out = refs
    rows = pieces[0].shape[0]
    heads = w_query.shape[1] // HEAD_SIZE
    for at, piece in enumerate(pieces):
        normed = rms_scale(piece[...].astype(jnp.float32), gain[...]).astype(jnp.bfloat16)
        queries = jnp.dot(normed, w_query[...], preferred_element_type=jnp.float32)
        here = pl.ds(at * rows, rows)
        turn = both_halves(cosine[here, :], sine[here, :])
        for head in range(heads):
            cols = slice(head * HEAD_SIZE, (head + 1) * HEAD_SIZE)
            rotated = normed_rotated(queries[:, cols], q_gain[...], *turn)
            out[at, pl.ds(head * rows, rows), :] = rotated.astype(jnp.bfloat16)


def attention_kernel(distances, rows, place, queries, both, w_out, *outs):
    block, me = place[0], place[1]
    heads = w_out.shape[0] // HEAD_SIZE
    width = heads * rows
    span = rows * (place.shape[0] - 2)
    stride = span + 2 * TOP * (place.shape[0] - 2)
    scale = HEAD_SIZE ** (-0.5) * LOG2E

    def step(first, states, masked):
        keys = both[pl.ds(first, span), :HEAD_SIZE]
        values = both[pl.ds(first, span), HEAD_SIZE:]
        result = []
        for at, (top, total, mixed) in enumerate(states):
            scores = lax.dot_general(
                keys, queries[at], (((1,), (1,)), ((), ())), preferred_element_type=jnp.float32
            )
            if masked:
                row = lax.broadcasted_iota(jnp.int32, (span, width), 0)
                key_pos = (me ^ (row // rows)) * rows + row % rows
                query = lax.broadcasted_iota(jnp.int32, (span, width), 1) % rows
                query_pos = (me ^ distances[at]) * rows + query
                scores = jnp.where(key_pos <= query_pos, scores, floor_value)
            new_top = jnp.maximum(top, jnp.max(scores, axis=0, keepdims=True))
            weights = jnp.exp2((scores - new_top) * scale)
            rescale = jnp.exp2((top - new_top) * scale)
            total = total * rescale + jnp.sum(weights, axis=0, keepdims=True)
            mixed = mixed * rescale + lax.dot_general(
                values,
                weights.astype(jnp.bfloat16),
                (((0,), (0,)), ((), ())),
                preferred_element_type=jnp.float32,
            )
            result.append((new_top, total, mixed))
        return tuple(result)

    states = tuple(
        (
            jnp.full((1, width), floor_value, jnp.float32),
            jnp.zeros((1, width), jnp.float32),
            jnp.zeros((HEAD_SIZE, width), jnp.float32),
        )
        for _ in distances
    )
    states = step(pl.multiple_of(block * stride, 2 * TOP), states, True)
    states = lax.fori_loop(
        0, block, lambda i, s: step(pl.multiple_of(i * stride, 2 * TOP), s, False), states
    )
    for (_, total, mixed), out in zip(states, outs):
        attended = (mixed / total).astype(jnp.bfloat16)
        attended = jnp.concatenate(
            [attended[:, head * rows : (head + 1) * rows] for head in range(heads)], axis=0
        )
        out[...] = lax.dot_general(
            attended, w_out[...], (((0,), (0,)), ((), ())), preferred_element_type=jnp.float32
        ).astype(jnp.bfloat16)


def residual_kernel(tokens, attention, partial, gain, residual, normed):
    summed = attention[...].astype(jnp.float32) + partial[...].astype(jnp.float32)
    rounded = (tokens[...].astype(jnp.float32) + summed).astype(jnp.bfloat16)
    residual[...] = rounded
    normed[...] = rms_scale(rounded.astype(jnp.float32), gain[...]).astype(jnp.bfloat16)


def slot_targets(table, expert):
    table = table.astype(jnp.float32)
    rows = table.shape[1] // 2
    named = table[:TOP, :rows] == expert.astype(jnp.float32)
    slot = jnp.max(jnp.where(named, table[:TOP, rows:], -1.0), axis=0, keepdims=True)
    weight = jnp.sum(jnp.where(named, table[TOP:, :rows], 0.0), axis=0, keepdims=True)
    return slot.astype(jnp.int32), weight * (1.0 / 1024.0)


def plane_targets(group, place, routing, near, away):
    block, me, count = place[0], place[1], routing.shape[1]
    table = routing[block ^ (2 * group), near]
    return [slot_targets(table, (block ^ core) * count + (me ^ away)) for core in (0, 1)]


def route_order(route):
    near, away = route
    return [n ^ a for a in away for n in near]


def dispatch_kernel(routes, group, capacity, place, routing, *refs):
    sources = refs[: sum(len(near) for near, _ in routes)]
    outs = refs[len(sources) :]
    rows = sources[0].shape[0]
    slots = lax.broadcasted_iota(jnp.int32, (capacity, rows), 0)
    for near, away in routes:
        some, sources = sources[: len(near)], sources[len(near) :]
        mine, outs = outs[: len(away)], outs[len(away) :]
        for at, (n, source) in enumerate(zip(near, some)):
            parts = []
            for a in away:
                for slot, _ in plane_targets(group, place, routing, n, a):
                    parts.append(jnp.where(slots == slot, 1.0, 0.0))
            hot = jnp.concatenate(parts, axis=0).astype(jnp.bfloat16)
            picked = jnp.dot(hot, source[...], preferred_element_type=jnp.float32)
            picked = picked.astype(jnp.bfloat16)
            for part in range(2 * len(away)):
                first = ((part % 2) * len(near) + at) * capacity
                mine[part // 2][first : first + capacity, :] = picked[
                    part * capacity : (part + 1) * capacity
                ]


def combine_kernel(routes, group, capacity, place, routing, *refs):
    arrived = refs[: sum(len(away) + 1 for _, away in routes)]
    kept, *outs = refs[len(arrived) :]
    rows, width = kept.shape[0], arrived[0].shape[1]
    slots = lax.broadcasted_iota(jnp.int32, (capacity, rows), 0)
    for side, (near, away) in enumerate(routes):
        some, arrived = arrived[: len(away) + 1], arrived[len(away) + 1 :]
        for at, n in enumerate(near):
            shares, produced = [], []
            for index, a in enumerate(away):
                for core, (slot, weight) in enumerate(plane_targets(group, place, routing, n, a)):
                    shares.append(jnp.where(slots == slot, weight, 0.0))
                    piece = some[index + 1] if index else some[core]
                    first = ((core if index else 0) * len(near) + at) * capacity
                    produced.append(piece[first : first + capacity, :])
            total = lax.dot_general(
                jnp.concatenate(shares, axis=0).astype(jnp.bfloat16),
                jnp.concatenate(produced, axis=0),
                (((0,), (0,)), ((), ())),
                preferred_element_type=jnp.float32,
            )
            if n:
                outs[0][...] = total.astype(jnp.bfloat16)
                outs = outs[1:]
            else:
                kept[:, side * width : (side + 1) * width] = total


def gather_kernel(counts, kept, *refs):
    *parts, out = refs
    width = out.shape[1] // len(counts)
    for side, count in enumerate(counts):
        cols = slice(side * width, (side + 1) * width)
        total = kept[:, cols]
        for part in parts[:count]:
            total = total + part[...].astype(jnp.float32)
        parts = parts[count:]
        for part in parts[sum(counts[side + 1 :]) :]:
            total = total + part[:, cols].astype(jnp.float32)
        out[:, cols] = total.astype(out.dtype)


def expert_kernel(routes, capacity, *refs):
    count = sum(len(away) for _, away in routes)
    came, (mate, w_gate, w_up, w_down) = refs[:count], refs[count : count + 4]
    own, other = refs[count + 4 : 2 * count + 4], refs[2 * count + 4 : 3 * count + 4]
    rows_in, hidden = refs[3 * count + 4 :]
    width = came[0].shape[1]
    half = rows_in.shape[1] // 2
    places = []
    for side, (near, away) in enumerate(routes):
        base = sum(len(some) for _, some in routes[:side])
        for at, d in enumerate(route_order((near, away))):
            places.append((side, base + at // len(near), (at % len(near)) * capacity, d * capacity))
    for at, (side, piece, first, to) in enumerate(places):
        rows_in[side, to : to + capacity, :] = came[piece][first : first + capacity, :]
        to = half + to
        rows_in[side, to : to + capacity, :] = mate[at * capacity : (at + 1) * capacity, :]
    for first in range(0, hidden.shape[1], 256):
        cols = slice(first, first + 256)
        gate = up = 0.0
        for side in range(len(routes)):
            depth = slice(side * width, (side + 1) * width)
            rows = rows_in[side]
            gate = gate + jnp.dot(rows, w_gate[depth, cols], preferred_element_type=jnp.float32)
            up = up + jnp.dot(rows, w_up[depth, cols], preferred_element_type=jnp.float32)
        hidden[:, cols] = (gate / (1.0 + jnp.exp(-gate)) * up).astype(jnp.bfloat16)
    for side in range(len(routes)):
        for first in range(0, width, 256):
            cols = slice(first, first + 256)
            down = w_down[:, side * width + first : side * width + first + 256]
            product = jnp.dot(hidden[...], down, preferred_element_type=jnp.float32)
            product = product.astype(jnp.bfloat16)
            for where, piece, to, at in places:
                if where == side:
                    here = slice(to, to + capacity)
                    own[piece][here, cols] = product[at : at + capacity]
                    other[piece][here, cols] = product[half + at : half + at + capacity]


def sum_kernel(*refs):
    *parts, out = refs
    total = parts[0][...].astype(jnp.float32)
    for part in parts[1:]:
        total = total + part[...].astype(jnp.float32)
    out[...] = total.astype(out.dtype)


def call(kernel, out_shape, specs, *args, name, scratch=(), limit=24, flops=1000):
    return pl.pallas_call(
        kernel,
        out_shape=out_shape,
        in_specs=specs,
        out_specs=jax.tree.map(lambda _: VMEM, out_shape),
        scratch_shapes=scratch,
        compiler_params=pltpu.CompilerParams(vmem_limit_bytes=limit * 1024 * 1024),
        cost_estimate=pl.CostEstimate(flops=flops, bytes_accessed=1000, transcendentals=0),
        name=name,
    )(*args)


def shards(
    tokens,
    ln1_gain,
    w_query,
    key_weight,
    value_weight,
    q_gain,
    k_gain,
    w_out,
    ln2_gain,
    expert_ids,
    route_weights,
    w_gate,
    w_up,
    w_down,
):
    rows, width = tokens.shape
    ctx_count = lax.axis_size("ctx")
    exp_count = lax.axis_size("exp")
    ctx_rows = rows * exp_count
    heads_dev = w_query.shape[1] // HEAD_SIZE
    group_width = QUERY_HEADS // KEY_VALUE_HEADS
    me_ctx = lax.axis_index("ctx").astype(jnp.int32)
    me_exp = lax.axis_index("exp").astype(jnp.int32)
    place = jnp.stack([me_ctx, me_exp] + [jnp.int32(0)] * exp_count)
    peers = list(range(exp_count))
    bf16 = functools.partial(jax.ShapeDtypeStruct, dtype=jnp.bfloat16)

    experts = ctx_count * exp_count
    capacity = max(2, 3 * rows * TOP // (2 * experts))
    capacity = -(-capacity // 16) * 16
    ln1_row = ln1_gain.reshape(1, width)
    own_first = me_ctx * ctx_rows + me_exp * rows
    cosine, sine = rope_tables(own_first + jnp.arange(rows))
    own_args = [
        expert_ids.T,
        route_weights.T,
        tokens,
        ln1_row,
        key_weight,
        value_weight,
        k_gain.reshape(1, HEAD_SIZE),
        cosine,
        sine,
    ]
    own_kv = call(
        functools.partial(own_rows_kernel, experts, heads_dev),
        [bf16((rows + 2 * TOP, 2 * HEAD_SIZE)) for _ in peers],
        [SMEM] + [ANY] * 9,
        place,
        *own_args,
        name="own_rows",
        scratch=[pltpu.VMEM(a.shape, a.dtype) for a in own_args] + [pltpu.SemaphoreType.DMA((18,))],
        limit=60,
    )
    block_kv = [own_kv[0]] + [swap(own_kv[d], "exp", d) for d in peers[1:]]
    both = [part[:rows] for part in block_kv] + [part[rows:] for part in block_kv]
    both = lax.all_gather(jnp.concatenate(both, axis=0), "ctx", axis=0, tiled=True)
    sent = tie(tokens, *block_kv[1:])
    pieces = [tokens] + [swap(sent, "exp", d) for d in peers[1:]]
    routing = both.reshape(ctx_count, -1, 2 * HEAD_SIZE)[:, ctx_rows:]
    routing = routing.reshape(ctx_count, exp_count, 2 * TOP, 2 * HEAD_SIZE)

    positions = jnp.concatenate(
        [me_ctx * ctx_rows + (me_exp ^ d) * rows + jnp.arange(rows) for d in peers]
    )
    cosine, sine = rope_tables(positions)
    queries = call(
        query_kernel,
        bf16((exp_count, heads_dev * rows, HEAD_SIZE)),
        [VMEM] * (exp_count + 5),
        *pieces,
        ln1_row,
        w_query,
        q_gain.reshape(1, HEAD_SIZE),
        cosine,
        sine,
        name="queries",
    )

    order = sorted(peers, key=lambda d: -bin(d).count("1"))
    partials, last = {}, ()
    for some in [[d] for d in order]:
        asked = queries[some[0] : some[0] + 1]
        made = call(
            functools.partial(attention_kernel, some, rows),
            [bf16((rows, width)) for _ in some],
            [SMEM, VMEM, VMEM, VMEM],
            place,
            tie(asked, *last),
            both,
            w_out,
            name="attention",
        )
        partials.update(zip(some, made))
        last = tuple(made)
    attention = partials[0]
    parts = [swap(partials[d], "exp", d) for d in order if d]
    for part in parts[:-1]:
        attention = call(
            sum_kernel,
            jax.ShapeDtypeStruct((rows, width), jnp.float32),
            [VMEM] * 2,
            attention,
            part,
            name="add",
            flops=3_000_000_000,
        )
    residual, normed = call(
        residual_kernel,
        [bf16((rows, width)), bf16((rows, width))],
        [VMEM] * 4,
        tokens,
        attention,
        parts[-1],
        ln2_gain.reshape(1, width),
        name="residual",
    )

    groups = ctx_count // 2
    low, high = [0, 1], list(range(0, exp_count, 2))
    routes = [(low, high), (high, low)]
    half = width // 2
    far = [normed]
    for g in range(1, groups):
        far.append(swap(far[g & (g - 1)], "ctx", 2 * (g & -g)))
    in_flight = {}

    def send(array, d, kind):
        came = swap(tie(array, *in_flight.get((kind, d), ())), "exp", d)
        in_flight[kind, d] = (came,)
        return came

    arrived = []
    for g in range(groups):
        sources = []
        for side, (near, _) in enumerate(routes):
            part = far[g][:, side * half : (side + 1) * half]
            sources += [part] + [send(part, n, "whole") for n in near[1:]]
        last_sources = sources
        outgoing = call(
            functools.partial(dispatch_kernel, routes, g, capacity),
            [bf16((2 * len(near) * capacity, half)) for near, away in routes for _ in away],
            [SMEM, VMEM] + [VMEM] * len(sources),
            place,
            routing,
            *sources,
            name="dispatch",
        )
        onward = [a for _, away in routes for a in away]
        ahead = far[g + 1 : g + 2] if g > 1 else []
        arrived.append(
            [send(tie(out, *ahead), a, "picked") if a else out for out, a in zip(outgoing, onward)]
        )

    produced, mates_before = [], ()
    slots = exp_count * capacity
    for g, came in enumerate(arrived):
        ahead = last_sources if g == groups - 2 else ()
        done = [mates for pair in produced[groups - 2 :] for _, mates in pair]
        mate = jnp.concatenate([part[part.shape[0] // 2 :] for part in came], axis=0)
        mate = swap(tie(mate, *ahead, *done, *mates_before), "ctx", 1)
        mates_before = (mate,)
        made = call(
            functools.partial(expert_kernel, routes, capacity),
            [bf16((len(near) * capacity, half)) for near, away in routes for _ in away] * 2,
            [VMEM] * (len(came) + 4),
            *came,
            mate,
            w_gate[0],
            w_up[0],
            w_down[0],
            name="expert",
            scratch=[
                pltpu.VMEM((2, 2 * slots, half), jnp.bfloat16),
                pltpu.VMEM((2 * slots, w_gate.shape[2]), jnp.bfloat16),
            ],
        )
        own, other = made[: len(came)], made[len(came) :]
        produced.append([(mine, swap(mates, "ctx", 1)) for mine, mates in zip(own, other)])

    totals, hop = [], ()
    for g in [*range(2, groups), *(g for g in (1, 0) if g < groups)]:
        back, pieces = [], iter(produced[g])
        for _, away in routes:
            for a in away:
                pair = next(pieces)
                back += [send(jnp.concatenate(pair, axis=0), a, "picked")] if a else pair
        onward = [n for near, _ in routes for n in near[1:]]
        kept, *sums = call(
            functools.partial(combine_kernel, routes, g, capacity),
            [jax.ShapeDtypeStruct((rows, width), jnp.float32)] + [bf16((rows, half)) for _ in onward],
            [SMEM, VMEM] + [VMEM] * len(back),
            place,
            routing,
            *back,
            name="combine",
        )
        sums = [send(part, n, "whole") for part, n in zip(sums, onward)]
        total = call(
            functools.partial(gather_kernel, [len(near) - 1 for near, _ in routes]),
            bf16((rows, width)) if g else jax.ShapeDtypeStruct((rows, width), jnp.float32),
            [VMEM] * (1 + len(sums)),
            kept,
            *sums,
            name="gather",
        )
        if g:
            total = swap(tie(total, *(hop if g > 1 else ())), "ctx", 2 * g)
            hop = (total,)
            totals.append(total)
    early = call(
        sum_kernel,
        jax.ShapeDtypeStruct((rows, width), jnp.float32),
        [VMEM] * groups,
        residual,
        *totals,
        name="add",
        flops=10_000_000_000,
    )
    return call(sum_kernel, bf16((rows, width)), [VMEM] * 2, early, total, name="add")


def solution(mesh):
    in_specs = (
        P(("ctx", "exp"), None),
        P(),
        P(None, "exp"),
        P(),
        P(),
        P(),
        P(),
        P("exp", None),
        P(),
        P(("ctx", "exp"), None),
        P(("ctx", "exp"), None),
        P(("ctx", "exp"), None, None),
        P(("ctx", "exp"), None, None),
        P(("ctx", "exp"), None, None),
    )
    out_specs = P(("ctx", "exp"), None)
    return jax.shard_map(shards, mesh=mesh, in_specs=in_specs, out_specs=out_specs, check_vma=False)
```

```python
import functools

import jax
import jax.numpy as jnp
from jax import lax
from jax.experimental import pallas as pl
from jax.experimental.pallas import tpu as pltpu
from jax.sharding import PartitionSpec as P

HEAD_SIZE = 128
QUERY_HEADS = 16
KEY_VALUE_HEADS = 2
TOP = 8
LOG2E = 1.4426950408889634

eps_value = 1e-06
theta_value = 1000000.0
floor_value = -1e30

VMEM = pl.BlockSpec(memory_space=pltpu.VMEM)
SMEM = pl.BlockSpec(memory_space=pltpu.SMEM)
ANY = pl.BlockSpec(memory_space=pl.ANY)


def rms_scale(value_states, norm_gain):
    return (
        value_states
        * lax.rsqrt(jnp.mean(value_states * value_states, axis=-1, keepdims=True) + eps_value)
        * norm_gain
    )


def swap(array, axis, distance):
    pairs = [(i, i ^ distance) for i in range(lax.axis_size(axis))]
    return lax.ppermute(array, axis, pairs)


def tie(array, *others):
    if not others:
        return array
    return lax.optimization_barrier((array, *others))[0]


def rope_tables(positions):
    half = HEAD_SIZE // 2
    frequency = theta_value ** (-2.0 * jnp.arange(half, dtype=jnp.float32) / HEAD_SIZE)
    angles = positions.astype(jnp.float32)[:, None] * frequency[None, :]
    return jnp.cos(angles), jnp.sin(angles)


def both_halves(cosine, sine):
    return jnp.concatenate([cosine, cosine], axis=1), jnp.concatenate([-sine, sine], axis=1)


def normed_rotated(states, gain, cosine, sine):
    states = rms_scale(states, gain)
    return states * cosine + pltpu.roll(states, HEAD_SIZE // 2, 1) * sine


def load_all(pairs, sems):
    copies = []
    for source, target in pairs:
        part = source.shape[0] // 4 if source.shape[0] >= 128 and source.shape[1] > 128 else source.shape[0]
        for first in range(0, source.shape[0], part):
            here = pl.ds(first, part)
            copies.append(
                pltpu.make_async_copy(source.at[here], target.at[here], sems.at[len(copies)])
            )
    for copy in copies:
        copy.start()
    return copies


def own_rows_kernel(experts, heads_dev, place, *refs):
    peers = len(refs) - 19
    sources, outs, targets, sems = refs[:9], refs[9:-10], refs[-10:-1], refs[-1]
    copies = load_all(list(zip(sources, targets)), sems)
    ids, shares, tokens, gain, key_weight, value_weight, k_gain, cosine, sine = targets
    copies[0].wait()
    copies[1].wait()
    rows = tokens.shape[0]
    chosen_ids = ids[...]
    lanes = lax.broadcasted_iota(jnp.int32, (experts, rows), 0)
    chosen = jnp.zeros((experts, rows), jnp.float32)
    for k in range(TOP):
        chosen = chosen + jnp.where(lanes == chosen_ids[k : k + 1], 1.0, 0.0)
    earlier = lax.broadcasted_iota(jnp.int32, (rows, rows), 0) < lax.broadcasted_iota(
        jnp.int32, (rows, rows), 1
    )
    rank = jnp.dot(
        chosen.astype(jnp.bfloat16),
        jnp.where(earlier, 1.0, 0.0).astype(jnp.bfloat16),
        preferred_element_type=jnp.float32,
    )
    slots = [
        jnp.sum(jnp.where(lanes == chosen_ids[k : k + 1], rank, 0.0), axis=0, keepdims=True)
        for k in range(TOP)
    ]
    slots = jnp.concatenate(slots, axis=0)
    left = jnp.concatenate([chosen_ids, shares[...]], axis=0).astype(jnp.float32)
    right = jnp.concatenate([slots, jnp.zeros_like(slots)], axis=0)
    for out in outs:
        out[rows:, :] = jnp.concatenate([left, right], axis=1).astype(jnp.bfloat16)
    for copy in copies[2:]:
        copy.wait()
    normed = rms_scale(tokens[...].astype(jnp.float32), gain[...]).astype(jnp.bfloat16)
    keys = jnp.dot(normed, key_weight[...], preferred_element_type=jnp.float32)
    values = jnp.dot(normed, value_weight[...], preferred_element_type=jnp.float32)
    cosine, sine = both_halves(cosine[...], sine[...])
    for head in range(KEY_VALUE_HEADS):
        cols = slice(head * HEAD_SIZE, (head + 1) * HEAD_SIZE)
        rotated = normed_rotated(keys[:, cols], k_gain[...], cosine, sine)
        pair = jnp.concatenate([rotated, values[:, cols]], axis=1).astype(jnp.bfloat16)
        for distance in range(peers):
            asked = (place[1] ^ distance) * heads_dev // (QUERY_HEADS // KEY_VALUE_HEADS)

            @pl.when(asked == head)
            def _(out=outs[distance], pair=pair):
                out[:rows, :] = pair


def query_kernel(*refs):
    *pieces, gain, w_query, q_gain, cosine, sine, out = refs
    rows = pieces[0].shape[0]
    heads = w_query.shape[1] // HEAD_SIZE
    for at, piece in enumerate(pieces):
        normed = rms_scale(piece[...].astype(jnp.float32), gain[...]).astype(jnp.bfloat16)
        queries = jnp.dot(normed, w_query[...], preferred_element_type=jnp.float32)
        here = pl.ds(at * rows, rows)
        turn = both_halves(cosine[here, :], sine[here, :])
        for head in range(heads):
            cols = slice(head * HEAD_SIZE, (head + 1) * HEAD_SIZE)
            rotated = normed_rotated(queries[:, cols], q_gain[...], *turn)
            out[at, pl.ds(head * rows, rows), :] = rotated.astype(jnp.bfloat16)


def attention_kernel(distances, rows, place, queries, both, w_out, *outs):
    block, me = place[0], place[1]
    heads = w_out.shape[0] // HEAD_SIZE
    width = heads * rows
    span = rows * (place.shape[0] - 2)
    stride = span + 2 * TOP * (place.shape[0] - 2)
    scale = HEAD_SIZE ** (-0.5) * LOG2E

    def step(first, states, masked):
        keys = both[pl.ds(first, span), :HEAD_SIZE]
        values = both[pl.ds(first, span), HEAD_SIZE:]
        result = []
        for at, (top, total, mixed) in enumerate(states):
            scores = lax.dot_general(
                keys, queries[at], (((1,), (1,)), ((), ())), preferred_element_type=jnp.float32
            )
            if masked:
                row = lax.broadcasted_iota(jnp.int32, (span, width), 0)
                key_pos = (me ^ (row // rows)) * rows + row % rows
                query = lax.broadcasted_iota(jnp.int32, (span, width), 1) % rows
                query_pos = (me ^ distances[at]) * rows + query
                scores = jnp.where(key_pos <= query_pos, scores, floor_value)
            new_top = jnp.maximum(top, jnp.max(scores, axis=0, keepdims=True))
            weights = jnp.exp2((scores - new_top) * scale)
            rescale = jnp.exp2((top - new_top) * scale)
            total = total * rescale + jnp.sum(weights, axis=0, keepdims=True)
            mixed = mixed * rescale + lax.dot_general(
                values,
                weights.astype(jnp.bfloat16),
                (((0,), (0,)), ((), ())),
                preferred_element_type=jnp.float32,
            )
            result.append((new_top, total, mixed))
        return tuple(result)

    states = tuple(
        (
            jnp.full((1, width), floor_value, jnp.float32),
            jnp.zeros((1, width), jnp.float32),
            jnp.zeros((HEAD_SIZE, width), jnp.float32),
        )
        for _ in distances
    )
    states = step(pl.multiple_of(block * stride, 2 * TOP), states, True)
    states = lax.fori_loop(
        0, block, lambda i, s: step(pl.multiple_of(i * stride, 2 * TOP), s, False), states
    )
    for (_, total, mixed), out in zip(states, outs):
        attended = (mixed / total).astype(jnp.bfloat16)
        attended = jnp.concatenate(
            [attended[:, head * rows : (head + 1) * rows] for head in range(heads)], axis=0
        )
        out[...] = lax.dot_general(
            attended, w_out[...], (((0,), (0,)), ((), ())), preferred_element_type=jnp.float32
        ).astype(jnp.bfloat16)


def residual_kernel(tokens, attention, partial, gain, residual, normed):
    summed = attention[...].astype(jnp.float32) + partial[...].astype(jnp.float32)
    rounded = (tokens[...].astype(jnp.float32) + summed).astype(jnp.bfloat16)
    residual[...] = rounded
    normed[...] = rms_scale(rounded.astype(jnp.float32), gain[...]).astype(jnp.bfloat16)


def slot_targets(table, expert):
    table = table.astype(jnp.float32)
    rows = table.shape[1] // 2
    named = table[:TOP, :rows] == expert.astype(jnp.float32)
    slot = jnp.max(jnp.where(named, table[:TOP, rows:], -1.0), axis=0, keepdims=True)
    weight = jnp.sum(jnp.where(named, table[TOP:, :rows], 0.0), axis=0, keepdims=True)
    return slot.astype(jnp.int32), weight * (1.0 / 1024.0)


def plane_targets(group, place, routing, near, away):
    block, me, count = place[0], place[1], routing.shape[1]
    table = routing[block ^ (2 * group), near]
    return [slot_targets(table, (block ^ core) * count + (me ^ away)) for core in (0, 1)]


def route_order(route):
    near, away = route
    return [n ^ a for a in away for n in near]


def dispatch_kernel(routes, group, capacity, place, routing, *refs):
    sources = refs[: sum(len(near) for near, _ in routes)]
    outs = refs[len(sources) :]
    rows = sources[0].shape[0]
    slots = lax.broadcasted_iota(jnp.int32, (capacity, rows), 0)
    for near, away in routes:
        some, sources = sources[: len(near)], sources[len(near) :]
        mine, outs = outs[: len(away)], outs[len(away) :]
        for at, (n, source) in enumerate(zip(near, some)):
            parts = []
            for a in away:
                for slot, _ in plane_targets(group, place, routing, n, a):
                    parts.append(jnp.where(slots == slot, 1.0, 0.0))
            hot = jnp.concatenate(parts, axis=0).astype(jnp.bfloat16)
            picked = jnp.dot(hot, source[...], preferred_element_type=jnp.float32)
            picked = picked.astype(jnp.bfloat16)
            for part in range(2 * len(away)):
                first = ((part % 2) * len(near) + at) * capacity
                mine[part // 2][first : first + capacity, :] = picked[
                    part * capacity : (part + 1) * capacity
                ]


def combine_kernel(routes, group, capacity, place, routing, *refs):
    count = sum(len(away) for _, away in routes)
    arrived, other, (kept, *outs) = refs[:count], refs[count], refs[count + 1 :]
    rows, width = kept.shape[0], other.shape[1]
    slots = lax.broadcasted_iota(jnp.int32, (capacity, rows), 0)
    base = 0
    for side, (near, away) in enumerate(routes):
        some, arrived = arrived[: len(away)], arrived[len(away) :]
        for at, n in enumerate(near):
            shares, produced = [], []
            for index, a in enumerate(away):
                for core, (slot, weight) in enumerate(plane_targets(group, place, routing, n, a)):
                    shares.append(jnp.where(slots == slot, weight, 0.0))
                    first = at * capacity
                    if core:
                        first += base + index * len(near) * capacity
                    piece = other if core else some[index]
                    produced.append(piece[first : first + capacity, :])
            total = lax.dot_general(
                jnp.concatenate(shares, axis=0).astype(jnp.bfloat16),
                jnp.concatenate(produced, axis=0),
                (((0,), (0,)), ((), ())),
                preferred_element_type=jnp.float32,
            )
            if n:
                outs[0][...] = total.astype(jnp.bfloat16)
                outs = outs[1:]
            else:
                kept[:, side * width : (side + 1) * width] = total
        base += len(near) * len(away) * capacity


def gather_kernel(counts, kept, *refs):
    *parts, out = refs
    width = out.shape[1] // len(counts)
    for side, count in enumerate(counts):
        cols = slice(side * width, (side + 1) * width)
        total = kept[:, cols]
        for part in parts[:count]:
            total = total + part[...].astype(jnp.float32)
        parts = parts[count:]
        for part in parts[sum(counts[side + 1 :]) :]:
            total = total + part[:, cols].astype(jnp.float32)
        out[:, cols] = total.astype(out.dtype)


def expert_kernel(routes, capacity, *refs):
    count = sum(len(away) for _, away in routes)
    came, (mate, w_gate, w_up, w_down) = refs[:count], refs[count : count + 4]
    outs = refs[count + 4 : 2 * count + 4]
    rows_in, hidden = refs[2 * count + 4 :]
    width = came[0].shape[1]
    half = rows_in.shape[1] // 2
    places = []
    for side, (near, away) in enumerate(routes):
        base = sum(len(some) for _, some in routes[:side])
        for at, d in enumerate(route_order((near, away))):
            places.append((side, base + at // len(near), (at % len(near)) * capacity, d * capacity))
    for at, (side, piece, first, to) in enumerate(places):
        rows_in[side, to : to + capacity, :] = came[piece][first : first + capacity, :]
        to = half + to
        rows_in[side, to : to + capacity, :] = mate[at * capacity : (at + 1) * capacity, :]
    for first in range(0, hidden.shape[1], 256):
        cols = slice(first, first + 256)
        gate = up = 0.0
        for side in range(len(routes)):
            depth = slice(side * width, (side + 1) * width)
            rows = rows_in[side]
            gate = gate + jnp.dot(rows, w_gate[depth, cols], preferred_element_type=jnp.float32)
            up = up + jnp.dot(rows, w_up[depth, cols], preferred_element_type=jnp.float32)
        hidden[:, cols] = (gate / (1.0 + jnp.exp(-gate)) * up).astype(jnp.bfloat16)
    for side in range(len(routes)):
        for first in range(0, width, 256):
            cols = slice(first, first + 256)
            down = w_down[:, side * width + first : side * width + first + 256]
            product = jnp.dot(hidden[...], down, preferred_element_type=jnp.float32)
            product = product.astype(jnp.bfloat16)
            for where, piece, to, at in places:
                if where == side:
                    out = outs[piece]
                    out[to : to + capacity, cols] = product[at : at + capacity]
                    to += out.shape[0] // 2
                    out[to : to + capacity, cols] = product[half + at : half + at + capacity]


def sum_kernel(*refs):
    *parts, out = refs
    total = parts[0][...].astype(jnp.float32)
    for part in parts[1:]:
        total = total + part[...].astype(jnp.float32)
    out[...] = total.astype(out.dtype)


def call(kernel, out_shape, specs, *args, name, scratch=(), limit=24, flops=1000):
    return pl.pallas_call(
        kernel,
        out_shape=out_shape,
        in_specs=specs,
        out_specs=jax.tree.map(lambda _: VMEM, out_shape),
        scratch_shapes=scratch,
        compiler_params=pltpu.CompilerParams(vmem_limit_bytes=limit * 1024 * 1024),
        cost_estimate=pl.CostEstimate(flops=flops, bytes_accessed=1000, transcendentals=0),
        name=name,
    )(*args)


def shards(
    tokens,
    ln1_gain,
    w_query,
    key_weight,
    value_weight,
    q_gain,
    k_gain,
    w_out,
    ln2_gain,
    expert_ids,
    route_weights,
    w_gate,
    w_up,
    w_down,
):
    rows, width = tokens.shape
    ctx_count = lax.axis_size("ctx")
    exp_count = lax.axis_size("exp")
    ctx_rows = rows * exp_count
    heads_dev = w_query.shape[1] // HEAD_SIZE
    group_width = QUERY_HEADS // KEY_VALUE_HEADS
    me_ctx = lax.axis_index("ctx").astype(jnp.int32)
    me_exp = lax.axis_index("exp").astype(jnp.int32)
    place = jnp.stack([me_ctx, me_exp] + [jnp.int32(0)] * exp_count)
    peers = list(range(exp_count))
    bf16 = functools.partial(jax.ShapeDtypeStruct, dtype=jnp.bfloat16)

    experts = ctx_count * exp_count
    capacity = max(2, 3 * rows * TOP // (2 * experts))
    capacity = -(-capacity // 16) * 16
    ln1_row = ln1_gain.reshape(1, width)
    own_first = me_ctx * ctx_rows + me_exp * rows
    cosine, sine = rope_tables(own_first + jnp.arange(rows))
    own_args = [
        expert_ids.T,
        route_weights.T,
        tokens,
        ln1_row,
        key_weight,
        value_weight,
        k_gain.reshape(1, HEAD_SIZE),
        cosine,
        sine,
    ]
    own_kv = call(
        functools.partial(own_rows_kernel, experts, heads_dev),
        [bf16((rows + 2 * TOP, 2 * HEAD_SIZE)) for _ in peers],
        [SMEM] + [ANY] * 9,
        place,
        *own_args,
        name="own_rows",
        scratch=[pltpu.VMEM(a.shape, a.dtype) for a in own_args] + [pltpu.SemaphoreType.DMA((18,))],
        limit=60,
    )
    block_kv = [own_kv[0]] + [swap(own_kv[d], "exp", d) for d in peers[1:]]
    both = [part[:rows] for part in block_kv] + [part[rows:] for part in block_kv]
    both = lax.all_gather(jnp.concatenate(both, axis=0), "ctx", axis=0, tiled=True)
    sent = tie(tokens, *block_kv[1:])
    pieces = [tokens] + [swap(sent, "exp", d) for d in peers[1:]]
    routing = both.reshape(ctx_count, -1, 2 * HEAD_SIZE)[:, ctx_rows:]
    routing = routing.reshape(ctx_count, exp_count, 2 * TOP, 2 * HEAD_SIZE)

    positions = jnp.concatenate(
        [me_ctx * ctx_rows + (me_exp ^ d) * rows + jnp.arange(rows) for d in peers]
    )
    cosine, sine = rope_tables(positions)
    queries = call(
        query_kernel,
        bf16((exp_count, heads_dev * rows, HEAD_SIZE)),
        [VMEM] * (exp_count + 5),
        *pieces,
        ln1_row,
        w_query,
        q_gain.reshape(1, HEAD_SIZE),
        cosine,
        sine,
        name="queries",
    )

    order = sorted(peers, key=lambda d: -bin(d).count("1"))
    partials, last = {}, ()
    for some in [[d] for d in order]:
        asked = queries[some[0] : some[0] + 1]
        made = call(
            functools.partial(attention_kernel, some, rows),
            [bf16((rows, width)) for _ in some],
            [SMEM, VMEM, VMEM, VMEM],
            place,
            tie(asked, *last),
            both,
            w_out,
            name="attention",
        )
        partials.update(zip(some, made))
        last = tuple(made)
    attention = partials[0]
    parts = [swap(partials[d], "exp", d) for d in order if d]
    for part in parts[:-1]:
        attention = call(
            sum_kernel,
            jax.ShapeDtypeStruct((rows, width), jnp.float32),
            [VMEM] * 2,
            attention,
            part,
            name="add",
            flops=3_000_000_000,
        )
    residual, normed = call(
        residual_kernel,
        [bf16((rows, width)), bf16((rows, width))],
        [VMEM] * 4,
        tokens,
        attention,
        parts[-1],
        ln2_gain.reshape(1, width),
        name="residual",
    )

    groups = ctx_count // 2
    low, high = [0, 1], list(range(0, exp_count, 2))
    routes = [(low, high), (high, low)]
    half = width // 2
    far = [normed]
    for g in range(1, groups):
        far.append(swap(far[g & (g - 1)], "ctx", 2 * (g & -g)))
    in_flight = {}

    def send(array, d, kind):
        came = swap(tie(array, *in_flight.get((kind, d), ())), "exp", d)
        in_flight[kind, d] = (came,)
        return came

    arrived = []
    for g in range(groups):
        sources = []
        for side, (near, _) in enumerate(routes):
            part = far[g][:, side * half : (side + 1) * half]
            sources += [part] + [send(part, n, "whole") for n in near[1:]]
        outgoing = call(
            functools.partial(dispatch_kernel, routes, g, capacity),
            [bf16((2 * len(near) * capacity, half)) for near, away in routes for _ in away],
            [SMEM, VMEM] + [VMEM] * len(sources),
            place,
            routing,
            *sources,
            name="dispatch",
        )
        onward = [a for _, away in routes for a in away]
        arrived.append([send(out, a, "picked") if a else out for out, a in zip(outgoing, onward)])

    def to_mate(parts, *others):
        halves = [part[part.shape[0] // 2 :] for part in parts]
        return swap(tie(jnp.concatenate(halves, axis=0), *others), "ctx", 1)

    produced = []
    slots = exp_count * capacity
    for g, came in enumerate(arrived):
        ready = produced if g >= groups - 2 else []
        produced.append(
            call(
                functools.partial(expert_kernel, routes, capacity),
                [bf16((2 * len(near) * capacity, half)) for near, away in routes for _ in away],
                [VMEM] * (len(came) + 4),
                *came,
                to_mate(came, *[made[0] for made in ready]),
                w_gate[0],
                w_up[0],
                w_down[0],
                name="expert",
                scratch=[
                    pltpu.VMEM((2, 2 * slots, half), jnp.bfloat16),
                    pltpu.VMEM((2 * slots, w_gate.shape[2]), jnp.bfloat16),
                ],
            )
        )

    totals, hop = [], ()
    onward_picked = [a for _, away in routes for a in away]
    for g in [*range(2, groups), *(g for g in (1, 0) if g < groups)]:
        back = [send(p, a, "picked") if a else p for p, a in zip(produced[g], onward_picked)]
        back.append(to_mate(back))
        onward = [n for near, _ in routes for n in near[1:]]
        kept, *sums = call(
            functools.partial(combine_kernel, routes, g, capacity),
            [jax.ShapeDtypeStruct((rows, width), jnp.float32)] + [bf16((rows, half)) for _ in onward],
            [SMEM, VMEM] + [VMEM] * len(back),
            place,
            routing,
            *back,
            name="combine",
        )
        sums = [send(part, n, "whole") for part, n in zip(sums, onward)]
        total = call(
            functools.partial(gather_kernel, [len(near) - 1 for near, _ in routes]),
            bf16((rows, width)) if g else jax.ShapeDtypeStruct((rows, width), jnp.float32),
            [VMEM] * (1 + len(sums)),
            kept,
            *sums,
            name="gather",
        )
        if g:
            total = swap(tie(total, *(hop if g > 1 else ())), "ctx", 2 * g)
            hop = (total,)
            totals.append(total)
    early = call(
        sum_kernel,
        jax.ShapeDtypeStruct((rows, width), jnp.float32),
        [VMEM] * groups,
        residual,
        *totals,
        name="add",
        flops=10_000_000_000,
    )
    return call(sum_kernel, bf16((rows, width)), [VMEM] * 2, early, total, name="add")


def solution(mesh):
    in_specs = (
        P(("ctx", "exp"), None),
        P(),
        P(None, "exp"),
        P(),
        P(),
        P(),
        P(),
        P("exp", None),
        P(),
        P(("ctx", "exp"), None),
        P(("ctx", "exp"), None),
        P(("ctx", "exp"), None, None),
        P(("ctx", "exp"), None, None),
        P(("ctx", "exp"), None, None),
    )
    out_specs = P(("ctx", "exp"), None)
    return jax.shard_map(shards, mesh=mesh, in_specs=in_specs, out_specs=out_specs, check_vma=False)
```

```python
import functools

import jax
import jax.numpy as jnp
from jax import lax
from jax.experimental import pallas as pl
from jax.experimental.pallas import tpu as pltpu
from jax.sharding import PartitionSpec as P

HEAD_SIZE = 128
QUERY_HEADS = 16
KEY_VALUE_HEADS = 2
TOP = 8
LOG2E = 1.4426950408889634

eps_value = 1e-06
theta_value = 1000000.0
floor_value = -1e30

VMEM = pl.BlockSpec(memory_space=pltpu.VMEM)
SMEM = pl.BlockSpec(memory_space=pltpu.SMEM)
ANY = pl.BlockSpec(memory_space=pl.ANY)


def rms_scale(value_states, norm_gain):
    return (
        value_states
        * lax.rsqrt(jnp.mean(value_states * value_states, axis=-1, keepdims=True) + eps_value)
        * norm_gain
    )


def swap(array, axis, distance):
    pairs = [(i, i ^ distance) for i in range(lax.axis_size(axis))]
    return lax.ppermute(array, axis, pairs)


def tie(array, *others):
    if not others:
        return array
    return lax.optimization_barrier((array, *others))[0]


def rope_tables(positions):
    half = HEAD_SIZE // 2
    frequency = theta_value ** (-2.0 * jnp.arange(half, dtype=jnp.float32) / HEAD_SIZE)
    angles = positions.astype(jnp.float32)[:, None] * frequency[None, :]
    return jnp.cos(angles), jnp.sin(angles)


def both_halves(cosine, sine):
    return jnp.concatenate([cosine, cosine], axis=1), jnp.concatenate([-sine, sine], axis=1)


def normed_rotated(states, gain, cosine, sine):
    states = rms_scale(states, gain)
    return states * cosine + pltpu.roll(states, HEAD_SIZE // 2, 1) * sine


def load_all(pairs, sems):
    copies = []
    for source, target in pairs:
        part = source.shape[0] // 4 if source.shape[0] >= 128 and source.shape[1] > 128 else source.shape[0]
        for first in range(0, source.shape[0], part):
            here = pl.ds(first, part)
            copies.append(
                pltpu.make_async_copy(source.at[here], target.at[here], sems.at[len(copies)])
            )
    for copy in copies:
        copy.start()
    return copies


def own_rows_kernel(experts, heads_dev, place, *refs):
    peers = len(refs) - 19
    sources, outs, targets, sems = refs[:9], refs[9:-10], refs[-10:-1], refs[-1]
    copies = load_all(list(zip(sources, targets)), sems)
    ids, shares, tokens, gain, key_weight, value_weight, k_gain, cosine, sine = targets
    copies[0].wait()
    copies[1].wait()
    rows = tokens.shape[0]
    chosen_ids = ids[...]
    lanes = lax.broadcasted_iota(jnp.int32, (experts, rows), 0)
    chosen = jnp.zeros((experts, rows), jnp.float32)
    for k in range(TOP):
        chosen = chosen + jnp.where(lanes == chosen_ids[k : k + 1], 1.0, 0.0)
    earlier = lax.broadcasted_iota(jnp.int32, (rows, rows), 0) < lax.broadcasted_iota(
        jnp.int32, (rows, rows), 1
    )
    rank = jnp.dot(
        chosen.astype(jnp.bfloat16),
        jnp.where(earlier, 1.0, 0.0).astype(jnp.bfloat16),
        preferred_element_type=jnp.float32,
    )
    slots = [
        jnp.sum(jnp.where(lanes == chosen_ids[k : k + 1], rank, 0.0), axis=0, keepdims=True)
        for k in range(TOP)
    ]
    slots = jnp.concatenate(slots, axis=0)
    left = jnp.concatenate([chosen_ids, shares[...]], axis=0).astype(jnp.float32)
    right = jnp.concatenate([slots, jnp.zeros_like(slots)], axis=0)
    for out in outs:
        out[rows:, :] = jnp.concatenate([left, right], axis=1).astype(jnp.bfloat16)
    for copy in copies[2:]:
        copy.wait()
    normed = rms_scale(tokens[...].astype(jnp.float32), gain[...]).astype(jnp.bfloat16)
    keys = jnp.dot(normed, key_weight[...], preferred_element_type=jnp.float32)
    values = jnp.dot(normed, value_weight[...], preferred_element_type=jnp.float32)
    cosine, sine = both_halves(cosine[...], sine[...])
    for head in range(KEY_VALUE_HEADS):
        cols = slice(head * HEAD_SIZE, (head + 1) * HEAD_SIZE)
        rotated = normed_rotated(keys[:, cols], k_gain[...], cosine, sine)
        pair = jnp.concatenate([rotated, values[:, cols]], axis=1).astype(jnp.bfloat16)
        for distance in range(peers):
            asked = (place[1] ^ distance) * heads_dev // (QUERY_HEADS // KEY_VALUE_HEADS)

            @pl.when(asked == head)
            def _(out=outs[distance], pair=pair):
                out[:rows, :] = pair


def query_kernel(*refs):
    *pieces, gain, w_query, q_gain, cosine, sine, out = refs
    rows = pieces[0].shape[0]
    heads = w_query.shape[1] // HEAD_SIZE
    for at, piece in enumerate(pieces):
        normed = rms_scale(piece[...].astype(jnp.float32), gain[...]).astype(jnp.bfloat16)
        queries = jnp.dot(normed, w_query[...], preferred_element_type=jnp.float32)
        here = pl.ds(at * rows, rows)
        turn = both_halves(cosine[here, :], sine[here, :])
        for head in range(heads):
            cols = slice(head * HEAD_SIZE, (head + 1) * HEAD_SIZE)
            rotated = normed_rotated(queries[:, cols], q_gain[...], *turn)
            out[at, pl.ds(head * rows, rows), :] = rotated.astype(jnp.bfloat16)


def attention_kernel(distances, rows, place, queries, both, w_out, *outs):
    block, me = place[0], place[1]
    heads = w_out.shape[0] // HEAD_SIZE
    width = heads * rows
    span = rows * (place.shape[0] - 2)
    stride = span + 2 * TOP * (place.shape[0] - 2)
    scale = HEAD_SIZE ** (-0.5) * LOG2E

    def step(first, states, masked):
        keys = both[pl.ds(first, span), :HEAD_SIZE]
        values = both[pl.ds(first, span), HEAD_SIZE:]
        result = []
        for at, (top, total, mixed) in enumerate(states):
            scores = lax.dot_general(
                keys, queries[at], (((1,), (1,)), ((), ())), preferred_element_type=jnp.float32
            )
            if masked:
                row = lax.broadcasted_iota(jnp.int32, (span, width), 0)
                key_pos = (me ^ (row // rows)) * rows + row % rows
                query = lax.broadcasted_iota(jnp.int32, (span, width), 1) % rows
                query_pos = (me ^ distances[at]) * rows + query
                scores = jnp.where(key_pos <= query_pos, scores, floor_value)
            new_top = jnp.maximum(top, jnp.max(scores, axis=0, keepdims=True))
            weights = jnp.exp2((scores - new_top) * scale)
            rescale = jnp.exp2((top - new_top) * scale)
            total = total * rescale + jnp.sum(weights, axis=0, keepdims=True)
            mixed = mixed * rescale + lax.dot_general(
                values,
                weights.astype(jnp.bfloat16),
                (((0,), (0,)), ((), ())),
                preferred_element_type=jnp.float32,
            )
            result.append((new_top, total, mixed))
        return tuple(result)

    states = tuple(
        (
            jnp.full((1, width), floor_value, jnp.float32),
            jnp.zeros((1, width), jnp.float32),
            jnp.zeros((HEAD_SIZE, width), jnp.float32),
        )
        for _ in distances
    )
    states = step(pl.multiple_of(block * stride, 2 * TOP), states, True)
    states = lax.fori_loop(
        0, block, lambda i, s: step(pl.multiple_of(i * stride, 2 * TOP), s, False), states
    )
    for (_, total, mixed), out in zip(states, outs):
        attended = (mixed / total).astype(jnp.bfloat16)
        attended = jnp.concatenate(
            [attended[:, head * rows : (head + 1) * rows] for head in range(heads)], axis=0
        )
        out[...] = lax.dot_general(
            attended, w_out[...], (((0,), (0,)), ((), ())), preferred_element_type=jnp.float32
        ).astype(jnp.bfloat16)


def residual_kernel(tokens, attention, partial, gain, residual, normed):
    summed = attention[...].astype(jnp.float32) + partial[...].astype(jnp.float32)
    rounded = (tokens[...].astype(jnp.float32) + summed).astype(jnp.bfloat16)
    residual[...] = rounded
    normed[...] = rms_scale(rounded.astype(jnp.float32), gain[...]).astype(jnp.bfloat16)


def slot_targets(table, expert):
    table = table.astype(jnp.float32)
    rows = table.shape[1] // 2
    named = table[:TOP, :rows] == expert.astype(jnp.float32)
    slot = jnp.max(jnp.where(named, table[:TOP, rows:], -1.0), axis=0, keepdims=True)
    weight = jnp.sum(jnp.where(named, table[TOP:, :rows], 0.0), axis=0, keepdims=True)
    return slot.astype(jnp.int32), weight * (1.0 / 1024.0)


def plane_targets(group, place, routing, near, away):
    block, me, count = place[0], place[1], routing.shape[1]
    table = routing[block ^ (2 * group), near]
    return [slot_targets(table, (block ^ core) * count + (me ^ away)) for core in (0, 1)]


def route_order(route):
    near, away = route
    return [n ^ a for a in away for n in near]


def dispatch_kernel(routes, group, capacity, place, routing, *refs):
    sources = refs[: sum(len(near) for near, _ in routes)]
    outs = refs[len(sources) :]
    rows = sources[0].shape[0]
    slots = lax.broadcasted_iota(jnp.int32, (capacity, rows), 0)
    for near, away in routes:
        some, sources = sources[: len(near)], sources[len(near) :]
        mine, outs = outs[: len(away)], outs[len(away) :]
        for at, (n, source) in enumerate(zip(near, some)):
            parts = []
            for a in away:
                for slot, _ in plane_targets(group, place, routing, n, a):
                    parts.append(jnp.where(slots == slot, 1.0, 0.0))
            hot = jnp.concatenate(parts, axis=0).astype(jnp.bfloat16)
            picked = jnp.dot(hot, source[...], preferred_element_type=jnp.float32)
            picked = picked.astype(jnp.bfloat16)
            for part in range(2 * len(away)):
                first = ((part % 2) * len(near) + at) * capacity
                mine[part // 2][first : first + capacity, :] = picked[
                    part * capacity : (part + 1) * capacity
                ]


def combine_kernel(routes, group, capacity, place, routing, *refs):
    count = sum(len(away) for _, away in routes)
    arrived, other, (kept, *outs) = refs[:count], refs[count], refs[count + 1 :]
    rows, width = kept.shape[0], other.shape[1]
    slots = lax.broadcasted_iota(jnp.int32, (capacity, rows), 0)
    base = 0
    for side, (near, away) in enumerate(routes):
        some, arrived = arrived[: len(away)], arrived[len(away) :]
        for at, n in enumerate(near):
            shares, produced = [], []
            for index, a in enumerate(away):
                for core, (slot, weight) in enumerate(plane_targets(group, place, routing, n, a)):
                    shares.append(jnp.where(slots == slot, weight, 0.0))
                    first = at * capacity
                    if core:
                        first += base + index * len(near) * capacity
                    piece = other if core else some[index]
                    produced.append(piece[first : first + capacity, :])
            total = lax.dot_general(
                jnp.concatenate(shares, axis=0).astype(jnp.bfloat16),
                jnp.concatenate(produced, axis=0),
                (((0,), (0,)), ((), ())),
                preferred_element_type=jnp.float32,
            )
            if n:
                outs[0][...] = total.astype(jnp.bfloat16)
                outs = outs[1:]
            else:
                kept[:, side * width : (side + 1) * width] = total
        base += len(near) * len(away) * capacity


def gather_kernel(counts, kept, *refs):
    *parts, out = refs
    width = out.shape[1] // len(counts)
    for side, count in enumerate(counts):
        cols = slice(side * width, (side + 1) * width)
        total = kept[:, cols]
        for part in parts[:count]:
            total = total + part[...].astype(jnp.float32)
        parts = parts[count:]
        for part in parts[sum(counts[side + 1 :]) :]:
            total = total + part[:, cols].astype(jnp.float32)
        out[:, cols] = total.astype(out.dtype)


def expert_kernel(routes, capacity, *refs):
    count = sum(len(away) for _, away in routes)
    came, (mate, w_gate, w_up, w_down) = refs[:count], refs[count : count + 4]
    outs = refs[count + 4 : 2 * count + 4]
    rows_in, hidden = refs[2 * count + 4 :]
    width = came[0].shape[1]
    half = rows_in.shape[1] // 2
    places = []
    for side, (near, away) in enumerate(routes):
        base = sum(len(some) for _, some in routes[:side])
        for at, d in enumerate(route_order((near, away))):
            places.append((side, base + at // len(near), (at % len(near)) * capacity, d * capacity))
    for at, (side, piece, first, to) in enumerate(places):
        rows_in[side, to : to + capacity, :] = came[piece][first : first + capacity, :]
        to = half + to
        rows_in[side, to : to + capacity, :] = mate[at * capacity : (at + 1) * capacity, :]
    for first in range(0, hidden.shape[1], 256):
        cols = slice(first, first + 256)
        gate = up = 0.0
        for side in range(len(routes)):
            depth = slice(side * width, (side + 1) * width)
            rows = rows_in[side]
            gate = gate + jnp.dot(rows, w_gate[depth, cols], preferred_element_type=jnp.float32)
            up = up + jnp.dot(rows, w_up[depth, cols], preferred_element_type=jnp.float32)
        hidden[:, cols] = (gate / (1.0 + jnp.exp(-gate)) * up).astype(jnp.bfloat16)
    for side in range(len(routes)):
        for first in range(0, width, 256):
            cols = slice(first, first + 256)
            down = w_down[:, side * width + first : side * width + first + 256]
            product = jnp.dot(hidden[...], down, preferred_element_type=jnp.float32)
            product = product.astype(jnp.bfloat16)
            for where, piece, to, at in places:
                if where == side:
                    out = outs[piece]
                    out[to : to + capacity, cols] = product[at : at + capacity]
                    to += out.shape[0] // 2
                    out[to : to + capacity, cols] = product[half + at : half + at + capacity]


def sum_kernel(*refs):
    *parts, out = refs
    total = parts[0][...].astype(jnp.float32)
    for part in parts[1:]:
        total = total + part[...].astype(jnp.float32)
    out[...] = total.astype(out.dtype)


def call(kernel, out_shape, specs, *args, name, scratch=(), limit=24, flops=1000):
    return pl.pallas_call(
        kernel,
        out_shape=out_shape,
        in_specs=specs,
        out_specs=jax.tree.map(lambda _: VMEM, out_shape),
        scratch_shapes=scratch,
        compiler_params=pltpu.CompilerParams(vmem_limit_bytes=limit * 1024 * 1024),
        cost_estimate=pl.CostEstimate(flops=flops, bytes_accessed=1000, transcendentals=0),
        name=name,
    )(*args)


def shards(
    tokens,
    ln1_gain,
    w_query,
    key_weight,
    value_weight,
    q_gain,
    k_gain,
    w_out,
    ln2_gain,
    expert_ids,
    route_weights,
    w_gate,
    w_up,
    w_down,
):
    rows, width = tokens.shape
    ctx_count = lax.axis_size("ctx")
    exp_count = lax.axis_size("exp")
    ctx_rows = rows * exp_count
    heads_dev = w_query.shape[1] // HEAD_SIZE
    group_width = QUERY_HEADS // KEY_VALUE_HEADS
    me_ctx = lax.axis_index("ctx").astype(jnp.int32)
    me_exp = lax.axis_index("exp").astype(jnp.int32)
    place = jnp.stack([me_ctx, me_exp] + [jnp.int32(0)] * exp_count)
    peers = list(range(exp_count))
    bf16 = functools.partial(jax.ShapeDtypeStruct, dtype=jnp.bfloat16)

    experts = ctx_count * exp_count
    capacity = max(2, 3 * rows * TOP // (2 * experts))
    capacity = -(-capacity // 16) * 16
    ln1_row = ln1_gain.reshape(1, width)
    own_first = me_ctx * ctx_rows + me_exp * rows
    cosine, sine = rope_tables(own_first + jnp.arange(rows))
    own_args = [
        expert_ids.T,
        route_weights.T,
        tokens,
        ln1_row,
        key_weight,
        value_weight,
        k_gain.reshape(1, HEAD_SIZE),
        cosine,
        sine,
    ]
    own_kv = call(
        functools.partial(own_rows_kernel, experts, heads_dev),
        [bf16((rows + 2 * TOP, 2 * HEAD_SIZE)) for _ in peers],
        [SMEM] + [ANY] * 9,
        place,
        *own_args,
        name="own_rows",
        scratch=[pltpu.VMEM(a.shape, a.dtype) for a in own_args] + [pltpu.SemaphoreType.DMA((18,))],
        limit=60,
    )
    block_kv = [own_kv[0]] + [swap(own_kv[d], "exp", d) for d in peers[1:]]
    both = [part[:rows] for part in block_kv] + [part[rows:] for part in block_kv]
    both = lax.all_gather(jnp.concatenate(both, axis=0), "ctx", axis=0, tiled=True)
    sent = tie(tokens, *block_kv[1:])
    pieces = [tokens] + [swap(sent, "exp", d) for d in peers[1:]]
    routing = both.reshape(ctx_count, -1, 2 * HEAD_SIZE)[:, ctx_rows:]
    routing = routing.reshape(ctx_count, exp_count, 2 * TOP, 2 * HEAD_SIZE)

    positions = jnp.concatenate(
        [me_ctx * ctx_rows + (me_exp ^ d) * rows + jnp.arange(rows) for d in peers]
    )
    cosine, sine = rope_tables(positions)
    queries = call(
        query_kernel,
        bf16((exp_count, heads_dev * rows, HEAD_SIZE)),
        [VMEM] * (exp_count + 5),
        *pieces,
        ln1_row,
        w_query,
        q_gain.reshape(1, HEAD_SIZE),
        cosine,
        sine,
        name="queries",
    )

    order = sorted(peers, key=lambda d: -bin(d).count("1"))
    partials, last = {}, ()
    for some in [[d] for d in order]:
        asked = queries[some[0] : some[0] + 1]
        made = call(
            functools.partial(attention_kernel, some, rows),
            [bf16((rows, width)) for _ in some],
            [SMEM, VMEM, VMEM, VMEM],
            place,
            tie(asked, *last),
            both,
            w_out,
            name="attention",
        )
        partials.update(zip(some, made))
        last = tuple(made)
    attention = partials[0]
    parts = [swap(partials[d], "exp", d) for d in order if d]
    for part in parts[:-1]:
        attention = call(
            sum_kernel,
            jax.ShapeDtypeStruct((rows, width), jnp.float32),
            [VMEM] * 2,
            attention,
            part,
            name="add",
            flops=3_000_000_000,
        )
    residual, normed = call(
        residual_kernel,
        [bf16((rows, width)), bf16((rows, width))],
        [VMEM] * 4,
        tokens,
        attention,
        parts[-1],
        ln2_gain.reshape(1, width),
        name="residual",
    )

    groups = ctx_count // 2
    low, high = [0, 1], list(range(0, exp_count, 2))
    routes = [(low, high), (high, low)]
    half = width // 2
    far = [normed]
    for g in range(1, groups):
        far.append(swap(far[g & (g - 1)], "ctx", 2 * (g & -g)))
    in_flight = {}

    def send(array, d, kind):
        came = swap(tie(array, *in_flight.get((kind, d), ())), "exp", d)
        in_flight[kind, d] = (came,)
        return came

    arrived = []
    for g in range(groups):
        sources = []
        for side, (near, _) in enumerate(routes):
            part = far[g][:, side * half : (side + 1) * half]
            sources += [part] + [send(part, n, "whole") for n in near[1:]]
        outgoing = call(
            functools.partial(dispatch_kernel, routes, g, capacity),
            [bf16((2 * len(near) * capacity, half)) for near, away in routes for _ in away],
            [SMEM, VMEM] + [VMEM] * len(sources),
            place,
            routing,
            *sources,
            name="dispatch",
        )
        onward = [a for _, away in routes for a in away]
        arrived.append([send(out, a, "picked") if a else out for out, a in zip(outgoing, onward)])

    def to_mate(parts, *others):
        halves = [part[part.shape[0] // 2 :] for part in parts]
        return swap(tie(jnp.concatenate(halves, axis=0), *others), "ctx", 1)

    produced = []
    slots = exp_count * capacity
    for g, came in enumerate(arrived):
        ready = produced if g == groups - 2 else []
        produced.append(
            call(
                functools.partial(expert_kernel, routes, capacity),
                [bf16((2 * len(near) * capacity, half)) for near, away in routes for _ in away],
                [VMEM] * (len(came) + 4),
                *came,
                to_mate(came, *[made[0] for made in ready]),
                w_gate[0],
                w_up[0],
                w_down[0],
                name="expert",
                scratch=[
                    pltpu.VMEM((2, 2 * slots, half), jnp.bfloat16),
                    pltpu.VMEM((2 * slots, w_gate.shape[2]), jnp.bfloat16),
                ],
            )
        )

    passing = [[] for _ in range(groups)]
    onward_picked = [a for _, away in routes for a in away]
    for g in reversed(range(groups)):
        back = [send(p, a, "picked") if a else p for p, a in zip(produced[g], onward_picked)]
        back.append(to_mate(back))
        onward = [n for near, _ in routes for n in near[1:]]
        kept, *sums = call(
            functools.partial(combine_kernel, routes, g, capacity),
            [jax.ShapeDtypeStruct((rows, width), jnp.float32)] + [bf16((rows, half)) for _ in onward],
            [SMEM, VMEM] + [VMEM] * len(back),
            place,
            routing,
            *back,
            name="combine",
        )
        sums = [send(part, n, "whole") for part, n in zip(sums, onward)]
        total = call(
            functools.partial(gather_kernel, [len(near) - 1 for near, _ in routes]),
            bf16((rows, width)) if g else jax.ShapeDtypeStruct((rows, width), jnp.float32),
            [VMEM] * (1 + len(sums) + (len(passing[g]) if g else 0)),
            kept,
            *sums,
            *(passing[g] if g else []),
            name="gather",
        )
        if g:
            passing[g & (g - 1)].append(swap(total, "ctx", 2 * (g & -g)))
    early = call(
        sum_kernel,
        jax.ShapeDtypeStruct((rows, width), jnp.float32),
        [VMEM] * (1 + len(passing[0])),
        residual,
        *passing[0],
        name="add",
        flops=10_000_000_000,
    )
    return call(sum_kernel, bf16((rows, width)), [VMEM] * 2, early, total, name="add")


def solution(mesh):
    in_specs = (
        P(("ctx", "exp"), None),
        P(),
        P(None, "exp"),
        P(),
        P(),
        P(),
        P(),
        P("exp", None),
        P(),
        P(("ctx", "exp"), None),
        P(("ctx", "exp"), None),
        P(("ctx", "exp"), None, None),
        P(("ctx", "exp"), None, None),
        P(("ctx", "exp"), None, None),
    )
    out_specs = P(("ctx", "exp"), None)
    return jax.shard_map(shards, mesh=mesh, in_specs=in_specs, out_specs=out_specs, check_vma=False)
```

```python
import functools

import jax
import jax.numpy as jnp
from jax import lax
from jax.experimental import pallas as pl
from jax.experimental.pallas import tpu as pltpu
from jax.sharding import PartitionSpec as P

HEAD_SIZE = 128
QUERY_HEADS = 16
KEY_VALUE_HEADS = 2
TOP = 8
LOG2E = 1.4426950408889634

eps_value = 1e-06
theta_value = 1000000.0
floor_value = -1e30

VMEM = pl.BlockSpec(memory_space=pltpu.VMEM)
SMEM = pl.BlockSpec(memory_space=pltpu.SMEM)
ANY = pl.BlockSpec(memory_space=pl.ANY)


def rms_scale(value_states, norm_gain):
    return (
        value_states
        * lax.rsqrt(jnp.mean(value_states * value_states, axis=-1, keepdims=True) + eps_value)
        * norm_gain
    )


def swap(array, axis, distance):
    pairs = [(i, i ^ distance) for i in range(lax.axis_size(axis))]
    return lax.ppermute(array, axis, pairs)


def tie(array, *others):
    if not others:
        return array
    return lax.optimization_barrier((array, *others))[0]


def rope_tables(positions):
    half = HEAD_SIZE // 2
    frequency = theta_value ** (-2.0 * jnp.arange(half, dtype=jnp.float32) / HEAD_SIZE)
    angles = positions.astype(jnp.float32)[:, None] * frequency[None, :]
    return jnp.cos(angles), jnp.sin(angles)


def both_halves(cosine, sine):
    return jnp.concatenate([cosine, cosine], axis=1), jnp.concatenate([-sine, sine], axis=1)


def normed_rotated(states, gain, cosine, sine):
    states = rms_scale(states, gain)
    return states * cosine + pltpu.roll(states, HEAD_SIZE // 2, 1) * sine


def load_all(pairs, sems):
    copies = []
    for source, target in pairs:
        part = source.shape[0] // 4 if source.shape[0] >= 128 and source.shape[1] > 128 else source.shape[0]
        for first in range(0, source.shape[0], part):
            here = pl.ds(first, part)
            copies.append(
                pltpu.make_async_copy(source.at[here], target.at[here], sems.at[len(copies)])
            )
    for copy in copies:
        copy.start()
    return copies


def own_rows_kernel(experts, heads_dev, place, *refs):
    peers = len(refs) - 19
    sources, outs, targets, sems = refs[:9], refs[9:-10], refs[-10:-1], refs[-1]
    copies = load_all(list(zip(sources, targets)), sems)
    ids, shares, tokens, gain, key_weight, value_weight, k_gain, cosine, sine = targets
    copies[0].wait()
    copies[1].wait()
    rows = tokens.shape[0]
    chosen_ids = ids[...]
    lanes = lax.broadcasted_iota(jnp.int32, (experts, rows), 0)
    chosen = jnp.zeros((experts, rows), jnp.float32)
    for k in range(TOP):
        chosen = chosen + jnp.where(lanes == chosen_ids[k : k + 1], 1.0, 0.0)
    earlier = lax.broadcasted_iota(jnp.int32, (rows, rows), 0) < lax.broadcasted_iota(
        jnp.int32, (rows, rows), 1
    )
    rank = jnp.dot(
        chosen.astype(jnp.bfloat16),
        jnp.where(earlier, 1.0, 0.0).astype(jnp.bfloat16),
        preferred_element_type=jnp.float32,
    )
    slots = [
        jnp.sum(jnp.where(lanes == chosen_ids[k : k + 1], rank, 0.0), axis=0, keepdims=True)
        for k in range(TOP)
    ]
    slots = jnp.concatenate(slots, axis=0)
    left = jnp.concatenate([chosen_ids, shares[...]], axis=0).astype(jnp.float32)
    right = jnp.concatenate([slots, jnp.zeros_like(slots)], axis=0)
    for out in outs:
        out[rows:, :] = jnp.concatenate([left, right], axis=1).astype(jnp.bfloat16)
    for copy in copies[2:]:
        copy.wait()
    normed = rms_scale(tokens[...].astype(jnp.float32), gain[...]).astype(jnp.bfloat16)
    keys = jnp.dot(normed, key_weight[...], preferred_element_type=jnp.float32)
    values = jnp.dot(normed, value_weight[...], preferred_element_type=jnp.float32)
    cosine, sine = both_halves(cosine[...], sine[...])
    for head in range(KEY_VALUE_HEADS):
        cols = slice(head * HEAD_SIZE, (head + 1) * HEAD_SIZE)
        rotated = normed_rotated(keys[:, cols], k_gain[...], cosine, sine)
        pair = jnp.concatenate([rotated, values[:, cols]], axis=1).astype(jnp.bfloat16)
        for distance in range(peers):
            asked = (place[1] ^ distance) * heads_dev // (QUERY_HEADS // KEY_VALUE_HEADS)

            @pl.when(asked == head)
            def _(out=outs[distance], pair=pair):
                out[:rows, :] = pair


def query_kernel(*refs):
    *pieces, gain, w_query, q_gain, cosine, sine, out = refs
    rows = pieces[0].shape[0]
    heads = w_query.shape[1] // HEAD_SIZE
    for at, piece in enumerate(pieces):
        normed = rms_scale(piece[...].astype(jnp.float32), gain[...]).astype(jnp.bfloat16)
        queries = jnp.dot(normed, w_query[...], preferred_element_type=jnp.float32)
        here = pl.ds(at * rows, rows)
        turn = both_halves(cosine[here, :], sine[here, :])
        for head in range(heads):
            cols = slice(head * HEAD_SIZE, (head + 1) * HEAD_SIZE)
            rotated = normed_rotated(queries[:, cols], q_gain[...], *turn)
            out[at, pl.ds(head * rows, rows), :] = rotated.astype(jnp.bfloat16)


def attention_kernel(distances, rows, place, queries, both, w_out, *outs):
    block, me = place[0], place[1]
    heads = w_out.shape[0] // HEAD_SIZE
    width = heads * rows
    span = rows * (place.shape[0] - 2)
    stride = span + 2 * TOP * (place.shape[0] - 2)
    scale = HEAD_SIZE ** (-0.5) * LOG2E

    def step(first, states, masked):
        keys = both[pl.ds(first, span), :HEAD_SIZE]
        values = both[pl.ds(first, span), HEAD_SIZE:]
        result = []
        for at, (top, total, mixed) in enumerate(states):
            scores = lax.dot_general(
                keys, queries[at], (((1,), (1,)), ((), ())), preferred_element_type=jnp.float32
            )
            if masked:
                row = lax.broadcasted_iota(jnp.int32, (span, width), 0)
                key_pos = (me ^ (row // rows)) * rows + row % rows
                query = lax.broadcasted_iota(jnp.int32, (span, width), 1) % rows
                query_pos = (me ^ distances[at]) * rows + query
                scores = jnp.where(key_pos <= query_pos, scores, floor_value)
            new_top = jnp.maximum(top, jnp.max(scores, axis=0, keepdims=True))
            weights = jnp.exp2((scores - new_top) * scale)
            rescale = jnp.exp2((top - new_top) * scale)
            total = total * rescale + jnp.sum(weights, axis=0, keepdims=True)
            mixed = mixed * rescale + lax.dot_general(
                values,
                weights.astype(jnp.bfloat16),
                (((0,), (0,)), ((), ())),
                preferred_element_type=jnp.float32,
            )
            result.append((new_top, total, mixed))
        return tuple(result)

    states = tuple(
        (
            jnp.full((1, width), floor_value, jnp.float32),
            jnp.zeros((1, width), jnp.float32),
            jnp.zeros((HEAD_SIZE, width), jnp.float32),
        )
        for _ in distances
    )
    states = step(pl.multiple_of(block * stride, 2 * TOP), states, True)

    def blocks(first, count, states):
        for at in range(count):
            states = step(pl.multiple_of((first + at) * stride, 2 * TOP), states, False)
        return states

    states = lax.fori_loop(0, block // 2, lambda i, s: blocks(2 * i, 2, s), states)
    states = lax.fori_loop(0, block % 2, lambda i, s: blocks(block - 1, 1, s), states)
    for (_, total, mixed), out in zip(states, outs):
        attended = (mixed / total).astype(jnp.bfloat16)
        attended = jnp.concatenate(
            [attended[:, head * rows : (head + 1) * rows] for head in range(heads)], axis=0
        )
        out[...] = lax.dot_general(
            attended, w_out[...], (((0,), (0,)), ((), ())), preferred_element_type=jnp.float32
        ).astype(jnp.bfloat16)


def residual_kernel(tokens, attention, partial, gain, residual, normed):
    summed = attention[...].astype(jnp.float32) + partial[...].astype(jnp.float32)
    rounded = (tokens[...].astype(jnp.float32) + summed).astype(jnp.bfloat16)
    residual[...] = rounded
    normed[...] = rms_scale(rounded.astype(jnp.float32), gain[...]).astype(jnp.bfloat16)


def slot_targets(table, expert):
    table = table.astype(jnp.float32)
    rows = table.shape[1] // 2
    named = table[:TOP, :rows] == expert.astype(jnp.float32)
    slot = jnp.max(jnp.where(named, table[:TOP, rows:], -1.0), axis=0, keepdims=True)
    weight = jnp.sum(jnp.where(named, table[TOP:, :rows], 0.0), axis=0, keepdims=True)
    return slot.astype(jnp.int32), weight * (1.0 / 1024.0)


def plane_targets(group, place, routing, near, away):
    block, me, count = place[0], place[1], routing.shape[1]
    table = routing[block ^ (2 * group), near]
    return [slot_targets(table, (block ^ core) * count + (me ^ away)) for core in (0, 1)]


def route_order(route):
    near, away = route
    return [n ^ a for a in away for n in near]


def dispatch_kernel(routes, group, capacity, place, routing, *refs):
    sources = refs[: sum(len(near) for near, _ in routes)]
    outs = refs[len(sources) :]
    rows = sources[0].shape[0]
    slots = lax.broadcasted_iota(jnp.int32, (capacity, rows), 0)
    for near, away in routes:
        some, sources = sources[: len(near)], sources[len(near) :]
        mine, outs = outs[: len(away)], outs[len(away) :]
        for at, (n, source) in enumerate(zip(near, some)):
            parts = []
            for a in away:
                for slot, _ in plane_targets(group, place, routing, n, a):
                    parts.append(jnp.where(slots == slot, 1.0, 0.0))
            hot = jnp.concatenate(parts, axis=0).astype(jnp.bfloat16)
            picked = jnp.dot(hot, source[...], preferred_element_type=jnp.float32)
            picked = picked.astype(jnp.bfloat16)
            for part in range(2 * len(away)):
                first = ((part % 2) * len(near) + at) * capacity
                mine[part // 2][first : first + capacity, :] = picked[
                    part * capacity : (part + 1) * capacity
                ]


def combine_kernel(group, capacity, place, routing, *refs):
    count = routing.shape[1]
    returned, passing, out = refs[:count], refs[count:-1], refs[-1]
    slots = lax.broadcasted_iota(jnp.int32, (capacity, out.shape[0]), 0)
    parts = []
    for distance in range(len(returned)):
        for slot, weight in plane_targets(group, place, routing, 0, distance):
            parts.append(jnp.where(slots == slot, weight, 0.0))
    shares = jnp.concatenate(parts, axis=0).astype(jnp.bfloat16)
    produced = jnp.concatenate([ref[...] for ref in returned], axis=0)
    total = lax.dot_general(
        shares, produced, (((0,), (0,)), ((), ())), preferred_element_type=jnp.float32
    )
    for part in passing:
        total = total + part[...].astype(jnp.float32)
    out[...] = total.astype(out.dtype)


def expert_kernel(routes, capacity, *refs):
    count = sum(len(away) for _, away in routes)
    came, (mate, w_gate, w_up, w_down) = refs[:count], refs[count : count + 4]
    own, other, rows_in, hidden = refs[count + 4 :]
    width = came[0].shape[1]
    half = rows_in.shape[1] // 2
    places = []
    for side, (near, away) in enumerate(routes):
        base = sum(len(some) for _, some in routes[:side])
        for at, d in enumerate(route_order((near, away))):
            places.append((side, base + at // len(near), (at % len(near)) * capacity, d * capacity))
    for at, (side, piece, first, to) in enumerate(places):
        rows_in[side, to : to + capacity, :] = came[piece][first : first + capacity, :]
        to = half + to
        rows_in[side, to : to + capacity, :] = mate[at * capacity : (at + 1) * capacity, :]
    for first in range(0, hidden.shape[1], 256):
        cols = slice(first, first + 256)
        gate = up = 0.0
        for side in range(len(routes)):
            depth = slice(side * width, (side + 1) * width)
            rows = rows_in[side]
            gate = gate + jnp.dot(rows, w_gate[depth, cols], preferred_element_type=jnp.float32)
            up = up + jnp.dot(rows, w_up[depth, cols], preferred_element_type=jnp.float32)
        hidden[:, cols] = (gate / (1.0 + jnp.exp(-gate)) * up).astype(jnp.bfloat16)
    for side in range(len(routes)):
        for first in range(0, width, 256):
            down = w_down[:, side * width + first : side * width + first + 256]
            product = jnp.dot(hidden[...], down, preferred_element_type=jnp.float32)
            product = product.astype(jnp.bfloat16)
            cols = slice(side * width + first, side * width + first + 256)
            own[:, cols] = product[:half]
            other[:, cols] = product[half:]


def sum_kernel(*refs):
    *parts, out = refs
    total = parts[0][...].astype(jnp.float32)
    for part in parts[1:]:
        total = total + part[...].astype(jnp.float32)
    out[...] = total.astype(out.dtype)


def call(kernel, out_shape, specs, *args, name, scratch=(), limit=24, flops=1000):
    return pl.pallas_call(
        kernel,
        out_shape=out_shape,
        in_specs=specs,
        out_specs=jax.tree.map(lambda _: VMEM, out_shape),
        scratch_shapes=scratch,
        compiler_params=pltpu.CompilerParams(vmem_limit_bytes=limit * 1024 * 1024),
        cost_estimate=pl.CostEstimate(flops=flops, bytes_accessed=1000, transcendentals=0),
        name=name,
    )(*args)


def shards(
    tokens,
    ln1_gain,
    w_query,
    key_weight,
    value_weight,
    q_gain,
    k_gain,
    w_out,
    ln2_gain,
    expert_ids,
    route_weights,
    w_gate,
    w_up,
    w_down,
):
    rows, width = tokens.shape
    ctx_count = lax.axis_size("ctx")
    exp_count = lax.axis_size("exp")
    ctx_rows = rows * exp_count
    heads_dev = w_query.shape[1] // HEAD_SIZE
    group_width = QUERY_HEADS // KEY_VALUE_HEADS
    me_ctx = lax.axis_index("ctx").astype(jnp.int32)
    me_exp = lax.axis_index("exp").astype(jnp.int32)
    place = jnp.stack([me_ctx, me_exp] + [jnp.int32(0)] * exp_count)
    peers = list(range(exp_count))
    bf16 = functools.partial(jax.ShapeDtypeStruct, dtype=jnp.bfloat16)

    experts = ctx_count * exp_count
    capacity = max(2, 3 * rows * TOP // (2 * experts))
    capacity = -(-capacity // 16) * 16
    ln1_row = ln1_gain.reshape(1, width)
    own_first = me_ctx * ctx_rows + me_exp * rows
    cosine, sine = rope_tables(own_first + jnp.arange(rows))
    own_args = [
        expert_ids.T,
        route_weights.T,
        tokens,
        ln1_row,
        key_weight,
        value_weight,
        k_gain.reshape(1, HEAD_SIZE),
        cosine,
        sine,
    ]
    own_kv = call(
        functools.partial(own_rows_kernel, experts, heads_dev),
        [bf16((rows + 2 * TOP, 2 * HEAD_SIZE)) for _ in peers],
        [SMEM] + [ANY] * 9,
        place,
        *own_args,
        name="own_rows",
        scratch=[pltpu.VMEM(a.shape, a.dtype) for a in own_args] + [pltpu.SemaphoreType.DMA((18,))],
        limit=60,
    )
    block_kv = [own_kv[0]] + [swap(own_kv[d], "exp", d) for d in peers[1:]]
    both = [part[:rows] for part in block_kv] + [part[rows:] for part in block_kv]
    both = lax.all_gather(jnp.concatenate(both, axis=0), "ctx", axis=0, tiled=True)
    sent = tie(tokens, *block_kv[1:])
    pieces = [tokens] + [swap(sent, "exp", d) for d in peers[1:]]
    routing = both.reshape(ctx_count, -1, 2 * HEAD_SIZE)[:, ctx_rows:]
    routing = routing.reshape(ctx_count, exp_count, 2 * TOP, 2 * HEAD_SIZE)

    positions = jnp.concatenate(
        [me_ctx * ctx_rows + (me_exp ^ d) * rows + jnp.arange(rows) for d in peers]
    )
    cosine, sine = rope_tables(positions)
    queries = call(
        query_kernel,
        bf16((exp_count, heads_dev * rows, HEAD_SIZE)),
        [VMEM] * (exp_count + 5),
        *pieces,
        ln1_row,
        w_query,
        q_gain.reshape(1, HEAD_SIZE),
        cosine,
        sine,
        name="queries",
    )

    order = sorted(peers, key=lambda d: -bin(d).count("1"))
    partials, last = {}, ()
    for some in [[d] for d in order]:
        asked = queries[some[0] : some[0] + 1]
        made = call(
            functools.partial(attention_kernel, some, rows),
            [bf16((rows, width)) for _ in some],
            [SMEM, VMEM, VMEM, VMEM],
            place,
            tie(asked, *last),
            both,
            w_out,
            name="attention",
        )
        partials.update(zip(some, made))
        last = tuple(made)
    attention = partials[0]
    parts = [swap(partials[d], "exp", d) for d in order if d]
    for part in parts[:-1]:
        attention = call(
            sum_kernel,
            jax.ShapeDtypeStruct((rows, width), jnp.float32),
            [VMEM] * 2,
            attention,
            part,
            name="add",
            flops=3_000_000_000,
        )
    residual, normed = call(
        residual_kernel,
        [bf16((rows, width)), bf16((rows, width))],
        [VMEM] * 4,
        tokens,
        attention,
        parts[-1],
        ln2_gain.reshape(1, width),
        name="residual",
    )

    groups = ctx_count // 2
    low, high = [0, 1], list(range(0, exp_count, 2))
    routes = [(low, high), (high, low)]
    half = width // 2
    far = [normed]
    for g in range(1, groups):
        first = tie(far[g & (g - 1)], *(far[1:] if g == 2 else []))
        far.append(swap(first, "ctx", 2 * (g & -g)))
    in_flight = {}

    def send(array, d, kind):
        came = swap(tie(array, *in_flight.get((kind, d), ())), "exp", d)
        in_flight[kind, d] = (came,)
        return came

    arrived = []
    for g in range(groups):
        sources = []
        for side, (near, _) in enumerate(routes):
            part = far[g][:, side * half : (side + 1) * half]
            sources += [part] + [send(part, n, "whole") for n in near[1:]]
        outgoing = call(
            functools.partial(dispatch_kernel, routes, g, capacity),
            [bf16((2 * len(near) * capacity, half)) for near, away in routes for _ in away],
            [SMEM, VMEM] + [VMEM] * len(sources),
            place,
            tie(routing, *[part for came in arrived[-1:] for part in came]),
            *sources,
            name="dispatch",
        )
        onward = [a for _, away in routes for a in away]
        arrived.append([send(out, a, "picked") if a else out for out, a in zip(outgoing, onward)])

    produced = []
    slots = exp_count * capacity
    for came in arrived:
        mate = jnp.concatenate([part[part.shape[0] // 2 :] for part in came], axis=0)
        own, other = call(
            functools.partial(expert_kernel, routes, capacity),
            [bf16((slots, width)), bf16((slots, width))],
            [VMEM] * (len(came) + 4),
            *came,
            swap(mate, "ctx", 1),
            w_gate[0],
            w_up[0],
            w_down[0],
            name="expert",
            scratch=[
                pltpu.VMEM((2, 2 * slots, half), jnp.bfloat16),
                pltpu.VMEM((2 * slots, w_gate.shape[2]), jnp.bfloat16),
            ],
        )
        produced.append((own, swap(other, "ctx", 1)))

    passing, in_flight = [[] for _ in range(groups)], {}
    for g in [*range(1, min(2, groups)), *reversed(range(2, groups)), 0]:
        back = []
        for d in peers:
            mine = slice(d * capacity, (d + 1) * capacity)
            back.append(jnp.concatenate([part[mine] for part in produced[g]], axis=0))
        back = [back[0]] + [send(back[d], d, "back") for d in peers[1:]]
        total = call(
            functools.partial(combine_kernel, g, capacity),
            bf16((rows, width)) if g else jax.ShapeDtypeStruct((rows, width), jnp.float32),
            [SMEM, VMEM] + [VMEM] * (exp_count + (len(passing[g]) if g else 0)),
            place,
            routing,
            *back,
            *(passing[g] if g else []),
            name="combine",
        )
        if g:
            passing[g & (g - 1)].append(swap(total, "ctx", 2 * (g & -g)))
    early = call(
        sum_kernel,
        jax.ShapeDtypeStruct((rows, width), jnp.float32),
        [VMEM] * (1 + len(passing[0])),
        residual,
        *passing[0],
        name="add",
        flops=10_000_000_000,
    )
    return call(sum_kernel, bf16((rows, width)), [VMEM] * 2, early, total, name="add")


def solution(mesh):
    in_specs = (
        P(("ctx", "exp"), None),
        P(),
        P(None, "exp"),
        P(),
        P(),
        P(),
        P(),
        P("exp", None),
        P(),
        P(("ctx", "exp"), None),
        P(("ctx", "exp"), None),
        P(("ctx", "exp"), None, None),
        P(("ctx", "exp"), None, None),
        P(("ctx", "exp"), None, None),
    )
    out_specs = P(("ctx", "exp"), None)
    return jax.shard_map(shards, mesh=mesh, in_specs=in_specs, out_specs=out_specs, check_vma=False)
```

```python
import functools

import jax
import jax.numpy as jnp
from jax import lax
from jax.experimental import pallas as pl
from jax.experimental.pallas import tpu as pltpu
from jax.sharding import PartitionSpec as P

HEAD_SIZE = 128
QUERY_HEADS = 16
KEY_VALUE_HEADS = 2
TOP = 8
LOG2E = 1.4426950408889634

eps_value = 1e-06
theta_value = 1000000.0
floor_value = -1e30

VMEM = pl.BlockSpec(memory_space=pltpu.VMEM)
SMEM = pl.BlockSpec(memory_space=pltpu.SMEM)
ANY = pl.BlockSpec(memory_space=pl.ANY)


def rms_scale(value_states, norm_gain):
    return (
        value_states
        * lax.rsqrt(jnp.mean(value_states * value_states, axis=-1, keepdims=True) + eps_value)
        * norm_gain
    )


def swap(array, axis, distance):
    pairs = [(i, i ^ distance) for i in range(lax.axis_size(axis))]
    return lax.ppermute(array, axis, pairs)


def tie(array, *others):
    if not others:
        return array
    return lax.optimization_barrier((array, *others))[0]


def rope_tables(positions):
    half = HEAD_SIZE // 2
    frequency = theta_value ** (-2.0 * jnp.arange(half, dtype=jnp.float32) / HEAD_SIZE)
    angles = positions.astype(jnp.float32)[:, None] * frequency[None, :]
    return jnp.cos(angles), jnp.sin(angles)


def both_halves(cosine, sine):
    return jnp.concatenate([cosine, cosine], axis=1), jnp.concatenate([-sine, sine], axis=1)


def normed_rotated(states, gain, cosine, sine):
    states = rms_scale(states, gain)
    return states * cosine + pltpu.roll(states, HEAD_SIZE // 2, 1) * sine


def load_all(pairs, sems):
    copies = []
    for source, target in pairs:
        part = source.shape[0] // 4 if source.shape[0] >= 128 and source.shape[1] > 128 else source.shape[0]
        for first in range(0, source.shape[0], part):
            here = pl.ds(first, part)
            copies.append(
                pltpu.make_async_copy(source.at[here], target.at[here], sems.at[len(copies)])
            )
    for copy in copies:
        copy.start()
    return copies


def own_rows_kernel(experts, heads_dev, place, *refs):
    peers = len(refs) - 19
    sources, outs, targets, sems = refs[:9], refs[9:-10], refs[-10:-1], refs[-1]
    copies = load_all(list(zip(sources, targets)), sems)
    ids, shares, tokens, gain, key_weight, value_weight, k_gain, cosine, sine = targets
    copies[0].wait()
    copies[1].wait()
    rows = tokens.shape[0]
    chosen_ids = ids[...]
    lanes = lax.broadcasted_iota(jnp.int32, (experts, rows), 0)
    chosen = jnp.zeros((experts, rows), jnp.float32)
    for k in range(TOP):
        chosen = chosen + jnp.where(lanes == chosen_ids[k : k + 1], 1.0, 0.0)
    earlier = lax.broadcasted_iota(jnp.int32, (rows, rows), 0) < lax.broadcasted_iota(
        jnp.int32, (rows, rows), 1
    )
    rank = jnp.dot(
        chosen.astype(jnp.bfloat16),
        jnp.where(earlier, 1.0, 0.0).astype(jnp.bfloat16),
        preferred_element_type=jnp.float32,
    )
    slots = [
        jnp.sum(jnp.where(lanes == chosen_ids[k : k + 1], rank, 0.0), axis=0, keepdims=True)
        for k in range(TOP)
    ]
    slots = jnp.concatenate(slots, axis=0)
    left = jnp.concatenate([chosen_ids, shares[...]], axis=0).astype(jnp.float32)
    right = jnp.concatenate([slots, jnp.zeros_like(slots)], axis=0)
    for out in outs:
        out[rows:, :] = jnp.concatenate([left, right], axis=1).astype(jnp.bfloat16)
    for copy in copies[2:]:
        copy.wait()
    normed = rms_scale(tokens[...].astype(jnp.float32), gain[...]).astype(jnp.bfloat16)
    keys = jnp.dot(normed, key_weight[...], preferred_element_type=jnp.float32)
    values = jnp.dot(normed, value_weight[...], preferred_element_type=jnp.float32)
    cosine, sine = both_halves(cosine[...], sine[...])
    for head in range(KEY_VALUE_HEADS):
        cols = slice(head * HEAD_SIZE, (head + 1) * HEAD_SIZE)
        rotated = normed_rotated(keys[:, cols], k_gain[...], cosine, sine)
        pair = jnp.concatenate([rotated, values[:, cols]], axis=1).astype(jnp.bfloat16)
        for distance in range(peers):
            asked = (place[1] ^ distance) * heads_dev // (QUERY_HEADS // KEY_VALUE_HEADS)

            @pl.when(asked == head)
            def _(out=outs[distance], pair=pair):
                out[:rows, :] = pair


def query_kernel(*refs):
    *pieces, gain, w_query, q_gain, cosine, sine, out = refs
    rows = pieces[0].shape[0]
    heads = w_query.shape[1] // HEAD_SIZE
    for at, piece in enumerate(pieces):
        normed = rms_scale(piece[...].astype(jnp.float32), gain[...]).astype(jnp.bfloat16)
        queries = jnp.dot(normed, w_query[...], preferred_element_type=jnp.float32)
        here = pl.ds(at * rows, rows)
        turn = both_halves(cosine[here, :], sine[here, :])
        for head in range(heads):
            cols = slice(head * HEAD_SIZE, (head + 1) * HEAD_SIZE)
            rotated = normed_rotated(queries[:, cols], q_gain[...], *turn)
            out[at, pl.ds(head * rows, rows), :] = rotated.astype(jnp.bfloat16)


def attention_kernel(distances, rows, place, queries, both, w_out, *outs):
    block, me = place[0], place[1]
    heads = w_out.shape[0] // HEAD_SIZE
    width = heads * rows
    span = rows * (place.shape[0] - 2)
    stride = span + 2 * TOP * (place.shape[0] - 2)
    scale = HEAD_SIZE ** (-0.5) * LOG2E

    def step(first, states, masked):
        keys = both[pl.ds(first, span), :HEAD_SIZE]
        values = both[pl.ds(first, span), HEAD_SIZE:]
        result = []
        for at, (top, total, mixed) in enumerate(states):
            scores = lax.dot_general(
                keys, queries[at], (((1,), (1,)), ((), ())), preferred_element_type=jnp.float32
            )
            if masked:
                row = lax.broadcasted_iota(jnp.int32, (span, width), 0)
                key_pos = (me ^ (row // rows)) * rows + row % rows
                query = lax.broadcasted_iota(jnp.int32, (span, width), 1) % rows
                query_pos = (me ^ distances[at]) * rows + query
                scores = jnp.where(key_pos <= query_pos, scores, floor_value)
            new_top = jnp.maximum(top, jnp.max(scores, axis=0, keepdims=True))
            weights = jnp.exp2((scores - new_top) * scale)
            rescale = jnp.exp2((top - new_top) * scale)
            total = total * rescale + jnp.sum(weights, axis=0, keepdims=True)
            mixed = mixed * rescale + lax.dot_general(
                values,
                weights.astype(jnp.bfloat16),
                (((0,), (0,)), ((), ())),
                preferred_element_type=jnp.float32,
            )
            result.append((new_top, total, mixed))
        return tuple(result)

    states = tuple(
        (
            jnp.full((1, width), floor_value, jnp.float32),
            jnp.zeros((1, width), jnp.float32),
            jnp.zeros((HEAD_SIZE, width), jnp.float32),
        )
        for _ in distances
    )
    states = step(pl.multiple_of(block * stride, 2 * TOP), states, True)

    def blocks(first, count, states):
        for at in range(count):
            states = step(pl.multiple_of((first + at) * stride, 2 * TOP), states, False)
        return states

    states = lax.fori_loop(0, block // 2, lambda i, s: blocks(2 * i, 2, s), states)
    states = lax.fori_loop(0, block % 2, lambda i, s: blocks(block - 1, 1, s), states)
    for (_, total, mixed), out in zip(states, outs):
        attended = (mixed / total).astype(jnp.bfloat16)
        attended = jnp.concatenate(
            [attended[:, head * rows : (head + 1) * rows] for head in range(heads)], axis=0
        )
        out[...] = lax.dot_general(
            attended, w_out[...], (((0,), (0,)), ((), ())), preferred_element_type=jnp.float32
        ).astype(jnp.bfloat16)


def residual_kernel(tokens, attention, partial, gain, residual, normed):
    summed = attention[...].astype(jnp.float32) + partial[...].astype(jnp.float32)
    rounded = (tokens[...].astype(jnp.float32) + summed).astype(jnp.bfloat16)
    residual[...] = rounded
    normed[...] = rms_scale(rounded.astype(jnp.float32), gain[...]).astype(jnp.bfloat16)


def slot_targets(table, expert):
    table = table.astype(jnp.float32)
    rows = table.shape[1] // 2
    named = table[:TOP, :rows] == expert.astype(jnp.float32)
    slot = jnp.max(jnp.where(named, table[:TOP, rows:], -1.0), axis=0, keepdims=True)
    weight = jnp.sum(jnp.where(named, table[TOP:, :rows], 0.0), axis=0, keepdims=True)
    return slot.astype(jnp.int32), weight * (1.0 / 1024.0)


def plane_targets(group, place, routing, near, away):
    block, me, count = place[0], place[1], routing.shape[1]
    table = routing[block ^ (2 * group), near]
    return [slot_targets(table, (block ^ core) * count + (me ^ away)) for core in (0, 1)]


def route_order(route):
    near, away = route
    return [n ^ a for a in away for n in near]


def dispatch_kernel(routes, group, capacity, place, routing, *refs):
    sources = refs[: sum(len(near) for near, _ in routes)]
    outs = refs[len(sources) :]
    rows = sources[0].shape[0]
    slots = lax.broadcasted_iota(jnp.int32, (capacity, rows), 0)
    for near, away in routes:
        some, sources = sources[: len(near)], sources[len(near) :]
        mine, outs = outs[: len(away)], outs[len(away) :]
        for at, (n, source) in enumerate(zip(near, some)):
            parts = []
            for a in away:
                for slot, _ in plane_targets(group, place, routing, n, a):
                    parts.append(jnp.where(slots == slot, 1.0, 0.0))
            hot = jnp.concatenate(parts, axis=0).astype(jnp.bfloat16)
            picked = jnp.dot(hot, source[...], preferred_element_type=jnp.float32)
            picked = picked.astype(jnp.bfloat16)
            for part in range(2 * len(away)):
                first = ((part % 2) * len(near) + at) * capacity
                mine[part // 2][first : first + capacity, :] = picked[
                    part * capacity : (part + 1) * capacity
                ]


def combine_kernel(group, capacity, place, routing, *refs):
    *returned, out = refs
    slots = lax.broadcasted_iota(jnp.int32, (capacity, out.shape[0]), 0)
    parts = []
    for distance in range(len(returned)):
        for slot, weight in plane_targets(group, place, routing, 0, distance):
            parts.append(jnp.where(slots == slot, weight, 0.0))
    shares = jnp.concatenate(parts, axis=0).astype(jnp.bfloat16)
    produced = jnp.concatenate([ref[...] for ref in returned], axis=0)
    out[...] = lax.dot_general(
        shares, produced, (((0,), (0,)), ((), ())), preferred_element_type=jnp.float32
    ).astype(jnp.bfloat16)


def expert_kernel(routes, capacity, *refs):
    count = sum(len(away) for _, away in routes)
    came, (mate, w_gate, w_up, w_down) = refs[:count], refs[count : count + 4]
    own, other, rows_in, hidden = refs[count + 4 :]
    width = came[0].shape[1]
    half = rows_in.shape[1] // 2
    places = []
    for side, (near, away) in enumerate(routes):
        base = sum(len(some) for _, some in routes[:side])
        for at, d in enumerate(route_order((near, away))):
            places.append((side, base + at // len(near), (at % len(near)) * capacity, d * capacity))
    for at, (side, piece, first, to) in enumerate(places):
        rows_in[side, to : to + capacity, :] = came[piece][first : first + capacity, :]
        to = half + to
        rows_in[side, to : to + capacity, :] = mate[at * capacity : (at + 1) * capacity, :]
    for first in range(0, hidden.shape[1], 256):
        cols = slice(first, first + 256)
        gate = up = 0.0
        for side in range(len(routes)):
            depth = slice(side * width, (side + 1) * width)
            rows = rows_in[side]
            gate = gate + jnp.dot(rows, w_gate[depth, cols], preferred_element_type=jnp.float32)
            up = up + jnp.dot(rows, w_up[depth, cols], preferred_element_type=jnp.float32)
        hidden[:, cols] = (gate / (1.0 + jnp.exp(-gate)) * up).astype(jnp.bfloat16)
    for side in range(len(routes)):
        for first in range(0, width, 256):
            down = w_down[:, side * width + first : side * width + first + 256]
            product = jnp.dot(hidden[...], down, preferred_element_type=jnp.float32)
            product = product.astype(jnp.bfloat16)
            cols = slice(side * width + first, side * width + first + 256)
            own[:, cols] = product[:half]
            other[:, cols] = product[half:]


def sum_kernel(*refs):
    *parts, out = refs
    total = parts[0][...].astype(jnp.float32)
    for part in parts[1:]:
        total = total + part[...].astype(jnp.float32)
    out[...] = total.astype(out.dtype)


def call(kernel, out_shape, specs, *args, name, scratch=(), limit=24, flops=1000):
    return pl.pallas_call(
        kernel,
        out_shape=out_shape,
        in_specs=specs,
        out_specs=jax.tree.map(lambda _: VMEM, out_shape),
        scratch_shapes=scratch,
        compiler_params=pltpu.CompilerParams(vmem_limit_bytes=limit * 1024 * 1024),
        cost_estimate=pl.CostEstimate(flops=flops, bytes_accessed=1000, transcendentals=0),
        name=name,
    )(*args)


def shards(
    tokens,
    ln1_gain,
    w_query,
    key_weight,
    value_weight,
    q_gain,
    k_gain,
    w_out,
    ln2_gain,
    expert_ids,
    route_weights,
    w_gate,
    w_up,
    w_down,
):
    rows, width = tokens.shape
    ctx_count = lax.axis_size("ctx")
    exp_count = lax.axis_size("exp")
    ctx_rows = rows * exp_count
    heads_dev = w_query.shape[1] // HEAD_SIZE
    group_width = QUERY_HEADS // KEY_VALUE_HEADS
    me_ctx = lax.axis_index("ctx").astype(jnp.int32)
    me_exp = lax.axis_index("exp").astype(jnp.int32)
    place = jnp.stack([me_ctx, me_exp] + [jnp.int32(0)] * exp_count)
    peers = list(range(exp_count))
    bf16 = functools.partial(jax.ShapeDtypeStruct, dtype=jnp.bfloat16)

    experts = ctx_count * exp_count
    capacity = max(2, 3 * rows * TOP // (2 * experts))
    capacity = -(-capacity // 16) * 16
    ln1_row = ln1_gain.reshape(1, width)
    own_first = me_ctx * ctx_rows + me_exp * rows
    cosine, sine = rope_tables(own_first + jnp.arange(rows))
    own_args = [
        expert_ids.T,
        route_weights.T,
        tokens,
        ln1_row,
        key_weight,
        value_weight,
        k_gain.reshape(1, HEAD_SIZE),
        cosine,
        sine,
    ]
    own_kv = call(
        functools.partial(own_rows_kernel, experts, heads_dev),
        [bf16((rows + 2 * TOP, 2 * HEAD_SIZE)) for _ in peers],
        [SMEM] + [ANY] * 9,
        place,
        *own_args,
        name="own_rows",
        scratch=[pltpu.VMEM(a.shape, a.dtype) for a in own_args] + [pltpu.SemaphoreType.DMA((18,))],
        limit=60,
    )
    block_kv = [own_kv[0]] + [swap(own_kv[d], "exp", d) for d in peers[1:]]
    both = [part[:rows] for part in block_kv] + [part[rows:] for part in block_kv]
    both = lax.all_gather(jnp.concatenate(both, axis=0), "ctx", axis=0, tiled=True)
    sent = tie(tokens, *block_kv[1:])
    pieces = [tokens] + [swap(sent, "exp", d) for d in peers[1:]]
    routing = both.reshape(ctx_count, -1, 2 * HEAD_SIZE)[:, ctx_rows:]
    routing = routing.reshape(ctx_count, exp_count, 2 * TOP, 2 * HEAD_SIZE)

    positions = jnp.concatenate(
        [me_ctx * ctx_rows + (me_exp ^ d) * rows + jnp.arange(rows) for d in peers]
    )
    cosine, sine = rope_tables(positions)
    queries = call(
        query_kernel,
        bf16((exp_count, heads_dev * rows, HEAD_SIZE)),
        [VMEM] * (exp_count + 5),
        *pieces,
        ln1_row,
        w_query,
        q_gain.reshape(1, HEAD_SIZE),
        cosine,
        sine,
        name="queries",
    )

    order = sorted(peers, key=lambda d: -bin(d).count("1"))
    partials, last = {}, ()
    for some in [[d] for d in order]:
        asked = queries[some[0] : some[0] + 1]
        made = call(
            functools.partial(attention_kernel, some, rows),
            [bf16((rows, width)) for _ in some],
            [SMEM, VMEM, VMEM, VMEM],
            place,
            tie(asked, *last),
            both,
            w_out,
            name="attention",
        )
        partials.update(zip(some, made))
        last = tuple(made)
    attention = partials[0]
    parts = [swap(partials[d], "exp", d) for d in order if d]
    for part in parts[:-1]:
        attention = call(
            sum_kernel,
            jax.ShapeDtypeStruct((rows, width), jnp.float32),
            [VMEM] * 2,
            attention,
            part,
            name="add",
            flops=3_000_000_000,
        )
    residual, normed = call(
        residual_kernel,
        [bf16((rows, width)), bf16((rows, width))],
        [VMEM] * 4,
        tokens,
        attention,
        parts[-1],
        ln2_gain.reshape(1, width),
        name="residual",
    )

    groups = ctx_count // 2
    low, high = [0, 1], list(range(0, exp_count, 2))
    routes = [(low, high), (high, low)]
    half = width // 2
    far = [normed] + [swap(normed, "ctx", 2 * g) for g in (1, 2) if g < groups]
    in_flight = {}

    def send(array, d, kind):
        came = swap(tie(array, *in_flight.get((kind, d), ())), "exp", d)
        in_flight[kind, d] = (came,)
        return came

    arrived = []
    for g in range(groups):
        sources = []
        for side, (near, _) in enumerate(routes):
            part = far[g][:, side * half : (side + 1) * half]
            sources += [part] + [send(part, n, "whole") for n in near[1:]]
        ahead = g + 2
        if g and ahead < groups:
            first = far[ahead & (ahead - 1)]
            far.append(swap(tie(first, *sources), "ctx", 2 * (ahead & -ahead)))
        outgoing = call(
            functools.partial(dispatch_kernel, routes, g, capacity),
            [bf16((2 * len(near) * capacity, half)) for near, away in routes for _ in away],
            [SMEM, VMEM] + [VMEM] * len(sources),
            place,
            routing,
            *sources,
            name="dispatch",
        )
        onward = [a for _, away in routes for a in away]
        arrived.append([send(out, a, "picked") if a else out for out, a in zip(outgoing, onward)])

    produced = []
    slots = exp_count * capacity
    for g, came in enumerate(arrived):
        mate = jnp.concatenate([part[part.shape[0] // 2 :] for part in came], axis=0)
        own, other = call(
            functools.partial(expert_kernel, routes, capacity),
            [bf16((slots, width)), bf16((slots, width))],
            [VMEM] * (len(came) + 4),
            *came,
            swap(tie(mate, *(produced[-1][1] if g == groups - 1 else ())), "ctx", 1),
            w_gate[0],
            w_up[0],
            w_down[0],
            name="expert",
            scratch=[
                pltpu.VMEM((2, 2 * slots, half), jnp.bfloat16),
                pltpu.VMEM((2 * slots, w_gate.shape[2]), jnp.bfloat16),
            ],
        )
        ours = [slice(d * capacity, (d + 1) * capacity) for d in peers]
        if g == groups - 2:
            mates = [swap(other[mine], "ctx", 1) for mine in ours]
        else:
            mates = swap(other, "ctx", 1)
            mates = [mates[mine] for mine in ours]
        produced.append(([own[mine] for mine in ours], mates))

    totals, hop, in_flight = [], (), {}
    for g in [*range(2, groups), *(g for g in (1, 0) if g < groups)]:
        back = []
        for d in peers:
            back.append(jnp.concatenate([part[d] for part in produced[g]], axis=0))
        back = [back[0]] + [send(back[d], d, "back") for d in peers[1:]]
        total = call(
            functools.partial(combine_kernel, g, capacity),
            bf16((rows, width)),
            [SMEM, VMEM] + [VMEM] * exp_count,
            place,
            routing,
            *back,
            name="combine",
        )
        if g:
            total = swap(tie(total, *(hop if g > 1 else ())), "ctx", 2 * g)
            hop = (total,)
        totals.append(total)
    early = call(
        sum_kernel,
        jax.ShapeDtypeStruct((rows, width), jnp.float32),
        [VMEM] * groups,
        residual,
        *totals[:-1],
        name="add",
        flops=10_000_000_000,
    )
    return call(sum_kernel, bf16((rows, width)), [VMEM] * 2, early, totals[-1], name="add")


def solution(mesh):
    in_specs = (
        P(("ctx", "exp"), None),
        P(),
        P(None, "exp"),
        P(),
        P(),
        P(),
        P(),
        P("exp", None),
        P(),
        P(("ctx", "exp"), None),
        P(("ctx", "exp"), None),
        P(("ctx", "exp"), None, None),
        P(("ctx", "exp"), None, None),
        P(("ctx", "exp"), None, None),
    )
    out_specs = P(("ctx", "exp"), None)
    return jax.shard_map(shards, mesh=mesh, in_specs=in_specs, out_specs=out_specs, check_vma=False)
```

```python
import functools

import jax
import jax.numpy as jnp
from jax import lax
from jax.experimental import pallas as pl
from jax.experimental.pallas import tpu as pltpu
from jax.sharding import PartitionSpec as P

HEAD_SIZE = 128
QUERY_HEADS = 16
KEY_VALUE_HEADS = 2
TOP = 8
LOG2E = 1.4426950408889634

eps_value = 1e-06
theta_value = 1000000.0
floor_value = -1e30

VMEM = pl.BlockSpec(memory_space=pltpu.VMEM)
SMEM = pl.BlockSpec(memory_space=pltpu.SMEM)
ANY = pl.BlockSpec(memory_space=pl.ANY)


def rms_scale(value_states, norm_gain):
    return (
        value_states
        * lax.rsqrt(jnp.mean(value_states * value_states, axis=-1, keepdims=True) + eps_value)
        * norm_gain
    )


def swap(array, axis, distance):
    pairs = [(i, i ^ distance) for i in range(lax.axis_size(axis))]
    return lax.ppermute(array, axis, pairs)


def tie(array, *others):
    if not others:
        return array
    return lax.optimization_barrier((array, *others))[0]


def rope_tables(positions):
    half = HEAD_SIZE // 2
    frequency = theta_value ** (-2.0 * jnp.arange(half, dtype=jnp.float32) / HEAD_SIZE)
    angles = positions.astype(jnp.float32)[:, None] * frequency[None, :]
    return jnp.cos(angles), jnp.sin(angles)


def both_halves(cosine, sine):
    return jnp.concatenate([cosine, cosine], axis=1), jnp.concatenate([-sine, sine], axis=1)


def normed_rotated(states, gain, cosine, sine):
    states = rms_scale(states, gain)
    return states * cosine + pltpu.roll(states, HEAD_SIZE // 2, 1) * sine


def load_all(pairs, sems):
    copies = []
    for source, target in pairs:
        part = source.shape[0] // 4 if source.shape[0] >= 128 and source.shape[1] > 128 else source.shape[0]
        for first in range(0, source.shape[0], part):
            here = pl.ds(first, part)
            copies.append(
                pltpu.make_async_copy(source.at[here], target.at[here], sems.at[len(copies)])
            )
    for copy in copies:
        copy.start()
    return copies


def own_rows_kernel(experts, heads_dev, place, *refs):
    peers = len(refs) - 19
    sources, outs, targets, sems = refs[:9], refs[9:-10], refs[-10:-1], refs[-1]
    copies = load_all(list(zip(sources, targets)), sems)
    ids, shares, tokens, gain, key_weight, value_weight, k_gain, cosine, sine = targets
    copies[0].wait()
    copies[1].wait()
    rows = tokens.shape[0]
    chosen_ids = ids[...]
    lanes = lax.broadcasted_iota(jnp.int32, (experts, rows), 0)
    chosen = jnp.zeros((experts, rows), jnp.float32)
    for k in range(TOP):
        chosen = chosen + jnp.where(lanes == chosen_ids[k : k + 1], 1.0, 0.0)
    earlier = lax.broadcasted_iota(jnp.int32, (rows, rows), 0) < lax.broadcasted_iota(
        jnp.int32, (rows, rows), 1
    )
    rank = jnp.dot(
        chosen.astype(jnp.bfloat16),
        jnp.where(earlier, 1.0, 0.0).astype(jnp.bfloat16),
        preferred_element_type=jnp.float32,
    )
    slots = [
        jnp.sum(jnp.where(lanes == chosen_ids[k : k + 1], rank, 0.0), axis=0, keepdims=True)
        for k in range(TOP)
    ]
    slots = jnp.concatenate(slots, axis=0)
    left = jnp.concatenate([chosen_ids, shares[...]], axis=0).astype(jnp.float32)
    right = jnp.concatenate([slots, jnp.zeros_like(slots)], axis=0)
    for out in outs:
        out[rows:, :] = jnp.concatenate([left, right], axis=1).astype(jnp.bfloat16)
    for copy in copies[2:]:
        copy.wait()
    normed = rms_scale(tokens[...].astype(jnp.float32), gain[...]).astype(jnp.bfloat16)
    keys = jnp.dot(normed, key_weight[...], preferred_element_type=jnp.float32)
    values = jnp.dot(normed, value_weight[...], preferred_element_type=jnp.float32)
    cosine, sine = both_halves(cosine[...], sine[...])
    for head in range(KEY_VALUE_HEADS):
        cols = slice(head * HEAD_SIZE, (head + 1) * HEAD_SIZE)
        rotated = normed_rotated(keys[:, cols], k_gain[...], cosine, sine)
        pair = jnp.concatenate([rotated, values[:, cols]], axis=1).astype(jnp.bfloat16)
        for distance in range(peers):
            asked = (place[1] ^ distance) * heads_dev // (QUERY_HEADS // KEY_VALUE_HEADS)

            @pl.when(asked == head)
            def _(out=outs[distance], pair=pair):
                out[:rows, :] = pair


def query_kernel(*refs):
    *pieces, gain, w_query, q_gain, cosine, sine, out = refs
    rows = pieces[0].shape[0]
    heads = w_query.shape[1] // HEAD_SIZE
    for at, piece in enumerate(pieces):
        normed = rms_scale(piece[...].astype(jnp.float32), gain[...]).astype(jnp.bfloat16)
        queries = jnp.dot(normed, w_query[...], preferred_element_type=jnp.float32)
        here = pl.ds(at * rows, rows)
        turn = both_halves(cosine[here, :], sine[here, :])
        for head in range(heads):
            cols = slice(head * HEAD_SIZE, (head + 1) * HEAD_SIZE)
            rotated = normed_rotated(queries[:, cols], q_gain[...], *turn)
            out[at, pl.ds(head * rows, rows), :] = rotated.astype(jnp.bfloat16)


def attention_kernel(distances, rows, place, queries, both, w_out, *outs):
    block, me = place[0], place[1]
    heads = w_out.shape[0] // HEAD_SIZE
    width = heads * rows
    span = rows * (place.shape[0] - 2)
    stride = span + 2 * TOP * (place.shape[0] - 2)
    scale = HEAD_SIZE ** (-0.5) * LOG2E

    def step(first, states, masked):
        keys = both[pl.ds(first, span), :HEAD_SIZE]
        values = both[pl.ds(first, span), HEAD_SIZE:]
        result = []
        for at, (top, total, mixed) in enumerate(states):
            scores = lax.dot_general(
                keys, queries[at], (((1,), (1,)), ((), ())), preferred_element_type=jnp.float32
            )
            if masked:
                row = lax.broadcasted_iota(jnp.int32, (span, width), 0)
                key_pos = (me ^ (row // rows)) * rows + row % rows
                query = lax.broadcasted_iota(jnp.int32, (span, width), 1) % rows
                query_pos = (me ^ distances[at]) * rows + query
                scores = jnp.where(key_pos <= query_pos, scores, floor_value)
            new_top = jnp.maximum(top, jnp.max(scores, axis=0, keepdims=True))
            weights = jnp.exp2((scores - new_top) * scale)
            rescale = jnp.exp2((top - new_top) * scale)
            total = total * rescale + jnp.sum(weights, axis=0, keepdims=True)
            mixed = mixed * rescale + lax.dot_general(
                values,
                weights.astype(jnp.bfloat16),
                (((0,), (0,)), ((), ())),
                preferred_element_type=jnp.float32,
            )
            result.append((new_top, total, mixed))
        return tuple(result)

    states = tuple(
        (
            jnp.full((1, width), floor_value, jnp.float32),
            jnp.zeros((1, width), jnp.float32),
            jnp.zeros((HEAD_SIZE, width), jnp.float32),
        )
        for _ in distances
    )
    states = step(pl.multiple_of(block * stride, 2 * TOP), states, True)

    def blocks(first, count, states):
        for at in range(count):
            states = step(pl.multiple_of((first + at) * stride, 2 * TOP), states, False)
        return states

    states = lax.fori_loop(0, block // 2, lambda i, s: blocks(2 * i, 2, s), states)
    states = lax.fori_loop(0, block % 2, lambda i, s: blocks(block - 1, 1, s), states)
    for (_, total, mixed), out in zip(states, outs):
        attended = (mixed / total).astype(jnp.bfloat16)
        attended = jnp.concatenate(
            [attended[:, head * rows : (head + 1) * rows] for head in range(heads)], axis=0
        )
        out[...] = lax.dot_general(
            attended, w_out[...], (((0,), (0,)), ((), ())), preferred_element_type=jnp.float32
        ).astype(jnp.bfloat16)


def residual_kernel(tokens, attention, partial, gain, residual, normed):
    summed = attention[...].astype(jnp.float32) + partial[...].astype(jnp.float32)
    rounded = (tokens[...].astype(jnp.float32) + summed).astype(jnp.bfloat16)
    residual[...] = rounded
    normed[...] = rms_scale(rounded.astype(jnp.float32), gain[...]).astype(jnp.bfloat16)


def slot_targets(table, expert):
    table = table.astype(jnp.float32)
    rows = table.shape[1] // 2
    named = table[:TOP, :rows] == expert.astype(jnp.float32)
    slot = jnp.max(jnp.where(named, table[:TOP, rows:], -1.0), axis=0, keepdims=True)
    weight = jnp.sum(jnp.where(named, table[TOP:, :rows], 0.0), axis=0, keepdims=True)
    return slot.astype(jnp.int32), weight * (1.0 / 1024.0)


def plane_targets(group, place, routing, near, away):
    block, me, count = place[0], place[1], routing.shape[1]
    table = routing[block ^ (2 * group), near]
    return [slot_targets(table, (block ^ core) * count + (me ^ away)) for core in (0, 1)]


def route_order(route):
    near, away = route
    return [n ^ a for a in away for n in near]


def dispatch_kernel(routes, group, capacity, place, routing, *refs):
    sources = refs[: sum(len(near) for near, _ in routes)]
    outs = refs[len(sources) :]
    rows = sources[0].shape[0]
    slots = lax.broadcasted_iota(jnp.int32, (capacity, rows), 0)
    for near, away in routes:
        some, sources = sources[: len(near)], sources[len(near) :]
        mine, outs = outs[: len(away)], outs[len(away) :]
        for at, (n, source) in enumerate(zip(near, some)):
            parts = []
            for a in away:
                for slot, _ in plane_targets(group, place, routing, n, a):
                    parts.append(jnp.where(slots == slot, 1.0, 0.0))
            hot = jnp.concatenate(parts, axis=0).astype(jnp.bfloat16)
            picked = jnp.dot(hot, source[...], preferred_element_type=jnp.float32)
            picked = picked.astype(jnp.bfloat16)
            for part in range(2 * len(away)):
                first = ((part % 2) * len(near) + at) * capacity
                mine[part // 2][first : first + capacity, :] = picked[
                    part * capacity : (part + 1) * capacity
                ]


def combine_kernel(group, capacity, place, routing, *refs):
    *returned, out = refs
    slots = lax.broadcasted_iota(jnp.int32, (capacity, out.shape[0]), 0)
    parts = []
    for distance in range(len(returned)):
        for slot, weight in plane_targets(group, place, routing, 0, distance):
            parts.append(jnp.where(slots == slot, weight, 0.0))
    shares = jnp.concatenate(parts, axis=0).astype(jnp.bfloat16)
    produced = jnp.concatenate([ref[...] for ref in returned], axis=0)
    out[...] = lax.dot_general(
        shares, produced, (((0,), (0,)), ((), ())), preferred_element_type=jnp.float32
    ).astype(jnp.bfloat16)


def expert_kernel(routes, capacity, *refs):
    count = sum(len(away) for _, away in routes)
    came, (mate, w_gate, w_up, w_down) = refs[:count], refs[count : count + 4]
    own, other, rows_in, hidden = refs[count + 4 :]
    width = came[0].shape[1]
    half = rows_in.shape[1] // 2
    places = []
    for side, (near, away) in enumerate(routes):
        base = sum(len(some) for _, some in routes[:side])
        for at, d in enumerate(route_order((near, away))):
            places.append((side, base + at // len(near), (at % len(near)) * capacity, d * capacity))
    for at, (side, piece, first, to) in enumerate(places):
        rows_in[side, to : to + capacity, :] = came[piece][first : first + capacity, :]
        to = half + to
        rows_in[side, to : to + capacity, :] = mate[at * capacity : (at + 1) * capacity, :]
    for first in range(0, hidden.shape[1], 256):
        cols = slice(first, first + 256)
        gate = up = 0.0
        for side in range(len(routes)):
            depth = slice(side * width, (side + 1) * width)
            rows = rows_in[side]
            gate = gate + jnp.dot(rows, w_gate[depth, cols], preferred_element_type=jnp.float32)
            up = up + jnp.dot(rows, w_up[depth, cols], preferred_element_type=jnp.float32)
        hidden[:, cols] = (gate / (1.0 + jnp.exp(-gate)) * up).astype(jnp.bfloat16)
    for side in range(len(routes)):
        for first in range(0, width, 256):
            down = w_down[:, side * width + first : side * width + first + 256]
            product = jnp.dot(hidden[...], down, preferred_element_type=jnp.float32)
            product = product.astype(jnp.bfloat16)
            cols = slice(side * width + first, side * width + first + 256)
            own[:, cols] = product[:half]
            other[:, cols] = product[half:]


def sum_kernel(*refs):
    *parts, out = refs
    total = parts[0][...].astype(jnp.float32)
    for part in parts[1:]:
        total = total + part[...].astype(jnp.float32)
    out[...] = total.astype(out.dtype)


def call(kernel, out_shape, specs, *args, name, scratch=(), limit=24, flops=1000):
    return pl.pallas_call(
        kernel,
        out_shape=out_shape,
        in_specs=specs,
        out_specs=jax.tree.map(lambda _: VMEM, out_shape),
        scratch_shapes=scratch,
        compiler_params=pltpu.CompilerParams(vmem_limit_bytes=limit * 1024 * 1024),
        cost_estimate=pl.CostEstimate(flops=flops, bytes_accessed=1000, transcendentals=0),
        name=name,
    )(*args)


def shards(
    tokens,
    ln1_gain,
    w_query,
    key_weight,
    value_weight,
    q_gain,
    k_gain,
    w_out,
    ln2_gain,
    expert_ids,
    route_weights,
    w_gate,
    w_up,
    w_down,
):
    rows, width = tokens.shape
    ctx_count = lax.axis_size("ctx")
    exp_count = lax.axis_size("exp")
    ctx_rows = rows * exp_count
    heads_dev = w_query.shape[1] // HEAD_SIZE
    group_width = QUERY_HEADS // KEY_VALUE_HEADS
    me_ctx = lax.axis_index("ctx").astype(jnp.int32)
    me_exp = lax.axis_index("exp").astype(jnp.int32)
    place = jnp.stack([me_ctx, me_exp] + [jnp.int32(0)] * exp_count)
    peers = list(range(exp_count))
    bf16 = functools.partial(jax.ShapeDtypeStruct, dtype=jnp.bfloat16)

    experts = ctx_count * exp_count
    capacity = max(2, 3 * rows * TOP // (2 * experts))
    capacity = -(-capacity // 16) * 16
    ln1_row = ln1_gain.reshape(1, width)
    own_first = me_ctx * ctx_rows + me_exp * rows
    cosine, sine = rope_tables(own_first + jnp.arange(rows))
    own_args = [
        expert_ids.T,
        route_weights.T,
        tokens,
        ln1_row,
        key_weight,
        value_weight,
        k_gain.reshape(1, HEAD_SIZE),
        cosine,
        sine,
    ]
    own_kv = call(
        functools.partial(own_rows_kernel, experts, heads_dev),
        [bf16((rows + 2 * TOP, 2 * HEAD_SIZE)) for _ in peers],
        [SMEM] + [ANY] * 9,
        place,
        *own_args,
        name="own_rows",
        scratch=[pltpu.VMEM(a.shape, a.dtype) for a in own_args] + [pltpu.SemaphoreType.DMA((18,))],
        limit=60,
    )
    block_kv = [own_kv[0]] + [swap(own_kv[d], "exp", d) for d in peers[1:]]
    both = [part[:rows] for part in block_kv] + [part[rows:] for part in block_kv]
    both = lax.all_gather(jnp.concatenate(both, axis=0), "ctx", axis=0, tiled=True)
    sent = tie(tokens, *block_kv[1:])
    pieces = [tokens] + [swap(sent, "exp", d) for d in peers[1:]]
    routing = both.reshape(ctx_count, -1, 2 * HEAD_SIZE)[:, ctx_rows:]
    routing = routing.reshape(ctx_count, exp_count, 2 * TOP, 2 * HEAD_SIZE)

    positions = jnp.concatenate(
        [me_ctx * ctx_rows + (me_exp ^ d) * rows + jnp.arange(rows) for d in peers]
    )
    cosine, sine = rope_tables(positions)
    queries = call(
        query_kernel,
        bf16((exp_count, heads_dev * rows, HEAD_SIZE)),
        [VMEM] * (exp_count + 5),
        *pieces,
        ln1_row,
        w_query,
        q_gain.reshape(1, HEAD_SIZE),
        cosine,
        sine,
        name="queries",
    )

    order = sorted(peers, key=lambda d: -bin(d).count("1"))
    partials, last = {}, ()
    for some in [[d] for d in order]:
        asked = queries[some[0] : some[0] + 1]
        made = call(
            functools.partial(attention_kernel, some, rows),
            [bf16((rows, width)) for _ in some],
            [SMEM, VMEM, VMEM, VMEM],
            place,
            tie(asked, *last),
            both,
            w_out,
            name="attention",
        )
        partials.update(zip(some, made))
        last = tuple(made)
    attention = partials[0]
    parts = [swap(partials[d], "exp", d) for d in order if d]
    for part in parts[:-1]:
        attention = call(
            sum_kernel,
            jax.ShapeDtypeStruct((rows, width), jnp.float32),
            [VMEM] * 2,
            attention,
            part,
            name="add",
            flops=3_000_000_000,
        )
    residual, normed = call(
        residual_kernel,
        [bf16((rows, width)), bf16((rows, width))],
        [VMEM] * 4,
        tokens,
        attention,
        parts[-1],
        ln2_gain.reshape(1, width),
        name="residual",
    )

    groups = ctx_count // 2
    low, high = [0, 1], list(range(0, exp_count, 2))
    routes = [(low, high), (high, low)]
    half = width // 2
    far = [normed] + [swap(normed, "ctx", 2 * g) for g in (1, 2) if g < groups]
    in_flight = {}

    def send(array, d, kind):
        came = swap(tie(array, *in_flight.get((kind, d), ())), "exp", d)
        in_flight[kind, d] = (came,)
        return came

    arrived = []
    for g in range(groups):
        sources = []
        for side, (near, _) in enumerate(routes):
            part = far[g][:, side * half : (side + 1) * half]
            sources += [part] + [send(part, n, "whole") for n in near[1:]]
        ahead = g + 2
        if g and ahead < groups:
            first = far[ahead & (ahead - 1)]
            far.append(swap(tie(first, *sources), "ctx", 2 * (ahead & -ahead)))
        outgoing = call(
            functools.partial(dispatch_kernel, routes, g, capacity),
            [bf16((2 * len(near) * capacity, half)) for near, away in routes for _ in away],
            [SMEM, VMEM] + [VMEM] * len(sources),
            place,
            routing,
            *sources,
            name="dispatch",
        )
        onward = [a for _, away in routes for a in away]
        arrived.append([send(out, a, "picked") if a else out for out, a in zip(outgoing, onward)])

    produced = []
    slots = exp_count * capacity
    for g, came in enumerate(arrived):
        halves = [part[part.shape[0] // 2 :] for part in came]
        if g == groups - 1 and g:
            count = len(halves)
            halves = lax.optimization_barrier((*halves, *produced[-1][1]))[:count]
        mate = jnp.concatenate(halves, axis=0)
        own, other = call(
            functools.partial(expert_kernel, routes, capacity),
            [bf16((slots, width)), bf16((slots, width))],
            [VMEM] * (len(came) + 4),
            *came,
            swap(mate, "ctx", 1),
            w_gate[0],
            w_up[0],
            w_down[0],
            name="expert",
            scratch=[
                pltpu.VMEM((2, 2 * slots, half), jnp.bfloat16),
                pltpu.VMEM((2 * slots, w_gate.shape[2]), jnp.bfloat16),
            ],
        )
        ours = [slice(d * capacity, (d + 1) * capacity) for d in peers]
        if g == groups - 2:
            mates = [swap(other[mine], "ctx", 1) for mine in ours]
        else:
            mates = swap(other, "ctx", 1)
            mates = [mates[mine] for mine in ours]
        produced.append(([own[mine] for mine in ours], mates))

    totals, in_flight = [], {}
    for g in [*range(2, groups), *(g for g in (1, 0) if g < groups)]:
        back = []
        for d in peers:
            back.append(jnp.concatenate([part[d] for part in produced[g]], axis=0))
        back = [back[0]] + [send(back[d], d, "back") for d in peers[1:]]
        total = call(
            functools.partial(combine_kernel, g, capacity),
            bf16((rows, width)),
            [SMEM, VMEM] + [VMEM] * exp_count,
            place,
            routing,
            *back,
            name="combine",
        )
        if g:
            total = swap(total, "ctx", 2 * g)
        totals.append(total)
    early = residual
    for total in totals[:-1]:
        early = call(
            sum_kernel,
            jax.ShapeDtypeStruct((rows, width), jnp.float32),
            [VMEM] * 2,
            early,
            total,
            name="add",
            flops=3_000_000_000,
        )
    return call(sum_kernel, bf16((rows, width)), [VMEM] * 2, early, totals[-1], name="add")


def solution(mesh):
    in_specs = (
        P(("ctx", "exp"), None),
        P(),
        P(None, "exp"),
        P(),
        P(),
        P(),
        P(),
        P("exp", None),
        P(),
        P(("ctx", "exp"), None),
        P(("ctx", "exp"), None),
        P(("ctx", "exp"), None, None),
        P(("ctx", "exp"), None, None),
        P(("ctx", "exp"), None, None),
    )
    out_specs = P(("ctx", "exp"), None)
    return jax.shard_map(shards, mesh=mesh, in_specs=in_specs, out_specs=out_specs, check_vma=False)
```

```python
import functools

import jax
import jax.numpy as jnp
from jax import lax
from jax.experimental import pallas as pl
from jax.experimental.pallas import tpu as pltpu
from jax.sharding import PartitionSpec as P

HEAD_SIZE = 128
QUERY_HEADS = 16
KEY_VALUE_HEADS = 2
TOP = 8
LOG2E = 1.4426950408889634

eps_value = 1e-06
theta_value = 1000000.0
floor_value = -1e30

VMEM = pl.BlockSpec(memory_space=pltpu.VMEM)
SMEM = pl.BlockSpec(memory_space=pltpu.SMEM)
ANY = pl.BlockSpec(memory_space=pl.ANY)


def rms_scale(value_states, norm_gain):
    return (
        value_states
        * lax.rsqrt(jnp.mean(value_states * value_states, axis=-1, keepdims=True) + eps_value)
        * norm_gain
    )


def swap(array, axis, distance):
    pairs = [(i, i ^ distance) for i in range(lax.axis_size(axis))]
    return lax.ppermute(array, axis, pairs)


def tie(array, *others):
    if not others:
        return array
    return lax.optimization_barrier((array, *others))[0]


def rope_tables(positions):
    half = HEAD_SIZE // 2
    frequency = theta_value ** (-2.0 * jnp.arange(half, dtype=jnp.float32) / HEAD_SIZE)
    angles = positions.astype(jnp.float32)[:, None] * frequency[None, :]
    return jnp.cos(angles), jnp.sin(angles)


def both_halves(cosine, sine):
    return jnp.concatenate([cosine, cosine], axis=1), jnp.concatenate([-sine, sine], axis=1)


def normed_rotated(states, gain, cosine, sine):
    states = rms_scale(states, gain)
    return states * cosine + pltpu.roll(states, HEAD_SIZE // 2, 1) * sine


def load_all(pairs, sems):
    copies = []
    for source, target in pairs:
        part = source.shape[0] // 4 if source.shape[0] >= 128 and source.shape[1] > 128 else source.shape[0]
        for first in range(0, source.shape[0], part):
            here = pl.ds(first, part)
            copies.append(
                pltpu.make_async_copy(source.at[here], target.at[here], sems.at[len(copies)])
            )
    for copy in copies:
        copy.start()
    return copies


def own_rows_kernel(experts, heads_dev, place, *refs):
    peers = len(refs) - 19
    sources, outs, targets, sems = refs[:9], refs[9:-10], refs[-10:-1], refs[-1]
    copies = load_all(list(zip(sources, targets)), sems)
    ids, shares, tokens, gain, key_weight, value_weight, k_gain, cosine, sine = targets
    copies[0].wait()
    copies[1].wait()
    rows = tokens.shape[0]
    chosen_ids = ids[...]
    lanes = lax.broadcasted_iota(jnp.int32, (experts, rows), 0)
    chosen = jnp.zeros((experts, rows), jnp.float32)
    for k in range(TOP):
        chosen = chosen + jnp.where(lanes == chosen_ids[k : k + 1], 1.0, 0.0)
    earlier = lax.broadcasted_iota(jnp.int32, (rows, rows), 0) < lax.broadcasted_iota(
        jnp.int32, (rows, rows), 1
    )
    rank = jnp.dot(
        chosen.astype(jnp.bfloat16),
        jnp.where(earlier, 1.0, 0.0).astype(jnp.bfloat16),
        preferred_element_type=jnp.float32,
    )
    slots = [
        jnp.sum(jnp.where(lanes == chosen_ids[k : k + 1], rank, 0.0), axis=0, keepdims=True)
        for k in range(TOP)
    ]
    slots = jnp.concatenate(slots, axis=0)
    left = jnp.concatenate([chosen_ids, shares[...]], axis=0).astype(jnp.float32)
    right = jnp.concatenate([slots, jnp.zeros_like(slots)], axis=0)
    for out in outs:
        out[rows:, :] = jnp.concatenate([left, right], axis=1).astype(jnp.bfloat16)
    for copy in copies[2:]:
        copy.wait()
    normed = rms_scale(tokens[...].astype(jnp.float32), gain[...]).astype(jnp.bfloat16)
    keys = jnp.dot(normed, key_weight[...], preferred_element_type=jnp.float32)
    values = jnp.dot(normed, value_weight[...], preferred_element_type=jnp.float32)
    cosine, sine = both_halves(cosine[...], sine[...])
    for head in range(KEY_VALUE_HEADS):
        cols = slice(head * HEAD_SIZE, (head + 1) * HEAD_SIZE)
        rotated = normed_rotated(keys[:, cols], k_gain[...], cosine, sine)
        pair = jnp.concatenate([rotated, values[:, cols]], axis=1).astype(jnp.bfloat16)
        for distance in range(peers):
            asked = (place[1] ^ distance) * heads_dev // (QUERY_HEADS // KEY_VALUE_HEADS)

            @pl.when(asked == head)
            def _(out=outs[distance], pair=pair):
                out[:rows, :] = pair


def query_kernel(*refs):
    *pieces, gain, w_query, q_gain, cosine, sine, out = refs
    rows = pieces[0].shape[0]
    heads = w_query.shape[1] // HEAD_SIZE
    for at, piece in enumerate(pieces):
        normed = rms_scale(piece[...].astype(jnp.float32), gain[...]).astype(jnp.bfloat16)
        queries = jnp.dot(normed, w_query[...], preferred_element_type=jnp.float32)
        here = pl.ds(at * rows, rows)
        turn = both_halves(cosine[here, :], sine[here, :])
        for head in range(heads):
            cols = slice(head * HEAD_SIZE, (head + 1) * HEAD_SIZE)
            rotated = normed_rotated(queries[:, cols], q_gain[...], *turn)
            out[at, pl.ds(head * rows, rows), :] = rotated.astype(jnp.bfloat16)


def attention_kernel(distances, rows, place, queries, both, w_out, *outs):
    block, me = place[0], place[1]
    heads = w_out.shape[0] // HEAD_SIZE
    width = heads * rows
    span = rows * (place.shape[0] - 2)
    stride = span + 2 * TOP * (place.shape[0] - 2)
    scale = HEAD_SIZE ** (-0.5) * LOG2E

    def step(first, states, masked):
        keys = both[pl.ds(first, span), :HEAD_SIZE]
        values = both[pl.ds(first, span), HEAD_SIZE:]
        result = []
        for at, (top, total, mixed) in enumerate(states):
            scores = lax.dot_general(
                keys, queries[at], (((1,), (1,)), ((), ())), preferred_element_type=jnp.float32
            )
            if masked:
                row = lax.broadcasted_iota(jnp.int32, (span, width), 0)
                key_pos = (me ^ (row // rows)) * rows + row % rows
                query = lax.broadcasted_iota(jnp.int32, (span, width), 1) % rows
                query_pos = (me ^ distances[at]) * rows + query
                scores = jnp.where(key_pos <= query_pos, scores, floor_value)
            new_top = jnp.maximum(top, jnp.max(scores, axis=0, keepdims=True))
            weights = jnp.exp2((scores - new_top) * scale)
            rescale = jnp.exp2((top - new_top) * scale)
            total = total * rescale + jnp.sum(weights, axis=0, keepdims=True)
            mixed = mixed * rescale + lax.dot_general(
                values,
                weights.astype(jnp.bfloat16),
                (((0,), (0,)), ((), ())),
                preferred_element_type=jnp.float32,
            )
            result.append((new_top, total, mixed))
        return tuple(result)

    states = tuple(
        (
            jnp.full((1, width), floor_value, jnp.float32),
            jnp.zeros((1, width), jnp.float32),
            jnp.zeros((HEAD_SIZE, width), jnp.float32),
        )
        for _ in distances
    )
    states = step(pl.multiple_of(block * stride, 2 * TOP), states, True)

    def blocks(first, count, states):
        for at in range(count):
            states = step(pl.multiple_of((first + at) * stride, 2 * TOP), states, False)
        return states

    states = lax.fori_loop(0, block // 2, lambda i, s: blocks(2 * i, 2, s), states)
    states = lax.fori_loop(0, block % 2, lambda i, s: blocks(block - 1, 1, s), states)
    for (_, total, mixed), out in zip(states, outs):
        attended = (mixed / total).astype(jnp.bfloat16)
        attended = jnp.concatenate(
            [attended[:, head * rows : (head + 1) * rows] for head in range(heads)], axis=0
        )
        out[...] = lax.dot_general(
            attended, w_out[...], (((0,), (0,)), ((), ())), preferred_element_type=jnp.float32
        ).astype(jnp.bfloat16)


def residual_kernel(tokens, attention, partial, gain, residual, normed):
    summed = attention[...].astype(jnp.float32) + partial[...].astype(jnp.float32)
    rounded = (tokens[...].astype(jnp.float32) + summed).astype(jnp.bfloat16)
    residual[...] = rounded
    normed[...] = rms_scale(rounded.astype(jnp.float32), gain[...]).astype(jnp.bfloat16)


def slot_targets(table, expert):
    table = table.astype(jnp.float32)
    rows = table.shape[1] // 2
    named = table[:TOP, :rows] == expert.astype(jnp.float32)
    slot = jnp.max(jnp.where(named, table[:TOP, rows:], -1.0), axis=0, keepdims=True)
    weight = jnp.sum(jnp.where(named, table[TOP:, :rows], 0.0), axis=0, keepdims=True)
    return slot.astype(jnp.int32), weight * (1.0 / 1024.0)


def plane_targets(group, place, routing, near, away):
    block, me, count = place[0], place[1], routing.shape[1]
    table = routing[block ^ (2 * group), near]
    return [slot_targets(table, (block ^ core) * count + (me ^ away)) for core in (0, 1)]


def route_order(route):
    near, away = route
    return [n ^ a for a in away for n in near]


def dispatch_kernel(routes, group, capacity, place, routing, *refs):
    sources = refs[: sum(len(near) for near, _ in routes)]
    outs = refs[len(sources) :]
    rows = sources[0].shape[0]
    slots = lax.broadcasted_iota(jnp.int32, (capacity, rows), 0)
    for near, away in routes:
        some, sources = sources[: len(near)], sources[len(near) :]
        mine, outs = outs[: len(away)], outs[len(away) :]
        for at, (n, source) in enumerate(zip(near, some)):
            parts = []
            for a in away:
                for slot, _ in plane_targets(group, place, routing, n, a):
                    parts.append(jnp.where(slots == slot, 1.0, 0.0))
            hot = jnp.concatenate(parts, axis=0).astype(jnp.bfloat16)
            picked = jnp.dot(hot, source[...], preferred_element_type=jnp.float32)
            picked = picked.astype(jnp.bfloat16)
            for part in range(2 * len(away)):
                first = ((part % 2) * len(near) + at) * capacity
                mine[part // 2][first : first + capacity, :] = picked[
                    part * capacity : (part + 1) * capacity
                ]


def combine_kernel(group, capacity, place, routing, *refs):
    *returned, out = refs
    slots = lax.broadcasted_iota(jnp.int32, (capacity, out.shape[0]), 0)
    parts = []
    for distance in range(len(returned)):
        for slot, weight in plane_targets(group, place, routing, 0, distance):
            parts.append(jnp.where(slots == slot, weight, 0.0))
    shares = jnp.concatenate(parts, axis=0).astype(jnp.bfloat16)
    produced = jnp.concatenate([ref[...] for ref in returned], axis=0)
    out[...] = lax.dot_general(
        shares, produced, (((0,), (0,)), ((), ())), preferred_element_type=jnp.float32
    ).astype(jnp.bfloat16)


def expert_kernel(routes, capacity, *refs):
    count = sum(len(away) for _, away in routes)
    came, (mate, w_gate, w_up, w_down) = refs[:count], refs[count : count + 4]
    own, other, rows_in, hidden = refs[count + 4 :]
    width = came[0].shape[1]
    half = rows_in.shape[1] // 2
    places = []
    for side, (near, away) in enumerate(routes):
        base = sum(len(some) for _, some in routes[:side])
        for at, d in enumerate(route_order((near, away))):
            places.append((side, base + at // len(near), (at % len(near)) * capacity, d * capacity))
    for at, (side, piece, first, to) in enumerate(places):
        rows_in[side, to : to + capacity, :] = came[piece][first : first + capacity, :]
        to = half + to
        rows_in[side, to : to + capacity, :] = mate[at * capacity : (at + 1) * capacity, :]
    for first in range(0, hidden.shape[1], 256):
        cols = slice(first, first + 256)
        gate = up = 0.0
        for side in range(len(routes)):
            depth = slice(side * width, (side + 1) * width)
            rows = rows_in[side]
            gate = gate + jnp.dot(rows, w_gate[depth, cols], preferred_element_type=jnp.float32)
            up = up + jnp.dot(rows, w_up[depth, cols], preferred_element_type=jnp.float32)
        hidden[:, cols] = (gate / (1.0 + jnp.exp(-gate)) * up).astype(jnp.bfloat16)
    for side in range(len(routes)):
        for first in range(0, width, 256):
            down = w_down[:, side * width + first : side * width + first + 256]
            product = jnp.dot(hidden[...], down, preferred_element_type=jnp.float32)
            product = product.astype(jnp.bfloat16)
            cols = slice(side * width + first, side * width + first + 256)
            own[:, cols] = product[:half]
            other[:, cols] = product[half:]


def halves_kernel(*refs):
    *parts, out = refs
    first = 0
    for part in parts:
        count = part.shape[0] // 2
        out[first : first + count, :] = part[count:, :]
        first += count


def sum_kernel(*refs):
    *parts, out = refs
    total = parts[0][...].astype(jnp.float32)
    for part in parts[1:]:
        total = total + part[...].astype(jnp.float32)
    out[...] = total.astype(out.dtype)


def call(kernel, out_shape, specs, *args, name, scratch=(), limit=24, flops=1000):
    return pl.pallas_call(
        kernel,
        out_shape=out_shape,
        in_specs=specs,
        out_specs=jax.tree.map(lambda _: VMEM, out_shape),
        scratch_shapes=scratch,
        compiler_params=pltpu.CompilerParams(vmem_limit_bytes=limit * 1024 * 1024),
        cost_estimate=pl.CostEstimate(flops=flops, bytes_accessed=1000, transcendentals=0),
        name=name,
    )(*args)


def shards(
    tokens,
    ln1_gain,
    w_query,
    key_weight,
    value_weight,
    q_gain,
    k_gain,
    w_out,
    ln2_gain,
    expert_ids,
    route_weights,
    w_gate,
    w_up,
    w_down,
):
    rows, width = tokens.shape
    ctx_count = lax.axis_size("ctx")
    exp_count = lax.axis_size("exp")
    ctx_rows = rows * exp_count
    heads_dev = w_query.shape[1] // HEAD_SIZE
    group_width = QUERY_HEADS // KEY_VALUE_HEADS
    me_ctx = lax.axis_index("ctx").astype(jnp.int32)
    me_exp = lax.axis_index("exp").astype(jnp.int32)
    place = jnp.stack([me_ctx, me_exp] + [jnp.int32(0)] * exp_count)
    peers = list(range(exp_count))
    bf16 = functools.partial(jax.ShapeDtypeStruct, dtype=jnp.bfloat16)

    experts = ctx_count * exp_count
    capacity = max(2, 3 * rows * TOP // (2 * experts))
    capacity = -(-capacity // 16) * 16
    ln1_row = ln1_gain.reshape(1, width)
    own_first = me_ctx * ctx_rows + me_exp * rows
    cosine, sine = rope_tables(own_first + jnp.arange(rows))
    own_args = [
        expert_ids.T,
        route_weights.T,
        tokens,
        ln1_row,
        key_weight,
        value_weight,
        k_gain.reshape(1, HEAD_SIZE),
        cosine,
        sine,
    ]
    own_kv = call(
        functools.partial(own_rows_kernel, experts, heads_dev),
        [bf16((rows + 2 * TOP, 2 * HEAD_SIZE)) for _ in peers],
        [SMEM] + [ANY] * 9,
        place,
        *own_args,
        name="own_rows",
        scratch=[pltpu.VMEM(a.shape, a.dtype) for a in own_args] + [pltpu.SemaphoreType.DMA((18,))],
        limit=60,
    )
    block_kv = [own_kv[0]] + [swap(own_kv[d], "exp", d) for d in peers[1:]]
    both = [part[:rows] for part in block_kv] + [part[rows:] for part in block_kv]
    both = lax.all_gather(jnp.concatenate(both, axis=0), "ctx", axis=0, tiled=True)
    sent = tie(tokens, *block_kv[1:])
    pieces = [tokens] + [swap(sent, "exp", d) for d in peers[1:]]
    routing = both.reshape(ctx_count, -1, 2 * HEAD_SIZE)[:, ctx_rows:]
    routing = routing.reshape(ctx_count, exp_count, 2 * TOP, 2 * HEAD_SIZE)

    positions = jnp.concatenate(
        [me_ctx * ctx_rows + (me_exp ^ d) * rows + jnp.arange(rows) for d in peers]
    )
    cosine, sine = rope_tables(positions)
    queries = call(
        query_kernel,
        bf16((exp_count, heads_dev * rows, HEAD_SIZE)),
        [VMEM] * (exp_count + 5),
        *pieces,
        ln1_row,
        w_query,
        q_gain.reshape(1, HEAD_SIZE),
        cosine,
        sine,
        name="queries",
    )

    order = sorted(peers, key=lambda d: -bin(d).count("1"))
    partials, last = {}, ()
    for some in [[d] for d in order]:
        asked = queries[some[0] : some[0] + 1]
        made = call(
            functools.partial(attention_kernel, some, rows),
            [bf16((rows, width)) for _ in some],
            [SMEM, VMEM, VMEM, VMEM],
            place,
            tie(asked, *last),
            both,
            w_out,
            name="attention",
        )
        partials.update(zip(some, made))
        last = tuple(made)
    attention = partials[0]
    parts = [swap(partials[d], "exp", d) for d in order if d]
    for part in parts[:-1]:
        attention = call(
            sum_kernel,
            jax.ShapeDtypeStruct((rows, width), jnp.float32),
            [VMEM] * 2,
            attention,
            part,
            name="add",
            flops=3_000_000_000,
        )
    residual, normed = call(
        residual_kernel,
        [bf16((rows, width)), bf16((rows, width))],
        [VMEM] * 4,
        tokens,
        attention,
        parts[-1],
        ln2_gain.reshape(1, width),
        name="residual",
    )

    groups = ctx_count // 2
    low, high = [0, 1], list(range(0, exp_count, 2))
    routes = [(low, high), (high, low)]
    half = width // 2
    far = [normed] + [swap(normed, "ctx", 2 * g) for g in (1, 2) if g < groups]
    in_flight = {}

    def send(array, d, kind):
        came = swap(tie(array, *in_flight.get((kind, d), ())), "exp", d)
        in_flight[kind, d] = (came,)
        return came

    arrived = []
    for g in range(groups):
        sources = []
        for side, (near, _) in enumerate(routes):
            part = far[g][:, side * half : (side + 1) * half]
            sources += [part] + [send(part, n, "whole") for n in near[1:]]
        ahead = g + 2
        if g and ahead < groups:
            first = far[ahead & (ahead - 1)]
            far.append(swap(tie(first, *sources), "ctx", 2 * (ahead & -ahead)))
        outgoing = call(
            functools.partial(dispatch_kernel, routes, g, capacity),
            [bf16((2 * len(near) * capacity, half)) for near, away in routes for _ in away],
            [SMEM, VMEM] + [VMEM] * len(sources),
            place,
            routing,
            *sources,
            name="dispatch",
        )
        onward = [a for _, away in routes for a in away]
        arrived.append([send(out, a, "picked") if a else out for out, a in zip(outgoing, onward)])

    produced = []
    slots = exp_count * capacity
    for g, came in enumerate(arrived):
        parts = came
        if g == groups - 1 and g:
            parts = lax.optimization_barrier((*came, *produced[-1][1]))[: len(came)]
        mate = call(
            halves_kernel,
            bf16((2 * slots, half)),
            [VMEM] * len(parts),
            *parts,
            name="halves",
        )
        own, other = call(
            functools.partial(expert_kernel, routes, capacity),
            [bf16((slots, width)), bf16((slots, width))],
            [VMEM] * (len(came) + 4),
            *came,
            swap(mate, "ctx", 1),
            w_gate[0],
            w_up[0],
            w_down[0],
            name="expert",
            scratch=[
                pltpu.VMEM((2, 2 * slots, half), jnp.bfloat16),
                pltpu.VMEM((2 * slots, w_gate.shape[2]), jnp.bfloat16),
            ],
        )
        ours = [slice(d * capacity, (d + 1) * capacity) for d in peers]
        if g == groups - 2:
            mates = [swap(other[mine], "ctx", 1) for mine in ours]
        else:
            mates = swap(other, "ctx", 1)
            mates = [mates[mine] for mine in ours]
        produced.append(([own[mine] for mine in ours], mates))

    totals, in_flight = [], {}
    for g in [*range(2, groups), *(g for g in (1, 0) if g < groups)]:
        back = []
        for d in peers:
            back.append(jnp.concatenate([part[d] for part in produced[g]], axis=0))
        back = [back[0]] + [send(back[d], d, "back") for d in peers[1:]]
        total = call(
            functools.partial(combine_kernel, g, capacity),
            bf16((rows, width)),
            [SMEM, VMEM] + [VMEM] * exp_count,
            place,
            routing,
            *back,
            name="combine",
        )
        if g:
            total = swap(total, "ctx", 2 * g)
        totals.append(total)
    early = residual
    for total in totals[:-1]:
        early = call(
            sum_kernel,
            jax.ShapeDtypeStruct((rows, width), jnp.float32),
            [VMEM] * 2,
            early,
            total,
            name="add",
            flops=3_000_000_000,
        )
    return call(sum_kernel, bf16((rows, width)), [VMEM] * 2, early, totals[-1], name="add")


def solution(mesh):
    in_specs = (
        P(("ctx", "exp"), None),
        P(),
        P(None, "exp"),
        P(),
        P(),
        P(),
        P(),
        P("exp", None),
        P(),
        P(("ctx", "exp"), None),
        P(("ctx", "exp"), None),
        P(("ctx", "exp"), None, None),
        P(("ctx", "exp"), None, None),
        P(("ctx", "exp"), None, None),
    )
    out_specs = P(("ctx", "exp"), None)
    return jax.shard_map(shards, mesh=mesh, in_specs=in_specs, out_specs=out_specs, check_vma=False)
```

```python
import functools

import jax
import jax.numpy as jnp
from jax import lax
from jax.experimental import pallas as pl
from jax.experimental.pallas import tpu as pltpu
from jax.sharding import PartitionSpec as P

HEAD_SIZE = 128
QUERY_HEADS = 16
KEY_VALUE_HEADS = 2
TOP = 8
LOG2E = 1.4426950408889634

eps_value = 1e-06
theta_value = 1000000.0
floor_value = -1e30

VMEM = pl.BlockSpec(memory_space=pltpu.VMEM)
SMEM = pl.BlockSpec(memory_space=pltpu.SMEM)
ANY = pl.BlockSpec(memory_space=pl.ANY)


def rms_scale(value_states, norm_gain):
    return (
        value_states
        * lax.rsqrt(jnp.mean(value_states * value_states, axis=-1, keepdims=True) + eps_value)
        * norm_gain
    )


def swap(array, axis, distance):
    pairs = [(i, i ^ distance) for i in range(lax.axis_size(axis))]
    return lax.ppermute(array, axis, pairs)


def tie(array, *others):
    if not others:
        return array
    return lax.optimization_barrier((array, *others))[0]


def rope_tables(positions):
    half = HEAD_SIZE // 2
    frequency = theta_value ** (-2.0 * jnp.arange(half, dtype=jnp.float32) / HEAD_SIZE)
    angles = positions.astype(jnp.float32)[:, None] * frequency[None, :]
    return jnp.cos(angles), jnp.sin(angles)


def both_halves(cosine, sine):
    return jnp.concatenate([cosine, cosine], axis=1), jnp.concatenate([-sine, sine], axis=1)


def normed_rotated(states, gain, cosine, sine):
    states = rms_scale(states, gain)
    return states * cosine + pltpu.roll(states, HEAD_SIZE // 2, 1) * sine


def load_all(pairs, sems):
    copies = []
    for source, target in pairs:
        part = source.shape[0] // 4 if source.shape[0] >= 128 and source.shape[1] > 128 else source.shape[0]
        for first in range(0, source.shape[0], part):
            here = pl.ds(first, part)
            copies.append(
                pltpu.make_async_copy(source.at[here], target.at[here], sems.at[len(copies)])
            )
    for copy in copies:
        copy.start()
    return copies


def own_rows_kernel(experts, heads_dev, place, *refs):
    peers = len(refs) - 19
    sources, outs, targets, sems = refs[:9], refs[9:-10], refs[-10:-1], refs[-1]
    copies = load_all(list(zip(sources, targets)), sems)
    ids, shares, tokens, gain, key_weight, value_weight, k_gain, cosine, sine = targets
    copies[0].wait()
    copies[1].wait()
    rows = tokens.shape[0]
    chosen_ids = ids[...]
    lanes = lax.broadcasted_iota(jnp.int32, (experts, rows), 0)
    chosen = jnp.zeros((experts, rows), jnp.float32)
    for k in range(TOP):
        chosen = chosen + jnp.where(lanes == chosen_ids[k : k + 1], 1.0, 0.0)
    earlier = lax.broadcasted_iota(jnp.int32, (rows, rows), 0) < lax.broadcasted_iota(
        jnp.int32, (rows, rows), 1
    )
    rank = jnp.dot(
        chosen.astype(jnp.bfloat16),
        jnp.where(earlier, 1.0, 0.0).astype(jnp.bfloat16),
        preferred_element_type=jnp.float32,
    )
    slots = [
        jnp.sum(jnp.where(lanes == chosen_ids[k : k + 1], rank, 0.0), axis=0, keepdims=True)
        for k in range(TOP)
    ]
    slots = jnp.concatenate(slots, axis=0)
    left = jnp.concatenate([chosen_ids, shares[...]], axis=0).astype(jnp.float32)
    right = jnp.concatenate([slots, jnp.zeros_like(slots)], axis=0)
    for out in outs:
        out[rows:, :] = jnp.concatenate([left, right], axis=1).astype(jnp.bfloat16)
    for copy in copies[2:]:
        copy.wait()
    normed = rms_scale(tokens[...].astype(jnp.float32), gain[...]).astype(jnp.bfloat16)
    keys = jnp.dot(normed, key_weight[...], preferred_element_type=jnp.float32)
    values = jnp.dot(normed, value_weight[...], preferred_element_type=jnp.float32)
    cosine, sine = both_halves(cosine[...], sine[...])
    for head in range(KEY_VALUE_HEADS):
        cols = slice(head * HEAD_SIZE, (head + 1) * HEAD_SIZE)
        rotated = normed_rotated(keys[:, cols], k_gain[...], cosine, sine)
        pair = jnp.concatenate([rotated, values[:, cols]], axis=1).astype(jnp.bfloat16)
        for distance in range(peers):
            asked = (place[1] ^ distance) * heads_dev // (QUERY_HEADS // KEY_VALUE_HEADS)

            @pl.when(asked == head)
            def _(out=outs[distance], pair=pair):
                out[:rows, :] = pair


def query_kernel(*refs):
    *pieces, gain, w_query, q_gain, cosine, sine, out = refs
    rows = pieces[0].shape[0]
    heads = w_query.shape[1] // HEAD_SIZE
    for at, piece in enumerate(pieces):
        normed = rms_scale(piece[...].astype(jnp.float32), gain[...]).astype(jnp.bfloat16)
        queries = jnp.dot(normed, w_query[...], preferred_element_type=jnp.float32)
        here = pl.ds(at * rows, rows)
        turn = both_halves(cosine[here, :], sine[here, :])
        for head in range(heads):
            cols = slice(head * HEAD_SIZE, (head + 1) * HEAD_SIZE)
            rotated = normed_rotated(queries[:, cols], q_gain[...], *turn)
            out[at, pl.ds(head * rows, rows), :] = rotated.astype(jnp.bfloat16)


def attention_kernel(distances, rows, place, queries, both, w_out, *outs):
    block, me = place[0], place[1]
    heads = w_out.shape[0] // HEAD_SIZE
    width = heads * rows
    span = rows * (place.shape[0] - 2)
    stride = span + 2 * TOP * (place.shape[0] - 2)
    scale = HEAD_SIZE ** (-0.5) * LOG2E

    def step(first, states, masked):
        keys = both[pl.ds(first, span), :HEAD_SIZE]
        values = both[pl.ds(first, span), HEAD_SIZE:]
        result = []
        for at, (top, total, mixed) in enumerate(states):
            scores = lax.dot_general(
                keys, queries[at], (((1,), (1,)), ((), ())), preferred_element_type=jnp.float32
            )
            if masked:
                row = lax.broadcasted_iota(jnp.int32, (span, width), 0)
                key_pos = (me ^ (row // rows)) * rows + row % rows
                query = lax.broadcasted_iota(jnp.int32, (span, width), 1) % rows
                query_pos = (me ^ distances[at]) * rows + query
                scores = jnp.where(key_pos <= query_pos, scores, floor_value)
            new_top = jnp.maximum(top, jnp.max(scores, axis=0, keepdims=True))
            weights = jnp.exp2((scores - new_top) * scale)
            rescale = jnp.exp2((top - new_top) * scale)
            total = total * rescale + jnp.sum(weights, axis=0, keepdims=True)
            mixed = mixed * rescale + lax.dot_general(
                values,
                weights.astype(jnp.bfloat16),
                (((0,), (0,)), ((), ())),
                preferred_element_type=jnp.float32,
            )
            result.append((new_top, total, mixed))
        return tuple(result)

    states = tuple(
        (
            jnp.full((1, width), floor_value, jnp.float32),
            jnp.zeros((1, width), jnp.float32),
            jnp.zeros((HEAD_SIZE, width), jnp.float32),
        )
        for _ in distances
    )
    states = step(pl.multiple_of(block * stride, 2 * TOP), states, True)

    def blocks(first, count, states):
        for at in range(count):
            states = step(pl.multiple_of((first + at) * stride, 2 * TOP), states, False)
        return states

    states = lax.fori_loop(0, block // 2, lambda i, s: blocks(2 * i, 2, s), states)
    states = lax.fori_loop(0, block % 2, lambda i, s: blocks(block - 1, 1, s), states)
    for (_, total, mixed), out in zip(states, outs):
        attended = (mixed / total).astype(jnp.bfloat16)
        attended = jnp.concatenate(
            [attended[:, head * rows : (head + 1) * rows] for head in range(heads)], axis=0
        )
        out[...] = lax.dot_general(
            attended, w_out[...], (((0,), (0,)), ((), ())), preferred_element_type=jnp.float32
        ).astype(jnp.bfloat16)


def residual_kernel(tokens, attention, partial, gain, residual, normed):
    summed = attention[...].astype(jnp.float32) + partial[...].astype(jnp.float32)
    rounded = (tokens[...].astype(jnp.float32) + summed).astype(jnp.bfloat16)
    residual[...] = rounded
    normed[...] = rms_scale(rounded.astype(jnp.float32), gain[...]).astype(jnp.bfloat16)


def slot_targets(table, expert):
    table = table.astype(jnp.float32)
    rows = table.shape[1] // 2
    named = table[:TOP, :rows] == expert.astype(jnp.float32)
    slot = jnp.max(jnp.where(named, table[:TOP, rows:], -1.0), axis=0, keepdims=True)
    weight = jnp.sum(jnp.where(named, table[TOP:, :rows], 0.0), axis=0, keepdims=True)
    return slot.astype(jnp.int32), weight * (1.0 / 1024.0)


def plane_targets(group, place, routing, near, away):
    block, me, count = place[0], place[1], routing.shape[1]
    table = routing[block ^ (2 * group), near]
    return [slot_targets(table, (block ^ core) * count + (me ^ away)) for core in (0, 1)]


def route_order(route):
    near, away = route
    return [n ^ a for a in away for n in near]


def dispatch_kernel(routes, group, capacity, place, routing, *refs):
    sources = refs[: sum(len(near) for near, _ in routes)]
    outs = refs[len(sources) :]
    rows = sources[0].shape[0]
    slots = lax.broadcasted_iota(jnp.int32, (capacity, rows), 0)
    for near, away in routes:
        some, sources = sources[: len(near)], sources[len(near) :]
        mine, outs = outs[: len(away)], outs[len(away) :]
        for at, (n, source) in enumerate(zip(near, some)):
            parts = []
            for a in away:
                for slot, _ in plane_targets(group, place, routing, n, a):
                    parts.append(jnp.where(slots == slot, 1.0, 0.0))
            hot = jnp.concatenate(parts, axis=0).astype(jnp.bfloat16)
            picked = jnp.dot(hot, source[...], preferred_element_type=jnp.float32)
            picked = picked.astype(jnp.bfloat16)
            for part in range(2 * len(away)):
                first = ((part % 2) * len(near) + at) * capacity
                mine[part // 2][first : first + capacity, :] = picked[
                    part * capacity : (part + 1) * capacity
                ]


def combine_kernel(group, capacity, place, routing, *refs):
    count = routing.shape[1]
    returned, others, out = refs[:count], refs[count:-1], refs[-1]
    slots = lax.broadcasted_iota(jnp.int32, (capacity, out.shape[0]), 0)
    parts = []
    for distance in range(count):
        for slot, weight in plane_targets(group, place, routing, 0, distance):
            parts.append(jnp.where(slots == slot, weight, 0.0))
    shares = jnp.concatenate(parts, axis=0).astype(jnp.bfloat16)
    produced = jnp.concatenate([ref[...] for ref in returned], axis=0)
    total = lax.dot_general(
        shares, produced, (((0,), (0,)), ((), ())), preferred_element_type=jnp.float32
    )
    for other in others:
        total = total + other[...]
    out[...] = total.astype(jnp.bfloat16)


def expert_kernel(routes, capacity, *refs):
    count = sum(len(away) for _, away in routes)
    came, (mate, w_gate, w_up, w_down) = refs[:count], refs[count : count + 4]
    own, other, rows_in, hidden = refs[count + 4 :]
    width = came[0].shape[1]
    half = rows_in.shape[1] // 2
    places = []
    for side, (near, away) in enumerate(routes):
        base = sum(len(some) for _, some in routes[:side])
        for at, d in enumerate(route_order((near, away))):
            places.append((side, base + at // len(near), (at % len(near)) * capacity, d * capacity))
    for at, (side, piece, first, to) in enumerate(places):
        rows_in[side, to : to + capacity, :] = came[piece][first : first + capacity, :]
        to = half + to
        rows_in[side, to : to + capacity, :] = mate[at * capacity : (at + 1) * capacity, :]
    for first in range(0, hidden.shape[1], 256):
        cols = slice(first, first + 256)
        gate = up = 0.0
        for side in range(len(routes)):
            depth = slice(side * width, (side + 1) * width)
            rows = rows_in[side]
            gate = gate + jnp.dot(rows, w_gate[depth, cols], preferred_element_type=jnp.float32)
            up = up + jnp.dot(rows, w_up[depth, cols], preferred_element_type=jnp.float32)
        hidden[:, cols] = (gate / (1.0 + jnp.exp(-gate)) * up).astype(jnp.bfloat16)
    for side in range(len(routes)):
        for first in range(0, width, 256):
            down = w_down[:, side * width + first : side * width + first + 256]
            product = jnp.dot(hidden[...], down, preferred_element_type=jnp.float32)
            product = product.astype(jnp.bfloat16)
            cols = slice(side * width + first, side * width + first + 256)
            own[:, cols] = product[:half]
            other[:, cols] = product[half:]


def halves_kernel(*refs):
    *parts, out = refs
    first = 0
    for part in parts:
        count = part.shape[0] // 2
        out[first : first + count, :] = part[count:, :]
        first += count


def sum_kernel(*refs):
    *parts, out = refs
    total = parts[0][...].astype(jnp.float32)
    for part in parts[1:]:
        total = total + part[...].astype(jnp.float32)
    out[...] = total.astype(out.dtype)


def call(kernel, out_shape, specs, *args, name, scratch=(), limit=24, flops=1000):
    return pl.pallas_call(
        kernel,
        out_shape=out_shape,
        in_specs=specs,
        out_specs=jax.tree.map(lambda _: VMEM, out_shape),
        scratch_shapes=scratch,
        compiler_params=pltpu.CompilerParams(vmem_limit_bytes=limit * 1024 * 1024),
        cost_estimate=pl.CostEstimate(flops=flops, bytes_accessed=1000, transcendentals=0),
        name=name,
    )(*args)


def shards(
    tokens,
    ln1_gain,
    w_query,
    key_weight,
    value_weight,
    q_gain,
    k_gain,
    w_out,
    ln2_gain,
    expert_ids,
    route_weights,
    w_gate,
    w_up,
    w_down,
):
    rows, width = tokens.shape
    ctx_count = lax.axis_size("ctx")
    exp_count = lax.axis_size("exp")
    ctx_rows = rows * exp_count
    heads_dev = w_query.shape[1] // HEAD_SIZE
    group_width = QUERY_HEADS // KEY_VALUE_HEADS
    me_ctx = lax.axis_index("ctx").astype(jnp.int32)
    me_exp = lax.axis_index("exp").astype(jnp.int32)
    place = jnp.stack([me_ctx, me_exp] + [jnp.int32(0)] * exp_count)
    peers = list(range(exp_count))
    bf16 = functools.partial(jax.ShapeDtypeStruct, dtype=jnp.bfloat16)

    experts = ctx_count * exp_count
    capacity = max(2, 3 * rows * TOP // (2 * experts))
    capacity = -(-capacity // 16) * 16
    ln1_row = ln1_gain.reshape(1, width)
    own_first = me_ctx * ctx_rows + me_exp * rows
    cosine, sine = rope_tables(own_first + jnp.arange(rows))
    own_args = [
        expert_ids.T,
        route_weights.T,
        tokens,
        ln1_row,
        key_weight,
        value_weight,
        k_gain.reshape(1, HEAD_SIZE),
        cosine,
        sine,
    ]
    own_kv = call(
        functools.partial(own_rows_kernel, experts, heads_dev),
        [bf16((rows + 2 * TOP, 2 * HEAD_SIZE)) for _ in peers],
        [SMEM] + [ANY] * 9,
        place,
        *own_args,
        name="own_rows",
        scratch=[pltpu.VMEM(a.shape, a.dtype) for a in own_args] + [pltpu.SemaphoreType.DMA((18,))],
        limit=60,
    )
    block_kv = [own_kv[0]] + [swap(own_kv[d], "exp", d) for d in peers[1:]]
    both = [part[:rows] for part in block_kv] + [part[rows:] for part in block_kv]
    both = lax.all_gather(jnp.concatenate(both, axis=0), "ctx", axis=0, tiled=True)
    sent = tie(tokens, *block_kv[1:])
    pieces = [tokens] + [swap(sent, "exp", d) for d in peers[1:]]
    routing = both.reshape(ctx_count, -1, 2 * HEAD_SIZE)[:, ctx_rows:]
    routing = routing.reshape(ctx_count, exp_count, 2 * TOP, 2 * HEAD_SIZE)

    positions = jnp.concatenate(
        [me_ctx * ctx_rows + (me_exp ^ d) * rows + jnp.arange(rows) for d in peers]
    )
    cosine, sine = rope_tables(positions)
    queries = call(
        query_kernel,
        bf16((exp_count, heads_dev * rows, HEAD_SIZE)),
        [VMEM] * (exp_count + 5),
        *pieces,
        ln1_row,
        w_query,
        q_gain.reshape(1, HEAD_SIZE),
        cosine,
        sine,
        name="queries",
    )

    order = sorted(peers, key=lambda d: -bin(d).count("1"))
    partials, last = {}, ()
    for some in [[d] for d in order]:
        asked = queries[some[0] : some[0] + 1]
        made = call(
            functools.partial(attention_kernel, some, rows),
            [bf16((rows, width)) for _ in some],
            [SMEM, VMEM, VMEM, VMEM],
            place,
            tie(asked, *last),
            both,
            w_out,
            name="attention",
        )
        partials.update(zip(some, made))
        last = tuple(made)
    attention = partials[0]
    parts = [swap(partials[d], "exp", d) for d in order if d]
    for part in parts[:-1]:
        attention = call(
            sum_kernel,
            jax.ShapeDtypeStruct((rows, width), jnp.float32),
            [VMEM] * 2,
            attention,
            part,
            name="add",
            flops=3_000_000_000,
        )
    residual, normed = call(
        residual_kernel,
        [bf16((rows, width)), bf16((rows, width))],
        [VMEM] * 4,
        tokens,
        attention,
        parts[-1],
        ln2_gain.reshape(1, width),
        name="residual",
    )

    groups = ctx_count // 2
    low, high = [0, 1], list(range(0, exp_count, 2))
    routes = [(low, high), (high, low)]
    half = width // 2
    far = [normed] + [swap(normed, "ctx", 2 * g) for g in (1, 2) if g < groups]
    in_flight = {}

    def send(array, d, kind):
        came = swap(tie(array, *in_flight.get((kind, d), ())), "exp", d)
        in_flight[kind, d] = (came,)
        return came

    arrived = []
    for g in range(groups):
        sources = []
        for side, (near, _) in enumerate(routes):
            part = far[g][:, side * half : (side + 1) * half]
            sources += [part] + [send(part, n, "whole") for n in near[1:]]
        ahead = g + 2
        if g and ahead < groups:
            first = far[ahead & (ahead - 1)]
            far.append(swap(tie(first, *sources), "ctx", 2 * (ahead & -ahead)))
        outgoing = call(
            functools.partial(dispatch_kernel, routes, g, capacity),
            [bf16((2 * len(near) * capacity, half)) for near, away in routes for _ in away],
            [SMEM, VMEM] + [VMEM] * len(sources),
            place,
            routing,
            *sources,
            name="dispatch",
        )
        onward = [a for _, away in routes for a in away]
        arrived.append([send(out, a, "picked") if a else out for out, a in zip(outgoing, onward)])

    produced = []
    slots = exp_count * capacity
    for g, came in enumerate(arrived):
        parts = came
        if g == groups - 1 and g:
            parts = lax.optimization_barrier((*came, *produced[-1][1]))[: len(came)]
        mate = call(
            halves_kernel,
            bf16((2 * slots, half)),
            [VMEM] * len(parts),
            *parts,
            name="halves",
        )
        own, other = call(
            functools.partial(expert_kernel, routes, capacity),
            [bf16((slots, width)), bf16((slots, width))],
            [VMEM] * (len(came) + 4),
            *came,
            swap(mate, "ctx", 1),
            w_gate[0],
            w_up[0],
            w_down[0],
            name="expert",
            scratch=[
                pltpu.VMEM((2, 2 * slots, half), jnp.bfloat16),
                pltpu.VMEM((2 * slots, w_gate.shape[2]), jnp.bfloat16),
            ],
        )
        ours = [slice(d * capacity, (d + 1) * capacity) for d in peers]
        if g == groups - 2:
            mates = [swap(other[mine], "ctx", 1) for mine in ours]
        else:
            mates = swap(other, "ctx", 1)
            mates = [mates[mine] for mine in ours]
        produced.append(([own[mine] for mine in ours], mates))

    totals, in_flight = [], {}
    for g in [*range(2, groups), *(g for g in (1, 0) if g < groups)]:
        back = []
        for d in peers:
            back.append(jnp.concatenate([part[d] for part in produced[g]], axis=0))
        back = [back[0]] + [send(back[d], d, "back") for d in peers[1:]]
        early = [] if g else [residual]
        for total in [] if g else totals:
            early = [
                call(
                    sum_kernel,
                    jax.ShapeDtypeStruct((rows, width), jnp.float32),
                    [VMEM] * 2,
                    *early,
                    total,
                    name="add",
                    flops=1_500_000_000,
                )
            ]
        total = call(
            functools.partial(combine_kernel, g, capacity),
            bf16((rows, width)),
            [SMEM, VMEM] + [VMEM] * (exp_count + len(early)),
            place,
            routing,
            *back,
            *early,
            name="combine",
        )
        if g:
            totals.append(swap(total, "ctx", 2 * g))
    return total


def solution(mesh):
    in_specs = (
        P(("ctx", "exp"), None),
        P(),
        P(None, "exp"),
        P(),
        P(),
        P(),
        P(),
        P("exp", None),
        P(),
        P(("ctx", "exp"), None),
        P(("ctx", "exp"), None),
        P(("ctx", "exp"), None, None),
        P(("ctx", "exp"), None, None),
        P(("ctx", "exp"), None, None),
    )
    out_specs = P(("ctx", "exp"), None)
    return jax.shard_map(shards, mesh=mesh, in_specs=in_specs, out_specs=out_specs, check_vma=False)
```
